32 devices in a mesh: ctx: 16 (over z, y, x), fsdp: 2 (over core).
Axes of the slice: x: 2, y: 2, z: 4, core: 2. Of those that a mesh axis runs over, the one named last changes fastest.
Arguments:
- hidden_in: bfloat16 [2, 2048, 2048], P('fsdp', 'ctx'), may hold values from -6 to 6
- block_map: int32 [2, 32], P('fsdp'), may hold values from 0 to 31, as said below
- query_weight: bfloat16 [2048, 2048], P(('ctx', 'fsdp')), may hold values from -0.125 to 0.125
- key_weight: bfloat16 [2048, 1024], P(('ctx', 'fsdp')), may hold values from -0.125 to 0.125
- value_weight: bfloat16 [2048, 1024], P(('ctx', 'fsdp')), may hold values from -0.125 to 0.125
- out_weight: bfloat16 [2048, 2048], P(('ctx', 'fsdp')), may hold values from -0.5 to 0.5
- gate_weight: bfloat16 [2048, 6144], P(('ctx', 'fsdp')), may hold values from -0.125 to 0.125
- up_weight: bfloat16 [2048, 6144], P(('ctx', 'fsdp')), may hold values from -0.125 to 0.125
- down_weight: bfloat16 [2048, 6144], P(('ctx', 'fsdp')), may hold values from -0.109375 to 0.109375
- attention_norm_gain: bfloat16 [2048], P(('ctx', 'fsdp')), may hold values from 0.25 to 1.75
- feedforward_gain: bfloat16 [2048], P(('ctx', 'fsdp')), may hold values from 0.25 to 1.75
- query_gain: bfloat16 [128], replicated, may hold values from 1 to 2
- key_gain: bfloat16 [128], replicated, may hold values from 1 to 2
- output_grad: bfloat16 [2, 2048, 2048], P('fsdp', 'ctx'), may hold values from -6 to 6
Outputs:
- layer_out: bfloat16 [2, 2048, 2048], P('fsdp', 'ctx')
- input_grad: bfloat16 [2, 2048, 2048], P('fsdp', 'ctx')
- query_weight_grad: float32 [2048, 2048], P(('ctx', 'fsdp'))
- key_weight_grad: float32 [2048, 1024], P(('ctx', 'fsdp'))
- value_weight_grad: float32 [2048, 1024], P(('ctx', 'fsdp'))
- out_weight_grad: float32 [2048, 2048], P(('ctx', 'fsdp'))
- gate_weight_grad: float32 [2048, 6144], P(('ctx', 'fsdp'))
- up_weight_grad: float32 [2048, 6144], P(('ctx', 'fsdp'))
- down_weight_grad: float32 [2048, 6144], P(('ctx', 'fsdp'))
- attention_norm_gain_grad: float32 [2048], P(('ctx', 'fsdp'))
- feedforward_gain_grad: float32 [2048], P(('ctx', 'fsdp'))
- query_gain_grad: float32 [128], replicated
- key_gain_grad: float32 [128], replicated
The draws below stay inside these ranges and needn't reach their ends.
Inputs may be any that keep to these rules, and one draw needn't show every extreme that they name: `block_map`: in each row, entries 2 d and 2 d + 1 are the blocks stored on ctx device d: a block c below 16, then 32 - 1 - c; every block appears once in a row.
All inputs are finite; a program needn't handle non-finite values.
Results may differ from the reference program's by a relative error of at most 0.017.
Values may be sent and summed in bfloat16 or wider, within the bound.
A program may use at most 704 MiB of HBM per device.

```python
import jax
import jax.numpy as jnp
from jax import lax

D = 2048
HEADS = 16
KV_HEADS = 8
HEAD_DIM = 128
FF = 6144
BLOCK = 64
BLOCKS = 32
LENGTH = 2048
BATCH = 2
QW = 2048
KW = 1024


def draw_block_map(key, part):
    key = jax.random.fold_in(key, 11)
    seq_keys = jax.random.split(key, BATCH)
    halves = jax.vmap(lambda member: jax.random.permutation(member, BLOCKS // 2))(seq_keys)
    mirrored = BLOCKS - 1 - halves
    return jnp.stack([halves, mirrored], axis=-1).reshape(BATCH, BLOCKS).astype(jnp.int32)


def spiked(array, own_key, source, target, parts, factor):
    owner, partner = [(jnp.arange(array.shape[axis_at]) // (array.shape[axis_at] // parts)).reshape([-1 if axis == axis_at else 1 for axis in range(array.ndim)]) for axis_at in (source, target)]
    chosen = jax.random.permutation(own_key, parts)[partner]
    strong = (owner == chosen) | (owner == (partner + parts // 2) % parts)
    return jnp.where(strong, factor * array, array)


def levels(stream_key, dims, shards, low, top_value):
    loudness, own = 1.0, jax.random.fold_in(stream_key, 6)
    for axis_at, shards_of in shards:
        steps = jnp.exp(jax.random.uniform(jax.random.fold_in(own, axis_at), (shards_of,), jnp.float32, low / len(shards), top_value / len(shards)))
        loudness = loudness * jnp.repeat(steps, dims[axis_at] // shards_of).reshape([-1 if axis == axis_at else 1 for axis in range(len(dims))])
    return loudness


def gaussian(own_key, dims, spread, limit, cuts=(), held_as=jnp.bfloat16):
    array = jax.random.normal(own_key, dims, jnp.float32) * spread
    if len(cuts) > 0:
        array = levels(own_key, dims, cuts, -0.22, 0.18) * array
    return jnp.clip(array, min=-limit, max=limit).astype(held_as)


def heavy_noise(key, shape, spread, bound, shards, heavy, kind=jnp.bfloat16):
    array = spread * jax.random.normal(key, shape, jnp.float32)
    if shards:
        array = array * levels(key, shape, shards, -0.22, 0.18)
    return jnp.clip(spiked(array, jax.random.fold_in(key, 3), *heavy), -bound, bound).astype(kind)


def setup_inputs(seed: int = 0) -> dict:
    seeds = jax.random.split(jax.random.key(seed), 15)
    hidden_in = gaussian(seeds[0], (BATCH, LENGTH, D), 1.0, 6.0, ((0, 2), (1, 16)))
    block_map = draw_block_map(jax.random.fold_in(seeds[14], 71), 0)
    query_weight = gaussian(seeds[2], (D, QW), D ** -0.5, 0.125, ((0, 32),))
    key_weight = gaussian(seeds[3], (D, KW), D ** -0.5, 0.125, ((0, 32),))
    value_weight = gaussian(seeds[4], (D, KW), D ** -0.5, 0.125, ((0, 32),))
    out_weight = gaussian(seeds[5], (D, QW), (QW // 16) ** -0.5, 0.5, ((0, 32),))
    gate_weight = gaussian(seeds[6], (D, FF), D ** -0.5, 0.125, ((0, 32),))
    up_weight = gaussian(seeds[7], (D, FF), D ** -0.5, 0.125, ((0, 32),))
    down_weight = gaussian(seeds[8], (D, FF), (FF // 2) ** -0.5, 0.109375, ((0, 32),))
    attention_norm_gain = jnp.clip(1.0 + 0.15 * jax.random.normal(seeds[9], (D,), jnp.float32), 0.25, 1.75).astype(jnp.bfloat16)
    feedforward_gain = jnp.clip(1.0 + 0.15 * jax.random.normal(seeds[10], (D,), jnp.float32), 0.25, 1.75).astype(jnp.bfloat16)
    query_gain = jnp.clip(jax.random.uniform(seeds[11], (HEAD_DIM,), jnp.float32, 1.0, 2.0), 1.0, 2.0).astype(jnp.bfloat16)
    key_gain = jnp.clip(jax.random.uniform(seeds[12], (HEAD_DIM,), jnp.float32, 1.0, 2.0), 1.0, 2.0).astype(jnp.bfloat16)
    output_grad = heavy_noise(seeds[13], (BATCH, LENGTH, D), 1.0, 6.0, ((0, 2), (1, 16)), (1, 2, 16, 2.0))
    return {"hidden_in": hidden_in, "block_map": block_map, "query_weight": query_weight, "key_weight": key_weight, "value_weight": value_weight, "out_weight": out_weight, "gate_weight": gate_weight, "up_weight": up_weight, "down_weight": down_weight, "attention_norm_gain": attention_norm_gain, "feedforward_gain": feedforward_gain, "query_gain": query_gain, "key_gain": key_gain, "output_grad": output_grad}


@jax.custom_vjp
def low(v):
    return lax.optimization_barrier(v.astype(jnp.bfloat16)).astype(jnp.float32)

@jax.custom_vjp
def low_back(v):
    return v

def low_keep(v):
    return (low(v), None)

def low_pass(kept, grad):
    return (grad,)

def back_keep(v):
    return (v, None)

def back_low(kept, grad):
    return (low(grad),)
low.defvjp(low_keep, low_pass)
low_back.defvjp(back_keep, back_low)
epsilon = 1e-06
rotary_base = 1000000.0
masked_score = -1e+30
highest = lax.Precision.HIGHEST

def norm_rows(values, gain):
    return values * lax.rsqrt(lax.optimization_barrier(jnp.mean(values * values, axis=-1, keepdims=True)) + epsilon) * gain

def rotate(values, cosine, sine_table):
    half_width = values.shape[-1] // 2
    turned = jnp.concatenate([-values[..., half_width:], values[..., :half_width]], axis=-1)
    return values * cosine + turned * sine_table

def matmul(left, right):
    return jnp.dot(left, right, precision=highest)

def matmul_trans(left, right):
    return lax.dot_general(left, right, (((1,), (1,)), ((), ())), precision=highest)

def sequence_forward(hidden, positions, weights):
    query_weight, key_weight, value_weight, out_weight, gate_weight, up_weight, down_weight, attention_norm_gain, feedforward_gain, query_gain, key_gain = weights
    length = hidden.shape[0]
    group_size = HEADS // KV_HEADS
    half_width = HEAD_DIM // 2
    frequency = rotary_base ** (-(jnp.arange(half_width, dtype=jnp.float32) * 2.0 / HEAD_DIM))
    angles = positions.astype(jnp.float32)[:, None] * frequency[None, :]
    angles = jnp.concatenate([angles, angles], axis=-1)
    cosine = jnp.cos(angles)[:, None, :]
    sine_table = jnp.sin(angles)[:, None, :]
    normed = low(norm_rows(hidden, attention_norm_gain))
    query_lin = low_back(matmul(normed, query_weight)).reshape(length, HEADS, HEAD_DIM)
    key_lin = low_back(matmul(normed, key_weight)).reshape(length, KV_HEADS, HEAD_DIM)
    value_rows = low(low_back(matmul(normed, value_weight))).reshape(length, KV_HEADS, HEAD_DIM)
    queries = low(rotate(norm_rows(query_lin, query_gain), cosine, sine_table))
    key_rows = low(rotate(norm_rows(key_lin, key_gain), cosine, sine_table))
    block_rows = min(512, length)
    block_count = length // block_rows
    factor = HEAD_DIM ** (-0.5)

    def attend_block(pieces):
        query_block, query_pos = pieces
        scores = jnp.einsum('qkgd,tkd->kgqt', query_block, key_rows, precision=highest) * factor
        scores = low_back(scores)
        allowed = positions[None, :] <= query_pos[:, None]
        scores = jnp.where(allowed[None, None], scores, masked_score)
        row_peak = lax.optimization_barrier(jnp.max(scores, axis=-1, keepdims=True))
        exponent = jnp.exp(scores - row_peak)
        probabilities = low(exponent / lax.optimization_barrier(jnp.sum(exponent, axis=-1, keepdims=True)))
        return jnp.einsum('kgqt,tkd->qkgd', probabilities, value_rows, precision=highest)
    blocked = queries.reshape(block_count, block_rows, KV_HEADS, group_size, HEAD_DIM)
    attended = lax.map(jax.checkpoint(attend_block), (blocked, positions.reshape(block_count, block_rows)))
    attended = low_back(low(attended.reshape(length, HEADS * HEAD_DIM)))
    residual = hidden + low_back(matmul_trans(attended, out_weight))
    normed_mlp = low(norm_rows(residual, feedforward_gain))
    gate_lin = low_back(matmul(normed_mlp, gate_weight))
    up_lin = low_back(matmul(normed_mlp, up_weight))
    activation = low(jax.nn.silu(gate_lin) * up_lin)
    return residual + low_back(matmul_trans(activation, down_weight))

def reference(hidden_in, block_map, query_weight, key_weight, value_weight, out_weight, gate_weight, up_weight, down_weight, attention_norm_gain, feedforward_gain, query_gain, key_gain, output_grad):
    slot_index = jnp.arange(LENGTH, dtype=jnp.int32)
    positions = block_map[:, slot_index // BLOCK] * BLOCK + (slot_index % BLOCK)[None, :]
    positions = positions.astype(jnp.int32)
    hidden_float = hidden_in.astype(jnp.float32)
    weight_floats = tuple((source.astype(jnp.float32) for source in (query_weight, key_weight, value_weight, out_weight, gate_weight, up_weight, down_weight, attention_norm_gain, feedforward_gain, query_gain, key_gain)))

    def forward(hidden_all, weights):
        outputs = [sequence_forward(hidden_all[seq_index], positions[seq_index], weights) for seq_index in range(BATCH)]
        return jnp.stack(outputs)
    result, pull_back = jax.vjp(forward, hidden_float, weight_floats)
    grad_hidden, grad_weights = pull_back(output_grad.astype(jnp.float32))
    return (result.astype(jnp.bfloat16), grad_hidden.astype(jnp.bfloat16), grad_weights[0], grad_weights[1], grad_weights[2], grad_weights[3], grad_weights[4], grad_weights[5], grad_weights[6], grad_weights[7], grad_weights[8], grad_weights[9], grad_weights[10])
```

```python
import jax
import jax.numpy as jnp
from jax import lax
from jax.sharding import Mesh, PartitionSpec as P

epsilon = 1e-06
rotary_base = 1000000.0
masked_score = -1e30
parts = 4
bf16 = jnp.bfloat16
f32 = jnp.float32


def unit_rows(values):
    scale_row = lax.rsqrt(jnp.mean(values * values, axis=-1, keepdims=True) + epsilon)
    return values * scale_row, scale_row


def norm_back(weighted, unit, scale_row):
    inner_mean = jnp.mean(weighted * unit, axis=-1, keepdims=True)
    return scale_row * (weighted - unit * inner_mean)


def rope_tables(positions, width):
    half_width = width // 2
    frequency = rotary_base ** (-(jnp.arange(half_width, dtype=f32) * 2.0 / width))
    angles = positions.astype(f32)[:, None] * frequency[None, :]
    angles = jnp.concatenate([angles, angles], axis=-1)
    return jnp.cos(angles)[:, None, :], jnp.sin(angles)[:, None, :]


def rotate(values, cosine, sine_table):
    half_width = values.shape[-1] // 2
    turned = jnp.concatenate([-values[..., half_width:], values[..., :half_width]], axis=-1)
    return values * cosine + turned * sine_table


def rotate_back(grads, cosine, sine_table):
    half_width = grads.shape[-1] // 2
    shifted = grads * sine_table
    turned = jnp.concatenate([shifted[..., half_width:], -shifted[..., :half_width]], axis=-1)
    return grads * cosine + turned


def multiply(left, right):
    return jnp.dot(left, right, preferred_element_type=f32)


def multiply_trans(left, right):
    return lax.dot_general(left, right, (((1,), (1,)), ((), ())), preferred_element_type=f32)


def outer_rows(left, right):
    return lax.dot_general(left, right, (((0,), (0,)), ((), ())), preferred_element_type=f32)


def block_scores(queries, query_pos, key_block, pos_block, factor):
    scores = (
        jnp.einsum("rkgd,tkd->kgrt", queries, key_block, preferred_element_type=f32) * factor
    )
    allowed = pos_block[None, :] <= query_pos[:, None]
    return jnp.where(allowed[None, None], scores, masked_score)


def split_blocks(key_rows, value_rows, key_pos):
    key_count = key_rows.shape[0]
    block_size = min(512, key_count)
    block_count = key_count // block_size
    return (
        key_rows.reshape(block_count, block_size, key_rows.shape[1], key_rows.shape[2]),
        value_rows.reshape(block_count, block_size, value_rows.shape[1], value_rows.shape[2]),
        key_pos.reshape(block_count, block_size),
    )


def attend(queries, query_pos, key_rows, value_rows, key_pos):
    factor = queries.shape[-1] ** (-0.5)
    key_blocks, value_blocks, pos_blocks = split_blocks(key_rows, value_rows, key_pos)
    stat_shape = (queries.shape[1], queries.shape[2], queries.shape[0])

    def row_stats(running, pieces):
        row_best, summed = running
        scores = block_scores(queries, query_pos, pieces[0], pieces[1], factor)
        new_best = jnp.maximum(row_best, jnp.max(scores, axis=-1))
        summed = summed * jnp.exp(row_best - new_best) + jnp.sum(
            jnp.exp(scores - new_best[..., None]), axis=-1
        )
        return ((new_best, summed), None)

    initial = (jnp.full(stat_shape, masked_score, f32), jnp.zeros(stat_shape, f32))
    (row_best, summed), unused = lax.scan(row_stats, initial, (key_blocks, pos_blocks))

    def mix_values(accumulated, pieces):
        scores = block_scores(queries, query_pos, pieces[0], pieces[2], factor)
        weights = (jnp.exp(scores - row_best[..., None]) / summed[..., None]).astype(bf16)
        return (
            accumulated
            + jnp.einsum("kgrt,tkd->rkgd", weights, pieces[1], preferred_element_type=f32),
            None,
        )

    attended, unused = lax.scan(
        mix_values, jnp.zeros(queries.shape, f32), (key_blocks, value_blocks, pos_blocks)
    )
    return attended, row_best, summed


def attend_back(
    queries, query_pos, key_rows, value_rows, key_pos, grad_out, row_delta, row_best, summed
):
    factor = queries.shape[-1] ** (-0.5)
    key_blocks, value_blocks, pos_blocks = split_blocks(key_rows, value_rows, key_pos)

    def back_block(accumulated, pieces):
        key_block, value_block, pos_block = pieces
        scores = block_scores(queries, query_pos, key_block, pos_block, factor)
        probabilities = jnp.exp(scores - row_best[..., None]) / summed[..., None]
        weights = probabilities.astype(bf16)
        grad_probs = jnp.einsum("rkgd,tkd->kgrt", grad_out, value_block, preferred_element_type=f32)
        grad_scores = (probabilities * (grad_probs - row_delta[..., None])).astype(bf16)
        accumulated = accumulated + jnp.einsum(
            "kgrt,tkd->rkgd", grad_scores, key_block, preferred_element_type=f32
        )
        grad_keys = jnp.einsum("kgrt,rkgd->tkd", grad_scores, queries, preferred_element_type=f32)
        grad_values = jnp.einsum("kgrt,rkgd->tkd", weights, grad_out, preferred_element_type=f32)
        return (accumulated, (grad_keys, grad_values))

    grad_queries, (grad_keys, grad_values) = lax.scan(
        back_block, jnp.zeros(queries.shape, f32), (key_blocks, value_blocks, pos_blocks)
    )
    return (
        grad_queries * factor,
        grad_keys.reshape(key_rows.shape) * factor,
        grad_values.reshape(value_rows.shape),
    )


def gather_z(rows):
    return lax.all_gather(rows, "z", axis=0, tiled=True)


def scatter_sum_z(partial_rows):
    count = partial_rows.shape[0] // parts
    pieces = partial_rows.astype(bf16).reshape(parts, count, partial_rows.shape[1])
    pieces = lax.all_to_all(pieces, "z", 0, 0, tiled=True)
    return jnp.sum(pieces.astype(f32), axis=0)


def columns_of(weight):
    rows, columns = weight.shape
    return weight.reshape(rows, parts, columns // parts).transpose(1, 0, 2)


def fetch_columns(slices):
    pieces = lax.all_to_all(slices, "z", 0, 0, tiled=True)
    pieces = pieces.reshape(parts * pieces.shape[1], pieces.shape[2])
    return lax.all_gather(pieces, ("p", "c"), axis=0, tiled=True)


def return_columns(grads):
    summed = lax.psum_scatter(grads.astype(bf16), ("p", "c"), scatter_dimension=0, tiled=True)
    pieces = summed.reshape(parts, summed.shape[0] // parts, summed.shape[1])
    return lax.all_to_all(pieces, "z", 0, 0, tiled=True)


def spread(pieces):
    return pieces.astype(f32).transpose(1, 0, 2).reshape(pieces.shape[1], -1)


def make_local(plane):
    def shuffle(values, shard):
        rows = values.shape[0]
        return values.reshape(rows, parts, plane, shard).transpose(0, 2, 1, 3).reshape(rows, -1)

    def unshuffle(values, shard):
        rows = values.shape[0]
        return values.reshape(rows, plane, parts, shard).transpose(0, 2, 1, 3).reshape(rows, -1)

    def local(
        hidden_in,
        block_map,
        query_weight,
        key_weight,
        value_weight,
        out_weight,
        gate_weight,
        up_weight,
        down_weight,
        attention_norm_gain,
        feedforward_gain,
        query_gain,
        key_gain,
        output_grad,
    ):
        shard = query_weight.shape[0]
        row_count = hidden_in.shape[1]
        piece_rows = row_count // 2
        head_width = query_gain.shape[0]
        query_heads = query_weight.shape[1] // head_width // parts
        key_heads = key_weight.shape[1] // head_width // parts
        group_size = query_heads // key_heads
        query_width = query_heads * head_width
        key_width = key_heads * head_width
        hidden_units = gate_weight.shape[1] // parts
        z_index = lax.axis_index("z")
        p_index = lax.axis_index("p")
        p_count = plane // lax.axis_size("c")

        hidden_own = shuffle(hidden_in[0], shard)
        grad_own = shuffle(output_grad[0], shard)

        gains = jnp.stack([attention_norm_gain, feedforward_gain], axis=1)
        gains = jnp.pad(gains, ((0, 0), (0, 128 - gains.shape[1])))
        attention_slices = jnp.concatenate(
            [
                columns_of(query_weight),
                columns_of(key_weight),
                columns_of(value_weight),
                columns_of(out_weight),
                jnp.broadcast_to(gains[None], (parts,) + gains.shape),
            ],
            axis=2,
        )
        attention_columns = fetch_columns(attention_slices)
        hidden = gather_z(hidden_own).astype(f32)
        gate_columns = fetch_columns(columns_of(gate_weight))
        up_columns = fetch_columns(columns_of(up_weight))
        down_columns = fetch_columns(columns_of(down_weight))
        grad_rows = gather_z(grad_own)

        ends = [query_width, query_width + key_width, query_width + 2 * key_width]
        ends.append(ends[-1] + query_width)
        projection = attention_columns[:, : ends[2]]
        out_columns = attention_columns[:, ends[2] : ends[3]]
        gains = attention_columns[:, ends[3] : ends[3] + 2].astype(f32).T
        first_gain, second_gain = gains[0], gains[1]

        blocks = block_map[0].reshape(parts, p_count, 2)
        offsets = jnp.arange(piece_rows, dtype=jnp.int32)
        all_pos = blocks.transpose(1, 0, 2)[..., None] * piece_rows + offsets
        all_pos = all_pos.reshape(p_count, parts * row_count)
        query_pos = lax.dynamic_index_in_dim(all_pos, p_index, 0, keepdims=False)
        key_pos = all_pos.reshape(-1)
        cosine, sine_table = rope_tables(query_pos, head_width)
        tokens = parts * row_count

        unit_one, scale_one = unit_rows(hidden)
        normed = (unit_one * first_gain).astype(bf16)
        lin = multiply(normed, projection)
        query_lin = lin[:, : ends[0]].reshape(tokens, query_heads, head_width)
        key_lin = lin[:, ends[0] : ends[1]].reshape(tokens, key_heads, head_width)
        value_rows = lin[:, ends[1] :].astype(bf16).reshape(tokens, key_heads, head_width)
        query_gain_float = query_gain.astype(f32)
        key_gain_float = key_gain.astype(f32)
        query_unit, query_scale = unit_rows(query_lin)
        queries = rotate(query_unit * query_gain_float, cosine, sine_table).astype(bf16)
        queries = queries.reshape(tokens, key_heads, group_size, head_width)
        key_unit, key_scale = unit_rows(key_lin)
        key_rows = rotate(key_unit * key_gain_float, cosine, sine_table).astype(bf16)
        both = lax.all_gather(
            jnp.concatenate([key_rows, value_rows], axis=1), "p", axis=0, tiled=True
        )
        all_keys, all_values = both[:, :key_heads], both[:, key_heads:]
        attended, row_best, summed = attend(queries, query_pos, all_keys, all_values, key_pos)
        attended_low = attended.reshape(tokens, query_width).astype(bf16)

        own_residual = hidden_own.astype(f32) + scatter_sum_z(
            multiply_trans(attended_low, out_columns)
        )
        unit_two, scale_two = unit_rows(own_residual)
        normed_mlp = gather_z((unit_two * second_gain).astype(bf16))
        gate_lin = multiply(normed_mlp, gate_columns)
        up_lin = multiply(normed_mlp, up_columns)
        sigmoid_gate = jax.nn.sigmoid(gate_lin)
        silu_gate = gate_lin * sigmoid_gate
        activation = (silu_gate * up_lin).astype(bf16)
        output = own_residual + scatter_sum_z(multiply_trans(activation, down_columns))
        output = unshuffle(output.astype(bf16), shard)

        down_pieces = return_columns(outer_rows(grad_rows, activation))
        grad_act = multiply(grad_rows, down_columns)
        grad_gate = (
            grad_act * up_lin * sigmoid_gate * (1.0 + gate_lin * (1.0 - sigmoid_gate))
        ).astype(bf16)
        grad_up = (grad_act * silu_gate).astype(bf16)
        grad_normed_mlp = scatter_sum_z(
            multiply_trans(grad_gate, gate_columns) + multiply_trans(grad_up, up_columns)
        )
        gate_pieces = return_columns(outer_rows(normed_mlp, grad_gate))
        up_pieces = return_columns(outer_rows(normed_mlp, grad_up))
        second_gain_sum = jnp.sum(grad_normed_mlp * unit_two, axis=0)
        grad_residual = grad_own.astype(f32) + norm_back(
            grad_normed_mlp * second_gain, unit_two, scale_two
        )
        grad_residual_low = gather_z(grad_residual.astype(bf16))
        grad_attended = multiply(grad_residual_low, out_columns).astype(bf16)
        grad_attended = grad_attended.reshape(tokens, key_heads, group_size, head_width)
        out_own = outer_rows(grad_residual_low, attended_low)
        row_delta = jnp.moveaxis(jnp.sum(grad_attended.astype(f32) * attended, axis=-1), 0, -1)
        grad_queries, grad_keys_all, grad_values_all = attend_back(
            queries,
            query_pos,
            all_keys,
            all_values,
            key_pos,
            grad_attended,
            row_delta,
            row_best,
            summed,
        )
        both = jnp.concatenate([grad_keys_all, grad_values_all], axis=1).astype(bf16)
        both = both.reshape(p_count, tokens, 2 * key_width)
        both = lax.all_to_all(both, "p", 0, 0, tiled=True)
        both = jnp.sum(both.astype(f32), axis=0).reshape(tokens, 2 * key_heads, head_width)
        grad_keys, grad_values = both[:, :key_heads], both[:, key_heads:]
        grad_query_rot = rotate_back(
            grad_queries.reshape(tokens, query_heads, head_width), cosine, sine_table
        )
        grad_key_rot = rotate_back(grad_keys, cosine, sine_table)
        query_gain_sum = jnp.sum(grad_query_rot * query_unit, axis=(0, 1))
        key_gain_sum = jnp.sum(grad_key_rot * key_unit, axis=(0, 1))
        grad_query_lin = norm_back(grad_query_rot * query_gain_float, query_unit, query_scale)
        grad_key_lin = norm_back(grad_key_rot * key_gain_float, key_unit, key_scale)
        grad_lin = jnp.concatenate(
            [
                grad_query_lin.reshape(tokens, query_width).astype(bf16),
                grad_key_lin.reshape(tokens, key_width).astype(bf16),
                grad_values.reshape(tokens, key_width).astype(bf16),
            ],
            axis=1,
        )
        grad_normed = scatter_sum_z(multiply_trans(grad_lin, projection))
        unit_own, scale_own = unit_rows(hidden_own.astype(f32))
        first_gain_sum = jnp.sum(grad_normed * unit_own, axis=0)
        grad_hidden = grad_residual + norm_back(grad_normed * first_gain, unit_own, scale_own)
        input_grad = unshuffle(grad_hidden.astype(bf16), shard)
        attention_pieces = return_columns(
            jnp.concatenate([outer_rows(normed, grad_lin), out_own], axis=1)
        )
        gain_sums = lax.psum_scatter(
            jnp.stack([first_gain_sum, second_gain_sum], axis=1).reshape(plane, parts, shard, 2),
            ("p", "c"),
            scatter_dimension=0,
            tiled=True,
        )
        gain_sums = lax.psum_scatter(gain_sums[0], "z", scatter_dimension=0, tiled=True)[0]
        head_sums = lax.psum(jnp.stack([query_gain_sum, key_gain_sum]), ("z", "p", "c"))
        return (
            output[None],
            input_grad[None],
            spread(attention_pieces[:, :, : ends[0]]),
            spread(attention_pieces[:, :, ends[0] : ends[1]]),
            spread(attention_pieces[:, :, ends[1] : ends[2]]),
            spread(attention_pieces[:, :, ends[2] :]),
            spread(gate_pieces),
            spread(up_pieces),
            spread(down_pieces),
            gain_sums[:, 0],
            gain_sums[:, 1],
            head_sums[0],
            head_sums[1],
        )

    return local


def solution(mesh):
    ctx_count, core_count = mesh.shape["ctx"], mesh.shape["fsdp"]
    plane = ctx_count // parts
    fine_mesh = Mesh(mesh.devices.reshape(parts, plane, core_count), ("z", "p", "c"))
    token_spec = P("c", ("z", "p"), None)
    weight_spec = P(("z", "p", "c"), None)
    gain_spec = P(("z", "p", "c"))
    return jax.shard_map(
        make_local(plane * core_count),
        mesh=fine_mesh,
        in_specs=(
            (token_spec, P("c", None)) + (weight_spec,) * 7 + (gain_spec,) * 2 + (P(), P(), token_spec)
        ),
        out_specs=(token_spec,) * 2 + (weight_spec,) * 7 + (gain_spec,) * 2 + (P(), P()),
        check_vma=False,
    )
```

```python
import functools

import jax
import jax.numpy as jnp
from jax import lax
from jax.experimental import pallas as pl
from jax.experimental.pallas import tpu as pltpu
from jax.sharding import Mesh, PartitionSpec as P

epsilon = 1e-06
rotary_base = 1000000.0
masked_score = -1e30
parts = 4
bf16 = jnp.bfloat16
f32 = jnp.float32


def unit_rows(values):
    scale_row = lax.rsqrt(jnp.mean(values * values, axis=-1, keepdims=True) + epsilon)
    return values * scale_row, scale_row


def norm_back(weighted, unit, scale_row):
    inner_mean = jnp.mean(weighted * unit, axis=-1, keepdims=True)
    return scale_row * (weighted - unit * inner_mean)


def rope_tables(positions, width):
    half_width = width // 2
    frequency = rotary_base ** (-(jnp.arange(half_width, dtype=f32) * 2.0 / width))
    angles = positions.astype(f32)[:, None] * frequency[None, :]
    angles = jnp.concatenate([angles, angles], axis=-1)
    return jnp.cos(angles)[:, None, :], jnp.sin(angles)[:, None, :]


def rotate(values, cosine, sine_table):
    half_width = values.shape[-1] // 2
    turned = jnp.concatenate([-values[..., half_width:], values[..., :half_width]], axis=-1)
    return values * cosine + turned * sine_table


def rotate_back(grads, cosine, sine_table):
    half_width = grads.shape[-1] // 2
    shifted = grads * sine_table
    turned = jnp.concatenate([shifted[..., half_width:], -shifted[..., :half_width]], axis=-1)
    return grads * cosine + turned


def multiply(left, right):
    return jnp.dot(left, right, preferred_element_type=f32)


def multiply_trans(left, right):
    return lax.dot_general(left, right, (((1,), (1,)), ((), ())), preferred_element_type=f32)


def outer_rows(left, right):
    return lax.dot_general(left, right, (((0,), (0,)), ((), ())), preferred_element_type=f32)


def spread(pieces):
    return pieces.astype(f32).transpose(1, 0, 2).reshape(pieces.shape[1], -1)


class Links:
    def __init__(self, send_sems, recv_sems, local_sems):
        self.send_sems, self.recv_sems, self.local_sems = send_sems, recv_sems, local_sems
        self.count, self.local_count = 0, 0
        self.sent, self.kept = [], []

    def send(self, source, target, **device):
        index = self.count
        self.count += 1
        copy = pltpu.make_async_remote_copy(
            src_ref=source,
            dst_ref=target,
            send_sem=self.send_sems.at[index],
            recv_sem=self.recv_sems.at[index],
            device_id=device,
            device_id_type=pl.DeviceIdType.MESH,
        )
        copy.start()
        self.sent.append(copy)
        return copy

    def local(self, source, target):
        index = self.local_count
        self.local_count += 1
        copy = pltpu.make_async_copy(source, target, self.local_sems.at[index])
        copy.start()
        return copy

    def keep(self, source, target):
        self.kept.append(self.local(source, target))

    def finish(self):
        for copy in self.sent:
            copy.wait_send()
        for copy in self.kept:
            copy.wait()


class Place:
    def __init__(self, plane, cores):
        self.plane, self.cores = plane, cores
        self.z, self.p, self.c = (lax.axis_index(axis) for axis in ("z", "p", "c"))
        self.column = self.p * cores + self.c

    def along_z(self, step):
        return lax.rem(self.z + step, parts)

    def in_plane(self, step):
        return lax.rem(self.p + step, self.plane)

    def before(self, step):
        return lax.rem(self.p + self.plane - step, self.plane) * self.cores + self.c

    def siblings(self):
        return [lax.rem(self.c + step, self.cores) for step in range(1, self.cores)]


z_steps = (1, 3, 2)


class Fetch:
    def __init__(self, links, place, pieces, gathered):
        self.links, self.place, self.pieces, self.gathered = links, place, pieces, gathered

    def begin(self):
        links, place = self.links, self.place
        mine = self.gathered.at[place.z, place.column]
        self.first, self.own = [], []
        for shard, width, start, split in self.pieces:
            for step in z_steps:
                other = place.along_z(step)
                at = pl.multiple_of(other * width, 128) if split else 0
                self.first.append(
                    links.send(shard.at[:, pl.ds(at, width)], mine.at[:, pl.ds(start, width)], z=other)
                )
            at = pl.multiple_of(place.z * width, 128) if split else 0
            self.own.append(
                links.local(shard.at[:, pl.ds(at, width)], mine.at[:, pl.ds(start, width)])
            )

    def spread(self):
        links, place = self.links, self.place
        for copy in self.own:
            copy.wait()
        for copy in self.first:
            copy.wait_recv()
        block = self.gathered.at[:, place.column]
        self.second = [
            links.send(block, block, p=place.in_plane(step)) for step in range(1, place.plane)
        ]
        self.third = [links.send(block, block, c=other) for other in place.siblings()]

    def forward(self):
        links, place = self.links, self.place
        for step, copy in enumerate(self.second, 1):
            copy.wait_recv()
            block = self.gathered.at[:, place.before(step)]
            self.third += [links.send(block, block, c=other) for other in place.siblings()]

    def finish(self):
        for copy in self.third:
            copy.wait_recv()


def front_kernel(
    plane,
    cores,
    hidden,
    query_weight,
    key_weight,
    value_weight,
    out_weight,
    gate_weight,
    up_weight,
    down_weight,
    gain_block,
    grad_out,
    cosine,
    sine_turned,
    query_pos,
    key_pos,
    query_gain,
    key_gain,
    normed_out,
    projection_out,
    lin_out,
    queries_out,
    both_out,
    attended_out,
    out_columns_out,
    normed_mlp_out,
    residual_out,
    gate_out,
    up_out,
    down_out,
    grad_rows_out,
    stats_out,
    gains_out,
    hidden_all,
    normed,
    projection,
    lin,
    queries,
    both,
    attended_all,
    out_full,
    residual,
    normed_mlp,
    mixed,
    send_sems,
    recv_sems,
    local_sems,
):
    links = Links(send_sems, recv_sems, local_sems)
    place = Place(plane, cores)
    token_rows, width = hidden.shape
    tokens = parts * token_rows
    head = query_gain.shape[1]
    query_width = query_weight.shape[1] // parts
    key_width = key_weight.shape[1] // parts
    query_heads, key_heads = query_width // head, key_width // head
    group = query_heads // key_heads
    hidden_units = gate_weight.shape[1] // parts
    lin_width = query_width + 2 * key_width

    heads_fetch = Fetch(
        links,
        place,
        [
            (query_weight, query_width, 0, True),
            (key_weight, key_width, query_width, True),
            (value_weight, key_width, query_width + key_width, True),
            (gain_block, 128, lin_width, False),
        ],
        projection,
    )
    out_fetch = Fetch(links, place, [(out_weight, out_weight.shape[1], 0, False)], out_full)
    mlp_fetches = [
        Fetch(links, place, [(weight, hidden_units, 0, True)], target)
        for weight, target in ((gate_weight, gate_out), (up_weight, up_out), (down_weight, down_out))
    ]
    heads_fetch.begin()
    hidden_copies = [
        links.send(hidden, hidden_all.at[place.z], z=place.along_z(step)) for step in z_steps
    ]
    hidden_own = links.local(hidden, hidden_all.at[place.z])
    heads_fetch.spread()
    out_fetch.begin()
    for fetch in mlp_fetches:
        fetch.begin()
    hidden_own.wait()
    for copy in hidden_copies:
        copy.wait_recv()
    heads_fetch.forward()
    heads_fetch.finish()
    links.keep(projection, projection_out)

    gain_columns = projection[:, :, :, lin_width : lin_width + 128].reshape(width, 128)
    gain_rows = gain_columns.astype(f32).T
    gains_out[...] = gain_rows[:8]

    def norm_one(index, carry):
        values = hidden_all[index].astype(f32)
        scale = lax.rsqrt(jnp.mean(values * values, axis=-1, keepdims=True) + epsilon)
        rows = pl.ds(pl.multiple_of(index * token_rows, token_rows), token_rows)
        normed[rows] = (values * scale * gains_out[0:1]).astype(bf16)
        return carry

    lax.fori_loop(0, parts, norm_one, 0)
    links.keep(normed, normed_out)

    tile = 2 * head

    def project(index, carry):
        columns = pl.ds(pl.multiple_of(index * tile, tile), tile)
        weights = projection[:, :, :, columns].reshape(width, tile)
        lin[:, columns] = jnp.dot(normed[...], weights, preferred_element_type=f32)
        return carry

    lax.fori_loop(0, lin_width // tile, project, 0)
    own_both = both.at[place.p]

    def rope(values, gain):
        scale = lax.rsqrt(jnp.mean(values * values, axis=-1, keepdims=True) + epsilon)
        gained = values * scale * gain
        turned = pltpu.roll(gained, head // 2, 1)
        return (gained * cosine[...] + turned * sine_turned[...]).astype(bf16)

    for index in range(key_heads):
        columns = slice(query_width + index * head, query_width + (index + 1) * head)
        own_both[:, index * head : (index + 1) * head] = rope(lin[:, columns], key_gain[...])
    own_both[:, key_width:] = lin[:, query_width + key_width :].astype(bf16)
    both_copies = [
        links.send(own_both, own_both, p=place.in_plane(step)) for step in range(1, plane)
    ]
    for index in range(query_heads):
        columns = slice(index * head, (index + 1) * head)
        queries[index] = rope(lin[:, columns], query_gain[...])
    links.keep(lin.at[:, pl.ds(0, query_width + key_width)], lin_out)
    links.keep(queries, queries_out)
    out_fetch.spread()
    mlp_fetches[0].spread()
    for copy in both_copies:
        copy.wait_recv()
    links.keep(both, both_out)

    factor = head ** (-0.5) * 1.4426950408889634
    chunk = min(256, tokens)
    chunks_each = tokens // chunk
    lanes = group * tokens
    own_attended = attended_all.at[place.z]
    attended_copies = []
    for key_head in range(key_heads):
        block = queries[key_head * group : (key_head + 1) * group].reshape(lanes, head)
        positions = jnp.concatenate([query_pos[...]] * group, axis=1)
        mixed[...] = jnp.zeros_like(mixed)

        def attend_chunk(index, carry):
            best, summed = carry
            source, row = index // chunks_each, index % chunks_each
            rows = pl.ds(pl.multiple_of(row * chunk, chunk), chunk)
            keys = both[source, rows, pl.ds(key_head * head, head)]
            values = both[source, rows, pl.ds(key_width + key_head * head, head)]
            scores = multiply_trans(keys, block) * factor
            spot = pl.ds(pl.multiple_of(index * chunk, chunk), chunk)
            scores = jnp.where(key_pos[spot] <= positions, scores, masked_score)
            new_best = jnp.maximum(best, jnp.max(scores, axis=0, keepdims=True))
            weights = jnp.exp2(scores - new_best)
            shrink = jnp.exp2(best - new_best)
            summed = summed * shrink + jnp.sum(weights, axis=0, keepdims=True)
            mixed[...] = mixed[...] * shrink + outer_rows(values, weights.astype(bf16))
            return new_best, summed

        best, summed = lax.fori_loop(
            0,
            plane * chunks_each,
            attend_chunk,
            (jnp.full((1, lanes), masked_score, f32), jnp.zeros((1, lanes), f32)),
        )
        mixed_rows = (mixed[...] / summed).T
        stats = best + jnp.log2(summed)
        for member in range(group):
            index = key_head * group + member
            stats_out[index : index + 1] = stats[:, member * tokens : (member + 1) * tokens]
            own_attended[:, index * head : (index + 1) * head] = mixed_rows[
                member * tokens : (member + 1) * tokens
            ].astype(bf16)
        part = own_attended.at[:, pl.ds(key_head * group * head, group * head)]
        attended_copies += [links.send(part, part, z=place.along_z(step)) for step in z_steps]
        if key_head == 0:
            out_fetch.forward()
            mlp_fetches[1].spread()
    grad_copies = [
        links.send(grad_out, grad_rows_out.at[place.z], z=place.along_z(step)) for step in z_steps
    ]
    links.keep(grad_out, grad_rows_out.at[place.z])
    links.keep(own_attended, attended_out)
    mlp_fetches[2].spread()
    out_fetch.finish()
    links.keep(out_full, out_columns_out)
    for copy in attended_copies:
        copy.wait_recv()

    def add_out(index, carry):
        weights = out_full[index].reshape(width // parts, parts * query_width)
        columns = pl.ds(pl.multiple_of(index * (width // parts), 128), width // parts)
        total = hidden_all[:, :, columns].reshape(tokens, width // parts).astype(f32)
        for other in range(parts):
            total += multiply_trans(
                attended_all[other], weights[:, other * query_width : (other + 1) * query_width]
            )
        residual[:, columns] = total
        return carry

    lax.fori_loop(0, parts, add_out, 0)
    mlp_fetches[0].forward()

    def norm_two(index, carry):
        rows = pl.ds(pl.multiple_of(index * token_rows, token_rows), token_rows)
        values = residual[rows]
        scale = lax.rsqrt(jnp.mean(values * values, axis=-1, keepdims=True) + epsilon)
        normed_mlp[rows] = (values * scale * gains_out[1:2]).astype(bf16)
        return carry

    lax.fori_loop(0, parts, norm_two, 0)
    links.keep(normed_mlp, normed_mlp_out)
    own_rows = pl.ds(pl.multiple_of(place.z * token_rows, token_rows), token_rows)
    links.keep(residual.at[own_rows], residual_out)
    mlp_fetches[1].forward()
    mlp_fetches[2].forward()
    for copy in grad_copies:
        copy.wait_recv()
    for fetch in mlp_fetches:
        fetch.finish()
    links.finish()


def front(plane, cores, hidden, weights, gain_block, grad_out, tables, positions, head_gains):
    token_rows, width = hidden.shape
    tokens = parts * token_rows
    shard = weights[0].shape[0]
    head = head_gains[0].shape[1]
    query_width, key_width = weights[0].shape[1] // parts, weights[1].shape[1] // parts
    hidden_units = weights[4].shape[1] // parts
    lin_width = query_width + 2 * key_width
    query_heads = query_width // head
    group = query_width // key_width
    stacked = (parts, plane * cores, shard)
    copies = 3 * 7 + 3 * 3 + 3 * 2 + 5 * (2 * plane - 1) + plane + 8
    any_space, vmem = pl.BlockSpec(memory_space=pl.ANY), pl.BlockSpec(memory_space=pltpu.VMEM)
    outputs = [
        ((tokens, width), bf16),
        (stacked + (lin_width + 128,), bf16),
        ((tokens, query_width + key_width), f32),
        ((query_heads, tokens, head), bf16),
        ((plane, tokens, 2 * key_width), bf16),
        ((tokens, query_width), bf16),
        (stacked + (parts * query_width,), bf16),
        ((tokens, width), bf16),
        ((token_rows, width), f32),
        (stacked + (hidden_units,), bf16),
        (stacked + (hidden_units,), bf16),
        (stacked + (hidden_units,), bf16),
        ((parts, token_rows, width), bf16),
        ((8, tokens), f32),
        ((8, width), f32),
    ]
    return pl.pallas_call(
        functools.partial(front_kernel, plane, cores),
        out_shape=[jax.ShapeDtypeStruct(shape, kind) for shape, kind in outputs],
        in_specs=[any_space] * 10 + [vmem] * 6,
        out_specs=[any_space] * 13 + [vmem] * 2,
        scratch_shapes=[
            pltpu.VMEM((parts, token_rows, width), bf16),
            pltpu.VMEM((tokens, width), bf16),
            pltpu.VMEM(stacked + (lin_width + 128,), bf16),
            pltpu.VMEM((tokens, lin_width), f32),
            pltpu.VMEM((query_heads, tokens, head), bf16),
            pltpu.VMEM((plane, tokens, 2 * key_width), bf16),
            pltpu.VMEM((parts, tokens, query_width), bf16),
            pltpu.VMEM(stacked + (parts * query_width,), bf16),
            pltpu.VMEM((tokens, width), f32),
            pltpu.VMEM((tokens, width), bf16),
            pltpu.VMEM((head, group * tokens), f32),
            pltpu.SemaphoreType.DMA((copies,)),
            pltpu.SemaphoreType.DMA((copies,)),
            pltpu.SemaphoreType.DMA((32,)),
        ],
        compiler_params=pltpu.CompilerParams(
            has_side_effects=True, vmem_limit_bytes=60 * 1024 * 1024
        ),
        cost_estimate=pl.CostEstimate(flops=12 * 10**9, bytes_accessed=10**8, transcendentals=10**7),
    )(hidden, *weights, gain_block, grad_out, *tables, *positions, *head_gains)


def half_turn(values):
    return pltpu.roll(values, values.shape[1] // 2, 1)


def scatter_sends(links, place, piece, landed, token_rows, columns):
    copies = []
    for step in z_steps:
        other = place.along_z(step)
        rows = pl.ds(pl.multiple_of(other * token_rows, token_rows), token_rows)
        copies.append(
            links.send(piece.at[rows, columns], landed.at[place.z, :, columns], z=other)
        )
    return copies


def total_of(landed):
    total = landed[0].astype(f32)
    for index in range(1, parts):
        total += landed[index].astype(f32)
    return total


def mlp_kernel(
    plane,
    cores,
    normed_in,
    gate_in,
    up_in,
    down_in,
    grad_in,
    residual_in,
    gains,
    output,
    gate_grad,
    up_grad,
    down_grad,
    grad_residual,
    gain_sum,
    normed,
    normed_turned,
    grad_rows,
    grad_turned,
    gate,
    up,
    down,
    act,
    d_gate,
    d_up,
    part_in,
    part_out,
    landed_in,
    landed_out,
    residual,
    stage,
    stage_sems,
    send_sems,
    recv_sems,
    local_sems,
):
    links = Links(send_sems, recv_sems, local_sems)
    place = Place(plane, cores)
    tokens, width = normed.shape
    token_rows = tokens // parts
    units = act.shape[1]
    block = width // parts
    tile = 256
    loads = [
        links.local(normed_in, normed),
        links.local(gate_in, gate),
        links.local(up_in, up),
        links.local(grad_in, grad_rows),
        links.local(down_in, down),
        links.local(residual_in, residual),
    ]
    for copy in loads[:3]:
        copy.wait()

    for copy in loads[3:]:
        copy.wait()

    def hidden_tile(index, carry):
        columns = pl.ds(pl.multiple_of(index * tile, tile), tile)
        gate_lin = multiply(normed[...], gate[:, :, :, columns].reshape(width, tile))
        up_lin = multiply(normed[...], up[:, :, :, columns].reshape(width, tile))
        grad_act = multiply(
            grad_rows[...].reshape(tokens, width), down[:, :, :, columns].reshape(width, tile)
        )
        sigmoid = jax.nn.sigmoid(gate_lin)
        silu = gate_lin * sigmoid
        act[:, columns] = (silu * up_lin).astype(bf16)
        d_up[:, columns] = (grad_act * silu).astype(bf16)
        d_gate[:, columns] = (grad_act * up_lin * (sigmoid + silu * (1.0 - sigmoid))).astype(bf16)
        return carry

    lax.fori_loop(0, units // tile, hidden_tile, 0)
    in_copies, out_copies = [], []
    own_rows = pl.ds(pl.multiple_of(place.z * token_rows, token_rows), token_rows)
    for index in range(parts):
        columns = pl.ds(index * block, block)
        part_in[:, columns] = (
            multiply_trans(d_gate[...], gate[index].reshape(block, units))
            + multiply_trans(d_up[...], up[index].reshape(block, units))
        ).astype(bf16)
        in_copies += scatter_sends(links, place, part_in, landed_in, token_rows, columns)
    landed_in[place.z] = part_in[own_rows]
    for index in range(parts):
        columns = pl.ds(index * block, block)
        part_out[:, columns] = multiply_trans(
            act[...], down[index].reshape(block, units)
        ).astype(bf16)
        out_copies += scatter_sends(links, place, part_out, landed_out, token_rows, columns)
    landed_out[place.z] = part_out[own_rows]

    for index in range(parts):
        columns = slice(index * block, (index + 1) * block)
        normed_turned[columns] = normed[:, columns].T
        grad_turned[columns] = grad_rows[:, :, columns].reshape(tokens, block).T

    writes = []
    turn = 0
    for left, right, target in (
        (normed_turned, d_gate, gate_grad),
        (normed_turned, d_up, up_grad),
        (grad_turned, act, down_grad),
    ):
        for index in range(parts):
            slot = turn % 2
            if turn >= 2:
                writes[turn - 2].wait()

            def weight_tile(place_at, carry):
                columns = pl.ds(pl.multiple_of(place_at * tile, tile), tile)
                rows = left[index * block : (index + 1) * block]
                product = multiply(rows, right[:, columns]).astype(bf16)
                stage[slot, :, :, columns] = product.reshape(stage.shape[1], stage.shape[2], tile)
                return carry

            lax.fori_loop(0, units // tile, weight_tile, 0)
            copy = pltpu.make_async_copy(
                stage.at[slot], target.at[:, index], stage_sems.at[turn]
            )
            copy.start()
            writes.append(copy)
            turn += 1

    for copy in in_copies:
        copy.wait_recv()
    grad_normed = total_of(landed_in)
    values = residual[...]
    scale = lax.rsqrt(jnp.mean(values * values, axis=-1, keepdims=True) + epsilon)
    unit = values * scale
    gain_sum[0:1] = jnp.zeros((1, width), f32)
    gain_sum[1:2] = jnp.sum(grad_normed * unit, axis=0, keepdims=True)
    own_grad = grad_rows[place.z].astype(f32)
    grad_residual[...] = own_grad + norm_back(grad_normed * gains[1:2], unit, scale)
    for copy in out_copies:
        copy.wait_recv()
    output[...] = (residual[...] + total_of(landed_out)).astype(bf16)
    for copy in writes[-2:]:
        copy.wait()
    links.finish()


def mlp(plane, cores, normed, gate, up, down, grad_rows, residual, gains):
    tokens, width = normed.shape
    token_rows = tokens // parts
    units = gate.shape[3]
    shard = gate.shape[2]
    columns = plane * cores
    any_space, vmem = pl.BlockSpec(memory_space=pl.ANY), pl.BlockSpec(memory_space=pltpu.VMEM)
    grads = jax.ShapeDtypeStruct((columns, parts, shard, units), bf16)
    return pl.pallas_call(
        functools.partial(mlp_kernel, plane, cores),
        out_shape=[
            jax.ShapeDtypeStruct((token_rows, width), bf16),
            grads,
            grads,
            grads,
            jax.ShapeDtypeStruct((token_rows, width), f32),
            jax.ShapeDtypeStruct((2, width), f32),
        ],
        in_specs=[any_space] * 6 + [vmem],
        out_specs=[vmem] + [any_space] * 3 + [vmem] * 2,
        scratch_shapes=[
            pltpu.VMEM((tokens, width), bf16),
            pltpu.VMEM((width, tokens), bf16),
            pltpu.VMEM((parts, token_rows, width), bf16),
            pltpu.VMEM((width, tokens), bf16),
            pltpu.VMEM((parts, columns, shard, units), bf16),
            pltpu.VMEM((parts, columns, shard, units), bf16),
            pltpu.VMEM((parts, columns, shard, units), bf16),
            pltpu.VMEM((tokens, units), bf16),
            pltpu.VMEM((tokens, units), bf16),
            pltpu.VMEM((tokens, units), bf16),
            pltpu.VMEM((tokens, width), bf16),
            pltpu.VMEM((tokens, width), bf16),
            pltpu.VMEM((parts, token_rows, width), bf16),
            pltpu.VMEM((parts, token_rows, width), bf16),
            pltpu.VMEM((token_rows, width), f32),
            pltpu.VMEM((2, columns, shard, units), bf16),
            pltpu.SemaphoreType.DMA((12,)),
            pltpu.SemaphoreType.DMA((24,)),
            pltpu.SemaphoreType.DMA((24,)),
            pltpu.SemaphoreType.DMA((6,)),
        ],
        compiler_params=pltpu.CompilerParams(
            has_side_effects=True, vmem_limit_bytes=62 * 1024 * 1024
        ),
        cost_estimate=pl.CostEstimate(flops=3 * 10**10, bytes_accessed=10**8, transcendentals=10**6),
    )(normed, gate, up, down, grad_rows, residual, gains)


def back_kernel(
    plane,
    cores,
    projection_in,
    out_in,
    normed_in,
    lin_in,
    queries_in,
    both_in,
    attended_in,
    hidden,
    grad_residual,
    stats,
    gains,
    gain_sum,
    cosine,
    sine_turned,
    query_pos,
    key_pos,
    query_gain,
    key_gain,
    input_grad,
    weight_grads,
    head_sums,
    projection,
    out_columns,
    normed,
    lin,
    queries,
    both,
    attended,
    low_rows,
    grad_heads,
    delta,
    both_grads,
    both_landed,
    query_total,
    grad_lin,
    part,
    landed,
    stage,
    gain_stage,
    sums,
    stage_sems,
    send_sems,
    recv_sems,
    local_sems,
):
    links = Links(send_sems, recv_sems, local_sems)
    place = Place(plane, cores)
    tokens, width = normed.shape
    token_rows = tokens // parts
    block = width // parts
    head = query_gain.shape[1]
    query_heads = queries.shape[0]
    query_width = query_heads * head
    key_width = both.shape[2] // 2
    key_heads = key_width // head
    group = query_heads // key_heads
    lin_width = query_width + 2 * key_width

    low_rows[place.z] = grad_residual[...].astype(bf16)
    own_low = low_rows.at[place.z]
    low_copies = [links.send(own_low, own_low, z=place.along_z(step)) for step in z_steps]
    out_at = pl.ds(pl.multiple_of(place.z * query_width, 128), query_width)
    loads = [
        links.local(out_in.at[:, :, :, out_at], out_columns),
        links.local(attended_in, attended),
        links.local(queries_in, queries),
        links.local(both_in, both),
        links.local(lin_in, lin),
        links.local(projection_in, projection),
        links.local(normed_in, normed),
    ]
    for copy in loads:
        copy.wait()
    for copy in low_copies:
        copy.wait_recv()

    tile = group * head
    for index in range(key_heads):
        columns = slice(index * tile, (index + 1) * tile)
        grads = multiply(
            low_rows[...].reshape(tokens, width), out_columns[:, :, :, columns].reshape(width, tile)
        ).astype(bf16)
        for member in range(group):
            number = index * group + member
            own = grads[:, member * head : (member + 1) * head]
            grad_heads[number] = own
            mixed = attended[:, number * head : (number + 1) * head].astype(f32)
            delta[number : number + 1] = jnp.sum(
                (own.astype(f32) * mixed).T, axis=0, keepdims=True
            )

    factor = head ** (-0.5)
    score_factor = factor * 1.4426950408889634
    chunk = min(256, tokens)
    chunks_each = tokens // chunk
    lanes = group * tokens
    both_copies = []
    for key_head in range(key_heads):
        members = slice(key_head * group, (key_head + 1) * group)
        query_block = queries[members].reshape(lanes, head)
        grad_block = grad_heads[members].reshape(lanes, head)
        numbers = range(key_head * group, (key_head + 1) * group)
        stats_row = jnp.concatenate([stats[number : number + 1] for number in numbers], axis=1)
        delta_row = jnp.concatenate([delta[number : number + 1] for number in numbers], axis=1)
        positions = jnp.concatenate([query_pos[...]] * group, axis=1)
        query_total[...] = jnp.zeros_like(query_total)

        def back_chunk(index, carry):
            source, row = index // chunks_each, index % chunks_each
            rows = pl.ds(pl.multiple_of(row * chunk, chunk), chunk)
            keys = both[source, rows, pl.ds(key_head * head, head)]
            values = both[source, rows, pl.ds(key_width + key_head * head, head)]
            scores = multiply_trans(keys, query_block) * score_factor
            spot = pl.ds(pl.multiple_of(index * chunk, chunk), chunk)
            weights = jnp.where(
                key_pos[spot] <= positions, jnp.exp2(scores - stats_row), 0.0
            )
            grad_weights = multiply_trans(values, grad_block)
            grad_scores = (weights * (grad_weights - delta_row)).astype(bf16)
            query_total[...] += outer_rows(keys, grad_scores)
            both_grads[key_head, source, rows, pl.ds(0, head)] = (
                multiply(grad_scores, query_block) * factor
            ).astype(bf16)
            both_grads[key_head, source, rows, pl.ds(head, head)] = multiply(
                weights.astype(bf16), grad_block
            ).astype(bf16)
            return carry

        lax.fori_loop(0, plane * chunks_each, back_chunk, 0)
        both_landed[key_head, place.p] = both_grads[key_head, place.p]
        for step in range(1, plane):
            other = place.in_plane(step)
            both_copies.append(
                links.send(
                    both_grads.at[key_head, other], both_landed.at[key_head, place.p], p=other
                )
            )
        grad_queries = query_total[...].T * factor
        for member in range(group):
            number = key_head * group + member
            rows = slice(member * tokens, (member + 1) * tokens)
            own = grad_queries[rows]
            lin_rows = lin[:, number * head : (number + 1) * head]
            scale = lax.rsqrt(jnp.mean(lin_rows * lin_rows, axis=-1, keepdims=True) + epsilon)
            unit = lin_rows * scale
            turned = own * cosine[...] - half_turn(own) * sine_turned[...]
            gained = jnp.sum(turned * unit, axis=0, keepdims=True)
            if number == 0:
                sums[place.z, 0:1] = gained
            else:
                sums[place.z, 0:1] = sums[place.z, 0:1] + gained
            grad_lin[:, number * head : (number + 1) * head] = norm_back(
                turned * query_gain[...], unit, scale
            ).astype(bf16)

    writes = []

    def write_rows(left, right, start, index):
        turn = len(writes)
        slot = turn % 2
        if turn >= 2:
            writes[turn - 2].wait()
        size = right.shape[1]
        product = outer_rows(left, right).astype(bf16)
        stage[slot, :, :, 0:size] = product.reshape(stage.shape[1], stage.shape[2], size)
        copy = pltpu.make_async_copy(
            stage.at[slot, :, :, pl.ds(0, size)],
            weight_grads.at[:, index, :, pl.ds(start, size)],
            stage_sems.at[turn],
        )
        copy.start()
        writes.append(copy)

    for index in range(parts):
        left = low_rows[:, :, index * block : (index + 1) * block].reshape(tokens, block)
        write_rows(left, attended[...], lin_width, index)

    for copy in both_copies:
        copy.wait_recv()
    for key_head in range(key_heads):
        own = both_landed[key_head, 0].astype(f32)
        for source in range(1, plane):
            own += both_landed[key_head, source].astype(f32)
        at = query_width + key_width + key_head * head
        grad_lin[:, at : at + head] = own[:, head:].astype(bf16)
        own = own[:, :head]
        at = query_width + key_head * head
        lin_rows = lin[:, at : at + head]
        scale = lax.rsqrt(jnp.mean(lin_rows * lin_rows, axis=-1, keepdims=True) + epsilon)
        unit = lin_rows * scale
        turned = own * cosine[...] - half_turn(own) * sine_turned[...]
        gained = jnp.sum(turned * unit, axis=0, keepdims=True)
        if key_head == 0:
            sums[place.z, 1:2] = gained
        else:
            sums[place.z, 1:2] = sums[place.z, 1:2] + gained
        grad_lin[:, at : at + head] = norm_back(turned * key_gain[...], unit, scale).astype(bf16)
    head_sums[...] = sums[place.z]

    landed_copies = []
    for index in range(parts):
        columns = pl.ds(index * block, block)
        part[:, columns] = multiply_trans(
            grad_lin[...], projection[index, :, :, 0:lin_width].reshape(block, lin_width)
        ).astype(bf16)
        landed_copies += scatter_sends(links, place, part, landed, token_rows, columns)
    own_rows = pl.ds(pl.multiple_of(place.z * token_rows, token_rows), token_rows)
    landed[place.z] = part[own_rows]
    for index in range(parts):
        left = normed[:, index * block : (index + 1) * block]
        write_rows(left, grad_lin[...], 0, index)

    for copy in landed_copies:
        copy.wait_recv()
    grad_normed = total_of(landed)
    values = hidden[...].astype(f32)
    scale = lax.rsqrt(jnp.mean(values * values, axis=-1, keepdims=True) + epsilon)
    unit = values * scale
    gain_stage[...] = jnp.zeros_like(gain_stage)
    gain_stage[0:1] = jnp.sum(grad_normed * unit, axis=0, keepdims=True)
    gain_stage[1:2] = gain_sum[1:2]
    input_grad[...] = (
        grad_residual[...] + norm_back(grad_normed * gains[0:1], unit, scale)
    ).astype(bf16)
    gain_columns = gain_stage[...].T.astype(bf16)
    for index in range(parts):
        turn = len(writes)
        slot = turn % 2
        writes[turn - 2].wait()
        stage[slot, :, :, 0:128] = gain_columns[index * block : (index + 1) * block].reshape(
            stage.shape[1], stage.shape[2], 128
        )
        copy = pltpu.make_async_copy(
            stage.at[slot, :, :, pl.ds(0, 128)],
            weight_grads.at[:, index, :, pl.ds(lin_width + query_width, 128)],
            stage_sems.at[turn],
        )
        copy.start()
        writes.append(copy)
    for copy in writes[-2:]:
        copy.wait()
    links.finish()


def back(plane, cores, large, small):
    projection, out_full, normed, lin, queries, both, attended = large
    tokens, width = normed.shape
    token_rows = tokens // parts
    shard = projection.shape[2]
    columns = plane * cores
    query_heads, _, head = queries.shape
    query_width = query_heads * head
    key_width = both.shape[2] // 2
    key_heads = key_width // head
    lin_width = query_width + 2 * key_width
    group = query_heads // key_heads
    any_space, vmem = pl.BlockSpec(memory_space=pl.ANY), pl.BlockSpec(memory_space=pltpu.VMEM)
    copies = 3 + 2 * (plane - 1) + 12
    return pl.pallas_call(
        functools.partial(back_kernel, plane, cores),
        out_shape=[
            jax.ShapeDtypeStruct((token_rows, width), bf16),
            jax.ShapeDtypeStruct((columns, parts, shard, lin_width + query_width + 128), bf16),
            jax.ShapeDtypeStruct((8, head), f32),
        ],
        in_specs=[any_space] * 7 + [vmem] * 11,
        out_specs=[vmem, any_space, vmem],
        scratch_shapes=[
            pltpu.VMEM(projection.shape, bf16),
            pltpu.VMEM((parts, columns, shard, query_width), bf16),
            pltpu.VMEM((tokens, width), bf16),
            pltpu.VMEM(lin.shape, f32),
            pltpu.VMEM(queries.shape, bf16),
            pltpu.VMEM(both.shape, bf16),
            pltpu.VMEM(attended.shape, bf16),
            pltpu.VMEM((parts, token_rows, width), bf16),
            pltpu.VMEM(queries.shape, bf16),
            pltpu.VMEM((8, tokens), f32),
            pltpu.VMEM((key_heads, plane, tokens, 2 * head), bf16),
            pltpu.VMEM((key_heads, plane, tokens, 2 * head), bf16),
            pltpu.VMEM((head, group * tokens), f32),
            pltpu.VMEM((tokens, lin_width), bf16),
            pltpu.VMEM((tokens, width), bf16),
            pltpu.VMEM((parts, token_rows, width), bf16),
            pltpu.VMEM((2, columns, shard, lin_width), bf16),
            pltpu.VMEM((128, width), f32),
            pltpu.VMEM((parts, 8, head), f32),
            pltpu.SemaphoreType.DMA((12,)),
            pltpu.SemaphoreType.DMA((copies,)),
            pltpu.SemaphoreType.DMA((copies,)),
            pltpu.SemaphoreType.DMA((8,)),
        ],
        compiler_params=pltpu.CompilerParams(
            has_side_effects=True, vmem_limit_bytes=62 * 1024 * 1024
        ),
        cost_estimate=pl.CostEstimate(flops=10**10, bytes_accessed=10**8, transcendentals=10**7),
    )(*large, *small)


def make_local(plane, cores):
    def return_columns(grads):
        grads = grads.reshape(-1, grads.shape[3])
        summed = lax.psum_scatter(grads, ("p", "c"), scatter_dimension=0, tiled=True)
        pieces = summed.reshape(parts, summed.shape[0] // parts, summed.shape[1])
        return lax.all_to_all(pieces, "z", 0, 0, tiled=True)

    def local(
        hidden_in,
        block_map,
        query_weight,
        key_weight,
        value_weight,
        out_weight,
        gate_weight,
        up_weight,
        down_weight,
        attention_norm_gain,
        feedforward_gain,
        query_gain,
        key_gain,
        output_grad,
    ):
        shard = query_weight.shape[0]
        hidden_own, grad_own = hidden_in[0], output_grad[0]
        row_count, features = hidden_own.shape
        piece_rows = row_count // 2
        head_width = query_gain.shape[0]
        query_heads = query_weight.shape[1] // head_width // parts
        key_heads = key_weight.shape[1] // head_width // parts
        group_size = query_heads // key_heads
        query_width = query_heads * head_width
        key_width = key_heads * head_width
        hidden_units = gate_weight.shape[1] // parts
        p_index = lax.axis_index("p")
        tokens = parts * row_count

        blocks = block_map[0].reshape(parts, plane, 2)
        offsets = jnp.arange(piece_rows, dtype=jnp.int32)
        all_pos = blocks.transpose(1, 0, 2)[..., None] * piece_rows + offsets
        all_pos = all_pos.reshape(plane, tokens)
        query_pos = lax.dynamic_index_in_dim(all_pos, p_index, 0, keepdims=False)
        key_pos = all_pos.reshape(-1)
        cosine, sine_table = rope_tables(query_pos, head_width)
        sign = jnp.where(jnp.arange(head_width) < head_width // 2, -1.0, 1.0).astype(f32)
        query_gain_float = query_gain.astype(f32)
        key_gain_float = key_gain.astype(f32)
        gain_block = jnp.stack([attention_norm_gain, feedforward_gain], axis=1)
        gain_block = jnp.pad(gain_block, ((0, 0), (0, 126)))

        (
            normed,
            projection,
            lin,
            queries,
            both,
            attended_low,
            out_full,
            normed_mlp,
            own_residual,
            gate_columns,
            up_columns,
            down_columns,
            grad_rows,
            stats,
            gains,
        ) = front(
            plane,
            cores,
            hidden_own,
            (
                query_weight,
                key_weight,
                value_weight,
                out_weight,
                gate_weight,
                up_weight,
                down_weight,
            ),
            gain_block,
            grad_own,
            (cosine[:, 0], sine_table[:, 0] * sign),
            (query_pos[None], key_pos[:, None]),
            (query_gain_float[None], key_gain_float[None]),
        )
        output, gate_grads, up_grads, down_grads, grad_residual, gain_sum = mlp(
            plane,
            cores,
            normed_mlp,
            gate_columns,
            up_columns,
            down_columns,
            grad_rows,
            own_residual,
            gains,
        )
        down_pieces = return_columns(down_grads)
        gate_pieces = return_columns(gate_grads)
        up_pieces = return_columns(up_grads)
        input_grad, attention_grads, head_sums = back(
            plane,
            cores,
            (projection, out_full, normed, lin, queries, both, attended_low),
            (
                hidden_own,
                grad_residual,
                stats,
                gains,
                gain_sum,
                cosine[:, 0],
                sine_table[:, 0] * sign,
                query_pos[None],
                key_pos[:, None],
                query_gain_float[None],
                key_gain_float[None],
            ),
        )
        attention_pieces = return_columns(attention_grads)
        head_sums = lax.psum(head_sums[:2], ("z", "p", "c"))
        ends = [query_width, query_width + key_width, query_width + 2 * key_width]
        ends.append(ends[2] + query_width)
        gain_sums = jnp.sum(attention_pieces[:, :, ends[3] : ends[3] + 2].astype(f32), axis=0)
        return (
            output[None],
            input_grad[None],
            spread(attention_pieces[:, :, : ends[0]]),
            spread(attention_pieces[:, :, ends[0] : ends[1]]),
            spread(attention_pieces[:, :, ends[1] : ends[2]]),
            spread(attention_pieces[:, :, ends[2] : ends[3]]),
            spread(gate_pieces),
            spread(up_pieces),
            spread(down_pieces),
            gain_sums[:, 0],
            gain_sums[:, 1],
            head_sums[0],
            head_sums[1],
        )

    return local


def solution(mesh):
    ctx_count, core_count = mesh.shape["ctx"], mesh.shape["fsdp"]
    plane = ctx_count // parts
    fine_mesh = Mesh(mesh.devices.reshape(parts, plane, core_count), ("z", "p", "c"))
    token_spec = P("c", ("z", "p"), None)
    weight_spec = P(("z", "p", "c"), None)
    gain_spec = P(("z", "p", "c"))
    return jax.shard_map(
        make_local(plane, core_count),
        mesh=fine_mesh,
        in_specs=(
            (token_spec, P("c", None)) + (weight_spec,) * 7 + (gain_spec,) * 2 + (P(), P(), token_spec)
        ),
        out_specs=(token_spec,) * 2 + (weight_spec,) * 7 + (gain_spec,) * 2 + (P(), P()),
        check_vma=False,
    )
```

```python
import functools

import jax
import jax.numpy as jnp
from jax import lax
from jax.experimental import pallas as pl
from jax.experimental.pallas import tpu as pltpu
from jax.sharding import Mesh, PartitionSpec as P

epsilon = 1e-06
rotary_base = 1000000.0
masked_score = -1e30
parts = 4
bf16 = jnp.bfloat16
f32 = jnp.float32


def unit_rows(values):
    scale_row = lax.rsqrt(jnp.mean(values * values, axis=-1, keepdims=True) + epsilon)
    return values * scale_row, scale_row


def norm_back(weighted, unit, scale_row):
    inner_mean = jnp.mean(weighted * unit, axis=-1, keepdims=True)
    return scale_row * (weighted - unit * inner_mean)


def rope_tables(positions, width):
    half_width = width // 2
    frequency = rotary_base ** (-(jnp.arange(half_width, dtype=f32) * 2.0 / width))
    angles = positions.astype(f32)[:, None] * frequency[None, :]
    angles = jnp.concatenate([angles, angles], axis=-1)
    return jnp.cos(angles)[:, None, :], jnp.sin(angles)[:, None, :]


def rotate(values, cosine, sine_table):
    half_width = values.shape[-1] // 2
    turned = jnp.concatenate([-values[..., half_width:], values[..., :half_width]], axis=-1)
    return values * cosine + turned * sine_table


def rotate_back(grads, cosine, sine_table):
    half_width = grads.shape[-1] // 2
    shifted = grads * sine_table
    turned = jnp.concatenate([shifted[..., half_width:], -shifted[..., :half_width]], axis=-1)
    return grads * cosine + turned


def multiply(left, right):
    return jnp.dot(left, right, preferred_element_type=f32)


def multiply_trans(left, right):
    return lax.dot_general(left, right, (((1,), (1,)), ((), ())), preferred_element_type=f32)


def outer_rows(left, right):
    return lax.dot_general(left, right, (((0,), (0,)), ((), ())), preferred_element_type=f32)


class Part:
    def __init__(self, ref, index=None):
        self.ref, self.index = ref, index

    def __getitem__(self, index):
        return Part(self.ref, index)

    def get(self):
        return self.ref if self.index is None else self.ref.at[self.index]


def at(ref):
    return Part(ref)


def found(ref):
    return ref.get() if isinstance(ref, Part) else ref


class Copy:
    def __init__(self, source, target, sems, device=None):
        self.source, self.target, self.sems, self.device = source, target, sems, device
        self.describe().start()

    def describe(self):
        source, target = found(self.source), found(self.target)
        sems = [array.at[index] for array, index in self.sems]
        if self.device is None:
            return pltpu.make_async_copy(source, target, sems[0])
        return pltpu.make_async_remote_copy(
            src_ref=source,
            dst_ref=target,
            send_sem=sems[0],
            recv_sem=sems[1],
            device_id=self.device,
            device_id_type=pl.DeviceIdType.MESH,
        )

    def wait(self):
        self.describe().wait()

    def wait_send(self):
        self.describe().wait_send()

    def wait_recv(self):
        self.describe().wait_recv()


class Links:
    def __init__(self, send_sems, recv_sems, local_sems):
        self.send_sems, self.recv_sems, self.local_sems = send_sems, recv_sems, local_sems
        self.count, self.local_count = 0, 0
        self.sent, self.kept = [], []

    def send(self, source, target, tracked=True, **device):
        index = self.count
        self.count += 1
        copy = Copy(source, target, [(self.send_sems, index), (self.recv_sems, index)], device)
        if tracked:
            self.sent.append(copy)
        return copy

    def local(self, source, target):
        index = self.local_count
        self.local_count += 1
        return Copy(source, target, [(self.local_sems, index)])

    def keep(self, source, target):
        self.kept.append(self.local(source, target))

    def finish(self):
        assert self.count <= self.send_sems.shape[0]
        assert self.local_count <= self.local_sems.shape[0]
        for copy in self.sent:
            copy.wait_send()
        for copy in self.kept:
            copy.wait()


class Place:
    def __init__(self, plane, cores, token_rows):
        self.plane, self.cores = plane, cores
        self.z, self.p, self.c = (lax.axis_index(axis) for axis in ("z", "p", "c"))
        self.column = self.p * cores + self.c
        self.other_core = lax.rem(self.c + 1, cores)
        self.z_others = [lax.rem(self.z + step, parts) for step in range(parts)]
        self.p_others = [lax.rem(self.p + step, plane) for step in range(plane)]
        self.columns_before = [
            lax.rem(self.p + plane - step, plane) * cores + self.c for step in range(plane)
        ]
        self.z_rows = [
            pl.ds(pl.multiple_of(other * token_rows, token_rows), token_rows)
            for other in self.z_others
        ]

    def along_z(self, step):
        return self.z_others[step]

    def in_plane(self, step):
        return self.p_others[step]

    def before(self, step):
        return self.columns_before[step]

    def siblings(self):
        return [self.other_core]


z_steps = (1, 3, 2)


class Fetch:
    def __init__(self, links, place, pieces, gathered):
        self.links, self.place, self.pieces, self.gathered = links, place, pieces, gathered

    def begin(self):
        links, place = self.links, self.place
        mine = self.gathered.at[place.z, place.column]
        self.first, self.own = [], []
        for shard, width, start, split in self.pieces:
            for step in z_steps:
                other = place.along_z(step)
                first = pl.multiple_of(other * width, 128) if split else 0
                self.first.append(
                    links.send(shard.at[:, pl.ds(first, width)], mine.at[:, pl.ds(start, width)], z=other)
                )
            first = pl.multiple_of(place.z * width, 128) if split else 0
            self.own.append(
                links.local(shard.at[:, pl.ds(first, width)], mine.at[:, pl.ds(start, width)])
            )

    def spread(self):
        links, place = self.links, self.place
        for copy in self.own:
            copy.wait()
        for copy in self.first:
            copy.wait_recv()
        block = self.gathered.at[:, place.column]
        self.second = [
            links.send(block, block, p=place.in_plane(step)) for step in range(1, place.plane)
        ]
        self.third = [links.send(block, block, c=other) for other in place.siblings()]

    def forward(self):
        links, place = self.links, self.place
        for step, copy in enumerate(self.second, 1):
            copy.wait_recv()
            block = self.gathered.at[:, place.before(step)]
            self.third += [links.send(block, block, c=other) for other in place.siblings()]

    def finish(self):
        for copy in self.third:
            copy.wait_recv()


def front_kernel(
    plane,
    cores,
    hidden,
    query_weight,
    key_weight,
    value_weight,
    out_weight,
    gate_weight,
    up_weight,
    down_weight,
    gain_block,
    grad_out,
    cosine,
    sine_turned,
    query_pos,
    key_pos,
    query_gain,
    key_gain,
    normed_out,
    projection_out,
    lin_out,
    queries_out,
    both_out,
    attended_out,
    out_columns_out,
    normed_mlp_out,
    residual_out,
    gate_out,
    up_out,
    down_out,
    grad_rows_out,
    stats_out,
    gains_out,
    hidden_all,
    normed,
    projection,
    lin,
    queries,
    both,
    attended_all,
    out_full,
    residual,
    normed_mlp,
    mixed,
    send_sems,
    recv_sems,
    local_sems,
):
    links = Links(send_sems, recv_sems, local_sems)
    token_rows, width = hidden.shape
    place = Place(plane, cores, token_rows)
    tokens = parts * token_rows
    head = query_gain.shape[1]
    query_width = query_weight.shape[1] // parts
    key_width = key_weight.shape[1] // parts
    query_heads, key_heads = query_width // head, key_width // head
    group = query_heads // key_heads
    hidden_units = gate_weight.shape[1] // parts
    lin_width = query_width + 2 * key_width

    heads_fetch = Fetch(
        links,
        place,
        [
            (query_weight, query_width, 0, True),
            (key_weight, key_width, query_width, True),
            (value_weight, key_width, query_width + key_width, True),
            (gain_block, 128, lin_width, False),
        ],
        projection,
    )
    out_fetch = Fetch(links, place, [(out_weight, out_weight.shape[1], 0, False)], out_full)
    mlp_fetches = [
        Fetch(links, place, [(weight, hidden_units, 0, True)], target)
        for weight, target in ((gate_weight, gate_out), (up_weight, up_out), (down_weight, down_out))
    ]
    heads_fetch.begin()
    hidden_copies = [
        links.send(hidden, hidden_all.at[place.z], z=place.along_z(step)) for step in z_steps
    ]
    hidden_own = links.local(hidden, hidden_all.at[place.z])
    heads_fetch.spread()
    out_fetch.begin()
    for fetch in mlp_fetches:
        fetch.begin()
    hidden_own.wait()
    for copy in hidden_copies:
        copy.wait_recv()
    heads_fetch.forward()
    heads_fetch.finish()
    links.keep(projection, projection_out)

    gain_columns = projection[:, :, :, lin_width : lin_width + 128].reshape(width, 128)
    gain_rows = gain_columns.astype(f32).T
    gains_out[...] = gain_rows[:8]

    def norm_one(index, carry):
        values = hidden_all[index].astype(f32)
        scale = lax.rsqrt(jnp.mean(values * values, axis=-1, keepdims=True) + epsilon)
        rows = pl.ds(pl.multiple_of(index * token_rows, token_rows), token_rows)
        normed[rows] = (values * scale * gains_out[0:1]).astype(bf16)
        return carry

    lax.fori_loop(0, parts, norm_one, 0)
    links.keep(normed, normed_out)

    tile = 2 * head

    def project(index, carry):
        columns = pl.ds(pl.multiple_of(index * tile, tile), tile)
        weights = projection[:, :, :, columns].reshape(width, tile)
        lin[:, columns] = jnp.dot(normed[...], weights, preferred_element_type=f32)
        return carry

    lax.fori_loop(0, lin_width // tile, project, 0)
    own_both = both.at[place.p]

    def rope(values, gain):
        scale = lax.rsqrt(jnp.mean(values * values, axis=-1, keepdims=True) + epsilon)
        gained = values * scale * gain
        turned = pltpu.roll(gained, head // 2, 1)
        return (gained * cosine[...] + turned * sine_turned[...]).astype(bf16)

    for index in range(key_heads):
        columns = slice(query_width + index * head, query_width + (index + 1) * head)
        own_both[:, index * head : (index + 1) * head] = rope(lin[:, columns], key_gain[...])
    own_both[:, key_width:] = lin[:, query_width + key_width :].astype(bf16)
    both_copies = [
        links.send(own_both, own_both, p=place.in_plane(step)) for step in range(1, plane)
    ]
    for index in range(query_heads):
        columns = slice(index * head, (index + 1) * head)
        queries[index] = rope(lin[:, columns], query_gain[...])
    links.keep(lin.at[:, pl.ds(0, query_width + key_width)], lin_out)
    links.keep(queries, queries_out)
    out_fetch.spread()
    mlp_fetches[0].spread()
    for copy in both_copies:
        copy.wait_recv()
    links.keep(both, both_out)

    factor = head ** (-0.5) * 1.4426950408889634
    chunk = min(256, tokens)
    chunks_each = tokens // chunk
    lanes = group * tokens
    own_attended = attended_all.at[place.z]
    attended_copies = []
    for key_head in range(key_heads):
        block = queries[key_head * group : (key_head + 1) * group].reshape(lanes, head)
        positions = jnp.concatenate([query_pos[...]] * group, axis=1)
        mixed[...] = jnp.zeros_like(mixed)

        def attend_chunk(index, carry):
            best, summed = carry
            source, row = index // chunks_each, index % chunks_each
            rows = pl.ds(pl.multiple_of(row * chunk, chunk), chunk)
            keys = both[source, rows, pl.ds(key_head * head, head)]
            values = both[source, rows, pl.ds(key_width + key_head * head, head)]
            scores = multiply_trans(keys, block) * factor
            spot = pl.ds(pl.multiple_of(index * chunk, chunk), chunk)
            scores = jnp.where(key_pos[spot] <= positions, scores, masked_score)
            new_best = jnp.maximum(best, jnp.max(scores, axis=0, keepdims=True))
            weights = jnp.exp2(scores - new_best)
            shrink = jnp.exp2(best - new_best)
            summed = summed * shrink + jnp.sum(weights, axis=0, keepdims=True)
            mixed[...] = mixed[...] * shrink + outer_rows(values, weights.astype(bf16))
            return new_best, summed

        best, summed = lax.fori_loop(
            0,
            plane * chunks_each,
            attend_chunk,
            (jnp.full((1, lanes), masked_score, f32), jnp.zeros((1, lanes), f32)),
        )
        mixed_rows = (mixed[...] / summed).T
        stats = best + jnp.log2(summed)
        for member in range(group):
            index = key_head * group + member
            stats_out[index : index + 1] = stats[:, member * tokens : (member + 1) * tokens]
            own_attended[:, index * head : (index + 1) * head] = mixed_rows[
                member * tokens : (member + 1) * tokens
            ].astype(bf16)
        part = own_attended.at[:, pl.ds(key_head * group * head, group * head)]
        attended_copies += [links.send(part, part, z=place.along_z(step)) for step in z_steps]
        if key_head == 0:
            out_fetch.forward()
            mlp_fetches[1].spread()
    grad_copies = [
        links.send(grad_out, grad_rows_out.at[place.z], z=place.along_z(step)) for step in z_steps
    ]
    links.keep(grad_out, grad_rows_out.at[place.z])
    links.keep(own_attended, attended_out)
    mlp_fetches[2].spread()
    out_fetch.finish()
    links.keep(out_full, out_columns_out)
    for copy in attended_copies:
        copy.wait_recv()

    def add_out(index, carry):
        weights = out_full[index].reshape(width // parts, parts * query_width)
        columns = pl.ds(pl.multiple_of(index * (width // parts), 128), width // parts)
        total = hidden_all[:, :, columns].reshape(tokens, width // parts).astype(f32)
        for other in range(parts):
            total += multiply_trans(
                attended_all[other], weights[:, other * query_width : (other + 1) * query_width]
            )
        residual[:, columns] = total
        return carry

    lax.fori_loop(0, parts, add_out, 0)
    mlp_fetches[0].forward()

    def norm_two(index, carry):
        rows = pl.ds(pl.multiple_of(index * token_rows, token_rows), token_rows)
        values = residual[rows]
        scale = lax.rsqrt(jnp.mean(values * values, axis=-1, keepdims=True) + epsilon)
        normed_mlp[rows] = (values * scale * gains_out[1:2]).astype(bf16)
        return carry

    lax.fori_loop(0, parts, norm_two, 0)
    links.keep(normed_mlp, normed_mlp_out)
    own_rows = place.z_rows[0]
    links.keep(residual.at[own_rows], residual_out)
    mlp_fetches[1].forward()
    mlp_fetches[2].forward()
    for copy in grad_copies:
        copy.wait_recv()
    for fetch in mlp_fetches:
        fetch.finish()
    links.finish()


def front(plane, cores, hidden, weights, gain_block, grad_out, tables, positions, head_gains):
    token_rows, width = hidden.shape
    tokens = parts * token_rows
    shard = weights[0].shape[0]
    head = head_gains[0].shape[1]
    query_width, key_width = weights[0].shape[1] // parts, weights[1].shape[1] // parts
    hidden_units = weights[4].shape[1] // parts
    lin_width = query_width + 2 * key_width
    query_heads = query_width // head
    group = query_width // key_width
    stacked = (parts, plane * cores, shard)
    copies = 3 * 7 + 3 * 3 + 3 * 2 + 5 * (2 * plane - 1) + plane + 8
    any_space, vmem = pl.BlockSpec(memory_space=pl.ANY), pl.BlockSpec(memory_space=pltpu.VMEM)
    outputs = [
        ((tokens, width), bf16),
        (stacked + (lin_width + 128,), bf16),
        ((tokens, query_width + key_width), f32),
        ((query_heads, tokens, head), bf16),
        ((plane, tokens, 2 * key_width), bf16),
        ((tokens, query_width), bf16),
        (stacked + (parts * query_width,), bf16),
        ((tokens, width), bf16),
        ((token_rows, width), f32),
        (stacked + (hidden_units,), bf16),
        (stacked + (hidden_units,), bf16),
        (stacked + (hidden_units,), bf16),
        ((parts, token_rows, width), bf16),
        ((8, tokens), f32),
        ((8, width), f32),
    ]
    return pl.pallas_call(
        functools.partial(front_kernel, plane, cores),
        out_shape=[jax.ShapeDtypeStruct(shape, kind) for shape, kind in outputs],
        in_specs=[any_space] * 10 + [vmem] * 6,
        out_specs=[any_space] * 13 + [vmem] * 2,
        scratch_shapes=[
            pltpu.VMEM((parts, token_rows, width), bf16),
            pltpu.VMEM((tokens, width), bf16),
            pltpu.VMEM(stacked + (lin_width + 128,), bf16),
            pltpu.VMEM((tokens, lin_width), f32),
            pltpu.VMEM((query_heads, tokens, head), bf16),
            pltpu.VMEM((plane, tokens, 2 * key_width), bf16),
            pltpu.VMEM((parts, tokens, query_width), bf16),
            pltpu.VMEM(stacked + (parts * query_width,), bf16),
            pltpu.VMEM((tokens, width), f32),
            pltpu.VMEM((tokens, width), bf16),
            pltpu.VMEM((head, group * tokens), f32),
            pltpu.SemaphoreType.DMA((copies,)),
            pltpu.SemaphoreType.DMA((copies,)),
            pltpu.SemaphoreType.DMA((32,)),
        ],
        compiler_params=pltpu.CompilerParams(
            has_side_effects=True, vmem_limit_bytes=60 * 1024 * 1024
        ),
        cost_estimate=pl.CostEstimate(flops=12 * 10**9, bytes_accessed=10**8, transcendentals=10**7),
    )(hidden, *weights, gain_block, grad_out, *tables, *positions, *head_gains)


def half_turn(values):
    return pltpu.roll(values, values.shape[1] // 2, 1)


def scatter_sends(links, place, piece, landed, token_rows, columns, tracked=True):
    copies = []
    for step in z_steps:
        other = place.along_z(step)
        rows = place.z_rows[step]
        copies.append(
            links.send(
                at(piece)[rows, columns], at(landed)[place.z, :, columns], tracked, z=other
            )
        )
    return copies


def total_of(landed):
    total = landed[0].astype(f32)
    for index in range(1, parts):
        total += landed[index].astype(f32)
    return total


class Returns:
    def __init__(self, links, place, ring, addend, ring_sems, buffers):
        self.links, self.place, self.ring, self.addend = links, place, ring, addend
        self.ring_sems = ring_sems
        self.from_sibling, self.halves, self.from_plane, self.sums, self.final = buffers
        self.pending = [[] for _ in range(ring.shape[0])]
        self.turn, self.used = 0, 0
        self.sibling_copies, self.plane_copies, self.z_copies = {}, {}, {}
        self.mine, self.own_final = {}, {}

    def slot(self):
        slot = self.turn % len(self.pending)
        self.turn += 1
        for wait in self.pending[slot]:
            wait()
        self.pending[slot] = []
        return slot

    def local(self, source, target):
        self.used += 1
        return Copy(source, target, [(self.ring_sems, self.used - 1)])

    def product(self, slot, left, half, right, start, index, added):
        size = right.shape[1]
        tile = 512 if size % 512 == 0 else 256

        def tile_of(step, carry):
            columns = pl.ds(pl.multiple_of(step * tile, tile), tile)
            target = pl.ds(pl.multiple_of(start + step * tile, 128), tile)
            rows = left[index, :, half]
            value = multiply(rows.reshape(-1, rows.shape[2]), right[:, columns])
            value = value.reshape(rows.shape[0], rows.shape[1], tile)
            if added is not None:
                value += self.addend[added, :, :, target].astype(f32)
            self.ring[slot, :, :, target] = value.astype(bf16)
            return carry

        lax.fori_loop(0, size // tile, tile_of, 0)

    def give(self, family, left, right, start=0):
        place, size = self.place, right.shape[1]
        other = place.other_core
        columns = pl.ds(start, size)
        for index in range(parts):
            slot = self.slot()
            self.product(slot, left, other, right, start, index, None)
            copy = self.links.send(
                at(self.ring)[slot, :, :, columns],
                at(self.from_sibling)[family, index, :, :, columns],
                tracked=False,
                c=other,
            )
            self.pending[slot].append(copy.wait_send)
            self.sibling_copies[family, start, index] = copy

    def take(self, family, left, right, start=0):
        size = right.shape[1]
        columns = pl.ds(start, size)
        kept = []
        for index in range(parts):
            slot = self.slot()
            self.sibling_copies[family, start, index].wait_recv()
            side = 0
            load = self.local(
                at(self.from_sibling)[family, index, :, :, columns],
                at(self.addend)[side, :, :, columns],
            )
            load.wait()
            self.product(slot, left, self.place.c, right, start, index, side)
            copy = self.local(
                at(self.ring)[slot, :, :, columns], at(self.halves)[family, index, :, :, columns]
            )
            kept.append(copy)
            self.pending[slot].append(lambda: None)
            if index >= 1:
                kept[index - 1].wait()
        kept[-1].wait()
        self.send_plane(family, columns)

    def send_plane(self, family, columns):
        links, place = self.links, self.place
        copies = []
        for step in range(1, place.plane):
            other = place.in_plane(step)
            copies.append(
                links.send(
                    at(self.halves)[family, :, other, :, columns],
                    at(self.from_plane)[family, place.p, :, :, columns],
                    p=other,
                )
            )
        self.plane_copies.setdefault(family, []).extend(copies)
        self.mine.setdefault(family, []).append(
            self.local(
                at(self.halves)[family, :, place.p, :, columns],
                at(self.from_plane)[family, place.p, :, :, columns],
            )
        )

    def along_z(self, family):
        links, place = self.links, self.place
        for copy in self.plane_copies[family]:
            copy.wait_recv()
        for copy in self.mine[family]:
            copy.wait()
        loads = []
        for index in range(parts):
            slot = self.slot()
            loads.append(
                (slot, self.local(at(self.from_plane)[family, :, index], at(self.ring)[slot]))
            )
        for index, (slot, load) in enumerate(loads):
            load.wait()
            total = self.ring[slot, 0].astype(f32)
            for source in range(1, place.plane):
                total += self.ring[slot, source].astype(f32)
            self.sums[family, index] = total.astype(bf16)
        copies = []
        for step in z_steps:
            other = place.along_z(step)
            copies.append(
                links.send(at(self.sums)[family, other], at(self.final)[family, place.z], z=other)
            )
        self.own_final[family] = self.local(
            at(self.sums)[family, place.z], at(self.final)[family, place.z]
        )
        self.z_copies[family] = copies

    def home(self, family, stage, stage_sems, targets):
        for copy in self.z_copies[family]:
            copy.wait_recv()
        self.own_final[family].wait()
        loads = []
        for index in range(parts):
            loaded = self.slot()
            loads.append(
                (loaded, self.local(at(self.final)[family, index], at(self.ring)[loaded, 0]))
            )
        for index in range(parts):
            slot = self.out_turn % stage.shape[0]
            for copy in self.out_pending[slot]:
                copy.wait()
            loaded, load = loads[index]
            load.wait()
            stage[slot] = self.ring[loaded, 0].astype(f32)
            self.out_pending[slot] = []
            for target, start, width in targets:
                copy = Copy(
                    at(stage)[slot, :, pl.ds(start, width)],
                    at(target)[:, pl.ds(index * width, width)],
                    [(stage_sems, self.out_used)],
                )
                self.out_used += 1
                self.out_pending[slot].append(copy)
            self.out_turn += 1

    out_turn = 0
    out_used = 0

    def finish(self):
        assert self.used <= self.ring_sems.shape[0]
        for waits in self.pending:
            for wait in waits:
                wait()
        for copies in self.out_pending:
            for copy in copies:
                copy.wait()


def rear_kernel(
    plane,
    cores,
    normed_mlp_in,
    gate_in,
    up_in,
    down_in,
    grad_in,
    residual_in,
    projection_in,
    out_in,
    normed_in,
    lin_in,
    queries_in,
    both_in,
    attended_in,
    hidden,
    stats,
    gains,
    cosine,
    sine_turned,
    query_pos,
    key_blocks,
    query_gain,
    key_gain,
    output,
    input_grad,
    query_grad,
    key_grad,
    value_grad,
    out_grad,
    gate_grad,
    up_grad,
    down_grad,
    small_sums,
    from_sibling,
    halves,
    from_plane,
    final,
    both_landed,
    normed,
    turned_left,
    turned_right,
    gate,
    up,
    down,
    part_in,
    landed_in,
    landed_out,
    residual,
    grad_residual,
    low_rows,
    sums,
    ring,
    addend,
    stage,
    gain_rows,
    messages,
    z_messages,
    plane_messages,
    core_messages,
    ring_sems,
    stage_sems,
    both_sems,
    send_sems,
    recv_sems,
    local_sems,
):
    links = Links(send_sems, recv_sems, local_sems)
    tokens, width = normed.shape
    token_rows = tokens // parts
    place = Place(plane, cores, token_rows)
    returns = Returns(
        links, place, ring, addend, ring_sems, (from_sibling, halves, from_plane, sums, final)
    )
    returns.out_pending = [[] for _ in range(stage.shape[0])]
    units = gate.shape[3]
    block = width // parts
    shard = gate.shape[2]
    head = query_gain.shape[1]
    query_heads = queries_in.shape[0]
    query_width = query_heads * head
    key_width = both_in.shape[2] // 2
    key_heads = key_width // head
    group = query_heads // key_heads
    lin_width = query_width + 2 * key_width
    own_rows = place.z_rows[0]
    part_out = normed
    split = (plane, cores, shard, tokens)

    low_copies, out_copies, landed_copies = [], [], []

    def feed_forward(grad_rows, act, d_gate, d_up):
        loads = [
            links.local(normed_mlp_in, normed),
            links.local(gate_in, gate),
            links.local(up_in, up),
            links.local(grad_in, grad_rows),
            links.local(down_in, down),
            links.local(residual_in, residual),
        ]
        for copy in loads:
            copy.wait()
        tile = 256

        def hidden_tile(index, carry):
            columns = pl.ds(pl.multiple_of(index * tile, tile), tile)
            gate_lin = multiply(normed[...], gate[:, :, :, columns].reshape(width, tile))
            up_lin = multiply(normed[...], up[:, :, :, columns].reshape(width, tile))
            grad_act = multiply(
                grad_rows[...].reshape(tokens, width), down[:, :, :, columns].reshape(width, tile)
            )
            sigmoid = jax.nn.sigmoid(gate_lin)
            silu = gate_lin * sigmoid
            act[:, columns] = (silu * up_lin).astype(bf16)
            d_up[:, columns] = (grad_act * silu).astype(bf16)
            d_gate[:, columns] = (
                grad_act * up_lin * (sigmoid + silu * (1.0 - sigmoid))
            ).astype(bf16)
            return carry

        lax.fori_loop(0, units // tile, hidden_tile, 0)
        in_copies = []
        for index in range(parts):
            columns = pl.ds(index * block, block)
            part_in[:, columns] = (
                multiply_trans(d_gate[...], gate[index].reshape(block, units))
                + multiply_trans(d_up[...], up[index].reshape(block, units))
            ).astype(bf16)
            in_copies += scatter_sends(
                links, place, part_in, landed_in, token_rows, columns, False
            )
        landed_in[place.z] = part_in[own_rows]
        for index in range(parts):
            columns = slice(index * block, (index + 1) * block)
            turned_left[index] = normed[:, columns].T.reshape(split)
            turned_right[index] = grad_rows[:, :, columns].reshape(tokens, block).T.reshape(split)
        returns.give(0, turned_left, d_gate)
        returns.give(1, turned_left, d_up)
        returns.take(0, turned_left, d_gate)
        returns.take(1, turned_left, d_up)
        for index in range(parts):
            columns = pl.ds(index * block, block)
            part_out[:, columns] = multiply_trans(
                act[...], down[index].reshape(block, units)
            ).astype(bf16)
        landed_out[place.z] = part_out[own_rows]

        for copy in in_copies:
            copy.wait_recv()
        grad_normed = total_of(landed_in)
        values = residual[...]
        scale = lax.rsqrt(jnp.mean(values * values, axis=-1, keepdims=True) + epsilon)
        unit = values * scale
        gain_rows[1:2] = jnp.sum(grad_normed * unit, axis=0, keepdims=True)
        own_grad = grad_rows[place.z].astype(f32)
        total = own_grad + norm_back(grad_normed * gains[1:2], unit, scale)
        grad_residual[...] = total
        low_rows[place.z] = total.astype(bf16)
        own_low = at(low_rows)[place.z]
        low_copies.extend(
            links.send(own_low, own_low, z=place.along_z(step)) for step in z_steps
        )
        out_copies.extend(
            scatter_sends(links, place, part_out, landed_out, token_rows, pl.ds(0, width))
        )
        returns.give(2, turned_right, act)
        returns.take(2, turned_right, act)
        for copy in in_copies:
            copy.wait_send()

    pl.run_scoped(
        feed_forward,
        pltpu.VMEM((parts, token_rows, width), bf16),
        pltpu.VMEM((tokens, units), bf16),
        pltpu.VMEM((tokens, units), bf16),
        pltpu.VMEM((tokens, units), bf16),
    )

    def attention(lin, queries, both, attended, grad_heads, delta, both_stage, both_total, query_total, grad_lin):
        out_at = pl.ds(pl.multiple_of(place.z * query_width, 128), query_width)
        out_columns = at(up)[:, :, :, pl.ds(0, query_width)]
        projection = at(gate)[:, :, :, pl.ds(0, lin_width)]
        loads = [
            links.local(at(out_in)[:, :, :, out_at], out_columns),
            links.local(attended_in, attended),
            links.local(queries_in, queries),
            links.local(both_in, both),
            links.local(lin_in, lin),
            links.local(at(projection_in)[:, :, :, pl.ds(0, lin_width)], projection),
            links.local(normed_in, part_in),
        ]
        for copy in loads:
            copy.wait()
        for index in range(parts):
            columns = slice(index * block, (index + 1) * block)
            turned_left[index] = part_in[:, columns].T.reshape(split)
        for copy in low_copies:
            copy.wait_recv()

        tile = group * head
        for index in range(key_heads):
            columns = slice(index * tile, (index + 1) * tile)
            grads = multiply(
                low_rows[...].reshape(tokens, width), up[:, :, :, columns].reshape(width, tile)
            ).astype(bf16)
            for member in range(group):
                number = index * group + member
                own = grads[:, member * head : (member + 1) * head]
                grad_heads[number] = own
                mixed = attended[:, number * head : (number + 1) * head].astype(f32)
                delta[number : number + 1] = jnp.sum(
                    (own.astype(f32) * mixed).T, axis=0, keepdims=True
                )

        factor = head ** (-0.5)
        score_factor = factor * 1.4426950408889634
        chunk = min(256, tokens)
        chunks_each = tokens // chunk
        lanes = group * tokens
        piece_rows = token_rows // 2
        both_copies, both_own = [], []
        for key_head in range(key_heads):
            members = slice(key_head * group, (key_head + 1) * group)
            query_block = queries[members].reshape(lanes, head)
            grad_block = grad_heads[members].reshape(lanes, head)
            numbers = range(key_head * group, (key_head + 1) * group)
            stats_row = jnp.concatenate([stats[number : number + 1] for number in numbers], axis=1)
            delta_row = jnp.concatenate([delta[number : number + 1] for number in numbers], axis=1)
            positions = jnp.concatenate([query_pos[...]] * group, axis=1)
            query_total[...] = jnp.zeros_like(query_total)

            def back_chunk(index, carry):
                source, row = index // chunks_each, index % chunks_each
                rows = pl.ds(pl.multiple_of(row * chunk, chunk), chunk)
                keys = both[source, rows, pl.ds(key_head * head, head)]
                values = both[source, rows, pl.ds(key_width + key_head * head, head)]
                scores = multiply_trans(keys, query_block) * score_factor
                spots = lax.broadcasted_iota(jnp.int32, (chunk, 1), 0)
                starts = jnp.zeros((chunk, 1), jnp.int32)
                for piece in range(chunk // piece_rows):
                    start = key_blocks[index * (chunk // piece_rows) + piece] * piece_rows
                    starts = jnp.where(spots >= piece * piece_rows, start - piece * piece_rows, starts)
                weights = jnp.where(
                    spots + starts <= positions, jnp.exp2(scores - stats_row), 0.0
                )
                grad_weights = multiply_trans(values, grad_block)
                grad_scores = (weights * (grad_weights - delta_row)).astype(bf16)
                query_total[...] += outer_rows(keys, grad_scores)
                both[source, rows, pl.ds(key_head * head, head)] = (
                    multiply(grad_scores, query_block) * factor
                ).astype(bf16)
                both[source, rows, pl.ds(key_width + key_head * head, head)] = multiply(
                    weights.astype(bf16), grad_block
                ).astype(bf16)
                return carry

            lax.fori_loop(0, plane * chunks_each, back_chunk, 0)
            for start in (key_head * head, key_width + key_head * head):
                columns = pl.ds(start, head)
                for step in range(1, plane):
                    other = place.in_plane(step)
                    both_copies.append(
                        links.send(
                            at(both)[other, :, columns],
                            at(both_landed)[place.p, :, columns],
                            tracked=False,
                            p=other,
                        )
                    )
                both_own.append(
                    links.local(
                        at(both)[place.p, :, columns], at(both_landed)[place.p, :, columns]
                    )
                )
            grad_queries = query_total[...].T * factor
            for member in range(group):
                number = key_head * group + member
                rows = slice(member * tokens, (member + 1) * tokens)
                own = grad_queries[rows]
                lin_rows = lin[:, number * head : (number + 1) * head]
                scale = lax.rsqrt(jnp.mean(lin_rows * lin_rows, axis=-1, keepdims=True) + epsilon)
                unit = lin_rows * scale
                turned = own * cosine[...] - half_turn(own) * sine_turned[...]
                gained = jnp.sum(turned * unit, axis=0, keepdims=True)
                if number == 0:
                    messages[0, 0:1, block : block + head] = gained
                else:
                    messages[0, 0:1, block : block + head] += gained
                grad_lin[:, number * head : (number + 1) * head] = norm_back(
                    turned * query_gain[...], unit, scale
                ).astype(bf16)

        for index in range(parts):
            columns = slice(index * block, (index + 1) * block)
            turned_right[index] = low_rows[:, :, columns].reshape(tokens, block).T.reshape(split)
        returns.give(3, turned_right, attended, lin_width)
        returns.take(3, turned_right, attended, lin_width)
        returns.along_z(0)

        for copy in both_copies:
            copy.wait_recv()
        for copy in both_own:
            copy.wait()

        def load_both(source):
            return Copy(
                at(both_landed)[source], at(both_stage)[source % 2], [(both_sems, source)]
            )

        load = load_both(0)
        for source in range(plane):
            load.wait()
            if source + 1 < plane:
                load = load_both(source + 1)
            landed = both_stage[source % 2].astype(f32)
            if source == 0:
                both_total[...] = landed
            else:
                both_total[...] += landed
        for key_head in range(key_heads):
            start = query_width + key_width + key_head * head
            grad_lin[:, start : start + head] = both_total[
                :, key_width + key_head * head : key_width + (key_head + 1) * head
            ].astype(bf16)
            own = both_total[:, key_head * head : (key_head + 1) * head]
            start = query_width + key_head * head
            lin_rows = lin[:, start : start + head]
            scale = lax.rsqrt(jnp.mean(lin_rows * lin_rows, axis=-1, keepdims=True) + epsilon)
            unit = lin_rows * scale
            turned = own * cosine[...] - half_turn(own) * sine_turned[...]
            gained = jnp.sum(turned * unit, axis=0, keepdims=True)
            if key_head == 0:
                messages[0, 1:2, block : block + head] = gained
            else:
                messages[0, 1:2, block : block + head] += gained
            grad_lin[:, start : start + head] = norm_back(turned * key_gain[...], unit, scale).astype(
                bf16
            )

        for index in range(parts):
            columns = pl.ds(index * block, block)
            part_in[:, columns] = multiply_trans(
                grad_lin[...], gate[index, :, :, 0:lin_width].reshape(block, lin_width)
            ).astype(bf16)
            landed_copies.extend(
                scatter_sends(links, place, part_in, landed_in, token_rows, columns)
            )
        landed_in[place.z] = part_in[own_rows]
        returns.give(3, turned_left, grad_lin)
        returns.take(3, turned_left, grad_lin)
        returns.along_z(1)
        returns.along_z(2)
        for copy in both_copies:
            copy.wait_send()

    pl.run_scoped(
        attention,
        pltpu.VMEM((tokens, query_width + key_width), f32),
        pltpu.VMEM((query_heads, tokens, head), bf16),
        pltpu.VMEM((plane, tokens, 2 * key_width), bf16),
        pltpu.VMEM((tokens, query_width), bf16),
        pltpu.VMEM((query_heads, tokens, head), bf16),
        pltpu.VMEM((8, tokens), f32),
        pltpu.VMEM((2, tokens, 2 * key_width), bf16),
        pltpu.VMEM((tokens, 2 * key_width), f32),
        pltpu.VMEM((head, group * tokens), f32),
        pltpu.VMEM((tokens, lin_width), bf16),
    )
    returns.along_z(3)

    for copy in landed_copies:
        copy.wait_recv()
    grad_normed = total_of(landed_in)
    values = hidden[...].astype(f32)
    scale = lax.rsqrt(jnp.mean(values * values, axis=-1, keepdims=True) + epsilon)
    unit = values * scale
    gain_rows[0:1] = jnp.sum(grad_normed * unit, axis=0, keepdims=True)
    input_grad[...] = (
        grad_residual[...] + norm_back(grad_normed * gains[0:1], unit, scale)
    ).astype(bf16)

    for index in range(1, parts):
        messages[index, :, block : block + head] = messages[0, :, block : block + head]
    for index in range(parts):
        messages[index, 0:2, 0:block] = gain_rows[:, index * block : (index + 1) * block]
    copies = [
        links.send(at(messages)[place.along_z(step)], at(z_messages)[place.z], z=place.along_z(step))
        for step in z_steps
    ]
    z_messages[place.z] = messages[place.z]
    for copy in out_copies:
        copy.wait_recv()
    output[...] = (residual[...] + total_of(landed_out)).astype(bf16)
    for copy in copies:
        copy.wait_recv()
    plane_messages[place.p] = (z_messages[0] + z_messages[1]) + (z_messages[2] + z_messages[3])
    copies = [
        links.send(
            at(plane_messages)[place.p], at(plane_messages)[place.p], p=place.in_plane(step)
        )
        for step in range(1, plane)
    ]
    returns.home(0, stage, stage_sems, [(gate_grad, 0, units)])
    for copy in copies:
        copy.wait_recv()
    total = plane_messages[0]
    for source in range(1, plane):
        total += plane_messages[source]
    core_messages[place.c] = total
    copies = [
        links.send(at(core_messages)[place.c], at(core_messages)[place.c], c=other)
        for other in place.siblings()
    ]
    returns.home(1, stage, stage_sems, [(up_grad, 0, units)])
    for copy in copies:
        copy.wait_recv()
    total = core_messages[0]
    for source in range(1, cores):
        total += core_messages[source]
    small_sums[...] = total
    returns.home(2, stage, stage_sems, [(down_grad, 0, units)])
    returns.home(
        3,
        stage,
        stage_sems,
        [
            (query_grad, 0, query_width),
            (key_grad, query_width, key_width),
            (value_grad, query_width + key_width, key_width),
            (out_grad, lin_width, query_width),
        ],
    )
    returns.finish()
    links.finish()


def rear(plane, cores, large, small):
    normed_mlp, gate = large[0], large[1]
    projection, lin, queries, both = large[6], large[9], large[10], large[11]
    tokens, width = normed_mlp.shape
    token_rows = tokens // parts
    _, columns, shard, units = gate.shape
    query_heads, _, head = queries.shape
    query_width = query_heads * head
    key_width = both.shape[2] // 2
    key_heads = key_width // head
    lin_width = query_width + 2 * key_width
    block = width // parts
    any_space, vmem = pl.BlockSpec(memory_space=pl.ANY), pl.BlockSpec(memory_space=pltpu.VMEM)
    copies = 16 + 12 + 6 + 12 + 20 + 10 * plane + 12 + 8
    wide = lin_width + query_width
    assert wide == units
    shapes = [
        ((token_rows, width), bf16),
        ((token_rows, width), bf16),
        ((shard, parts * query_width), f32),
        ((shard, parts * key_width), f32),
        ((shard, parts * key_width), f32),
        ((shard, parts * query_width), f32),
        ((shard, parts * units), f32),
        ((shard, parts * units), f32),
        ((shard, parts * units), f32),
        ((8, block + head), f32),
        ((4, parts, plane, shard, units), bf16),
        ((4, parts, plane, shard, units), bf16),
        ((4, plane, parts, shard, units), bf16),
        ((4, parts, shard, units), bf16),
        ((plane, tokens, 2 * key_width), bf16),
    ]
    turned = (parts, plane, cores, shard, tokens)
    message = (8, block + head)
    return pl.pallas_call(
        functools.partial(rear_kernel, plane, cores),
        out_shape=[jax.ShapeDtypeStruct(shape, kind) for shape, kind in shapes],
        in_specs=[any_space] * 13
        + [vmem] * 6
        + [pl.BlockSpec(memory_space=pltpu.SMEM)]
        + [vmem] * 2,
        out_specs=[vmem] * 2 + [any_space] * 7 + [vmem] + [any_space] * 5,
        scratch_shapes=[
            pltpu.VMEM((tokens, width), bf16),
            pltpu.VMEM(turned, bf16),
            pltpu.VMEM(turned, bf16),
            pltpu.VMEM(gate.shape, bf16),
            pltpu.VMEM(gate.shape, bf16),
            pltpu.VMEM(gate.shape, bf16),
            pltpu.VMEM((tokens, width), bf16),
            pltpu.VMEM((parts, token_rows, width), bf16),
            pltpu.VMEM((parts, token_rows, width), bf16),
            pltpu.VMEM((token_rows, width), f32),
            pltpu.VMEM((token_rows, width), f32),
            pltpu.VMEM((parts, token_rows, width), bf16),
            pltpu.VMEM((4, parts, shard, units), bf16),
            pltpu.VMEM((4, plane, shard, units), bf16),
            pltpu.VMEM((1, plane, shard, units), bf16),
            pltpu.VMEM((2, shard, units), f32),
            pltpu.VMEM((2, width), f32),
            pltpu.VMEM((parts,) + message, f32),
            pltpu.VMEM((parts,) + message, f32),
            pltpu.VMEM((plane,) + message, f32),
            pltpu.VMEM((cores,) + message, f32),
            pltpu.SemaphoreType.DMA((128,)),
            pltpu.SemaphoreType.DMA((32,)),
            pltpu.SemaphoreType.DMA((plane,)),
            pltpu.SemaphoreType.DMA((copies,)),
            pltpu.SemaphoreType.DMA((copies,)),
            pltpu.SemaphoreType.DMA((24,)),
        ],
        compiler_params=pltpu.CompilerParams(
            has_side_effects=True, vmem_limit_bytes=63 * 1024 * 1024
        ),
        cost_estimate=pl.CostEstimate(flops=4 * 10**10, bytes_accessed=10**8, transcendentals=10**7),
    )(*large, *small)


def make_local(plane, cores):
    def local(
        hidden_in,
        block_map,
        query_weight,
        key_weight,
        value_weight,
        out_weight,
        gate_weight,
        up_weight,
        down_weight,
        attention_norm_gain,
        feedforward_gain,
        query_gain,
        key_gain,
        output_grad,
    ):
        shard = query_weight.shape[0]
        hidden_own, grad_own = hidden_in[0], output_grad[0]
        row_count, features = hidden_own.shape
        piece_rows = row_count // 2
        head_width = query_gain.shape[0]
        p_index = lax.axis_index("p")
        tokens = parts * row_count

        blocks = block_map[0].reshape(parts, plane, 2)
        offsets = jnp.arange(piece_rows, dtype=jnp.int32)
        all_pos = blocks.transpose(1, 0, 2)[..., None] * piece_rows + offsets
        all_pos = all_pos.reshape(plane, tokens)
        query_pos = lax.dynamic_index_in_dim(all_pos, p_index, 0, keepdims=False)
        key_pos = all_pos.reshape(-1)
        cosine, sine_table = rope_tables(query_pos, head_width)
        sign = jnp.where(jnp.arange(head_width) < head_width // 2, -1.0, 1.0).astype(f32)
        query_gain_float = query_gain.astype(f32)
        key_gain_float = key_gain.astype(f32)
        gain_block = jnp.stack([attention_norm_gain, feedforward_gain], axis=1)
        gain_block = jnp.pad(gain_block, ((0, 0), (0, 126)))

        (
            normed,
            projection,
            lin,
            queries,
            both,
            attended_low,
            out_full,
            normed_mlp,
            own_residual,
            gate_columns,
            up_columns,
            down_columns,
            grad_rows,
            stats,
            gains,
        ) = front(
            plane,
            cores,
            hidden_own,
            (
                query_weight,
                key_weight,
                value_weight,
                out_weight,
                gate_weight,
                up_weight,
                down_weight,
            ),
            gain_block,
            grad_own,
            (cosine[:, 0], sine_table[:, 0] * sign),
            (query_pos[None], key_pos[:, None]),
            (query_gain_float[None], key_gain_float[None]),
        )
        results = rear(
            plane,
            cores,
            (
                normed_mlp,
                gate_columns,
                up_columns,
                down_columns,
                grad_rows,
                own_residual,
                projection,
                out_full,
                normed,
                lin,
                queries,
                both,
                attended_low,
            ),
            (
                hidden_own,
                stats,
                gains,
                cosine[:, 0],
                sine_table[:, 0] * sign,
                query_pos[None],
                blocks.transpose(1, 0, 2).reshape(-1),
                query_gain_float[None],
                key_gain_float[None],
            ),
        )
        output, input_grad = results[:2]
        small_sums = results[9]
        block = features // parts
        own_column = p_index * cores + lax.axis_index("c")
        own_gains = lax.dynamic_slice_in_dim(small_sums[:2, :block], own_column * shard, shard, 1)
        head_sums = small_sums[:2, block:]
        return (
            (output[None], input_grad[None])
            + tuple(results[2:9])
            + (own_gains[0], own_gains[1], head_sums[0], head_sums[1])
        )

    return local


def solution(mesh):
    ctx_count, core_count = mesh.shape["ctx"], mesh.shape["fsdp"]
    plane = ctx_count // parts
    fine_mesh = Mesh(mesh.devices.reshape(parts, plane, core_count), ("z", "p", "c"))
    token_spec = P("c", ("z", "p"), None)
    weight_spec = P(("z", "p", "c"), None)
    gain_spec = P(("z", "p", "c"))
    return jax.shard_map(
        make_local(plane, core_count),
        mesh=fine_mesh,
        in_specs=(
            (token_spec, P("c", None)) + (weight_spec,) * 7 + (gain_spec,) * 2 + (P(), P(), token_spec)
        ),
        out_specs=(token_spec,) * 2 + (weight_spec,) * 7 + (gain_spec,) * 2 + (P(), P()),
        check_vma=False,
    )
```

```python
import functools

import jax
import jax.numpy as jnp
from jax import lax
from jax.experimental import pallas as pl
from jax.experimental.pallas import tpu as pltpu
from jax.sharding import Mesh, PartitionSpec as P

epsilon = 1e-06
rotary_base = 1000000.0
masked_score = -1e30
parts = 4
bf16 = jnp.bfloat16
f32 = jnp.float32


def norm_back(weighted, unit, scale_row):
    inner_mean = jnp.mean(weighted * unit, axis=-1, keepdims=True)
    return scale_row * (weighted - unit * inner_mean)


def rope_tables(positions, width):
    half_width = width // 2
    frequency = rotary_base ** (-(jnp.arange(half_width, dtype=f32) * 2.0 / width))
    angles = positions.astype(f32)[:, None] * frequency[None, :]
    angles = jnp.concatenate([angles, angles], axis=-1)
    return jnp.cos(angles)[:, None, :], jnp.sin(angles)[:, None, :]


def multiply(left, right):
    return jnp.dot(left, right, preferred_element_type=f32)


def multiply_trans(left, right):
    return lax.dot_general(left, right, (((1,), (1,)), ((), ())), preferred_element_type=f32)


def outer_rows(left, right):
    return lax.dot_general(left, right, (((0,), (0,)), ((), ())), preferred_element_type=f32)


class Part:
    def __init__(self, ref, index=None):
        self.ref, self.index = ref, index

    def __getitem__(self, index):
        return Part(self.ref, index)

    def get(self):
        return self.ref if self.index is None else self.ref.at[self.index]


def at(ref):
    return Part(ref)


def found(ref):
    return ref.get() if isinstance(ref, Part) else ref


class Copy:
    def __init__(self, source, target, sems, device=None, when=None):
        self.source, self.target, self.sems = source, target, sems
        self.device, self.when = device, when
        self.guarded(lambda: self.describe().start())

    def guarded(self, action):
        if self.when is None:
            action()
        else:
            pl.when(self.when)(action)

    def describe(self):
        source, target = found(self.source), found(self.target)
        sems = [array.at[index] for array, index in self.sems]
        if self.device is None:
            return pltpu.make_async_copy(source, target, sems[0])
        return pltpu.make_async_remote_copy(
            src_ref=source,
            dst_ref=target,
            send_sem=sems[0],
            recv_sem=sems[1],
            device_id=self.device,
            device_id_type=pl.DeviceIdType.MESH,
        )

    def wait(self):
        self.describe().wait()

    def wait_send(self):
        self.guarded(lambda: self.describe().wait_send())

    def wait_recv(self):
        self.describe().wait_recv()


class Links:
    def __init__(self, send_sems, recv_sems, local_sems):
        self.send_sems, self.recv_sems, self.local_sems = send_sems, recv_sems, local_sems
        self.count, self.local_count = 0, 0
        self.sent, self.kept = [], []

    def send(self, source, target, tracked=True, when=None, lands=None, **device):
        index = self.count
        self.count += 1
        received = index if lands is None else lands.sems[1][1]
        copy = Copy(
            source, target, [(self.send_sems, index), (self.recv_sems, received)], device, when
        )
        if tracked:
            self.sent.append(copy)
        return copy

    def local(self, source, target):
        index = self.local_count
        self.local_count += 1
        return Copy(source, target, [(self.local_sems, index)])

    def keep(self, source, target):
        self.kept.append(self.local(source, target))

    def finish(self):
        assert self.count <= self.send_sems.shape[0]
        assert self.local_count <= self.local_sems.shape[0]
        for copy in self.sent:
            copy.wait_send()
        for copy in self.kept:
            copy.wait()


class LineGather:
    def __init__(self, links, place, source, block):
        self.links, self.place, self.block = links, place, block
        target = block(place.z)
        self.far = links.send(source, target, z=place.along_z(2))
        self.above = links.send(source, target, when=place.not_last, z=place.along_z(1))
        self.below = links.send(source, target, when=place.not_first, z=place.along_z(3))

    def relay(self):
        links, place = self.links, self.place
        self.far.wait_recv()
        block = self.block(place.along_z(2))
        self.relays = (
            links.send(block, block, False, place.second, self.above, z=place.along_z(3)),
            links.send(block, block, False, place.third, self.below, z=place.along_z(1)),
        )

    def wait(self):
        self.above.wait_recv()
        self.below.wait_recv()

    def relayed(self):
        for copy in self.relays:
            copy.wait_send()


class LineSum:
    def __init__(self, links, place, part, landed, extra):
        self.links, self.place = links, place
        self.part, self.landed, self.extra = part, landed, extra
        self.near, self.extras, self.far, self.columns = [], [], [], []

    def start(self, columns, tracked=True):
        links, place = self.links, self.place
        target = at(self.landed)[place.z, :, columns]
        rows = place.z_rows
        above, below = at(self.part)[rows[1], columns], at(self.part)[rows[3], columns]
        beyond = at(self.part)[rows[2], columns]
        self.columns.append(columns)
        self.far.append(links.send(beyond, target, tracked, place.at_end, z=place.along_z(2)))
        self.near.append(
            (
                links.send(above, target, tracked, place.not_last, z=place.along_z(1)),
                links.send(below, target, tracked, place.not_first, z=place.along_z(3)),
            )
        )
        extra = at(self.extra)[:, columns]
        self.extras.append(
            (
                links.send(below, extra, tracked, place.first, z=place.along_z(1)),
                links.send(above, extra, tracked, place.last, z=place.along_z(3)),
            )
        )

    def combine(self, tracked=True):
        links, place = self.links, self.place

        @pl.when(place.at_end)
        def nothing_comes():
            self.landed[place.opposite] = jnp.zeros(self.landed.shape[1:], bf16)

        for columns, extras, far in zip(self.columns, self.extras, self.far):
            rows = place.z_rows[2]

            @pl.when(place.second)
            def arrived():
                extras[0].wait_recv()

            @pl.when(place.third)
            def arrived_too():
                extras[1].wait_recv()

            @pl.when(place.inside)
            def add():
                total = self.part[rows, columns].astype(f32) + self.extra[:, columns].astype(f32)
                self.part[rows, columns] = total.astype(bf16)

            self.near.append(
                (
                    links.send(
                        at(self.part)[rows, columns],
                        at(self.landed)[place.z, :, columns],
                        tracked,
                        place.inside,
                        lands=far,
                        z=place.along_z(2),
                    ),
                )
            )

    def wait(self):
        place = self.place
        for index, far in enumerate(self.far):
            above, below = self.near[index]

            @pl.when(place.not_first)
            def from_below():
                above.wait_recv()

            @pl.when(place.not_last)
            def from_above():
                below.wait_recv()

            far.wait_recv()

    def sent(self):
        return self.far + [copy for copies in self.near + self.extras for copy in copies]


class Place:
    def __init__(self, plane, cores, token_rows):
        self.plane, self.cores = plane, cores
        self.z, self.p, self.c = (lax.axis_index(axis) for axis in ("z", "p", "c"))
        self.column = self.p * cores + self.c
        self.other_core = lax.rem(self.c + 1, cores)
        self.z_others = [lax.rem(self.z + step, parts) for step in range(parts)]
        self.p_others = [lax.rem(self.p + step, plane) for step in range(plane)]
        self.columns_before = [
            lax.rem(self.p + plane - step, plane) * cores + self.c for step in range(plane)
        ]
        self.first, self.last = self.z == 0, self.z == parts - 1
        self.second, self.third = self.z == 1, self.z == parts - 2
        self.not_first, self.not_last = self.z != 0, self.z != parts - 1
        self.at_end = jnp.logical_or(self.first, self.last)
        self.inside = jnp.logical_not(self.at_end)
        self.opposite = parts - 1 - self.z
        self.relayed = plane == 4
        if self.relayed:
            self.flips = [self.p + 1 - 2 * lax.rem(self.p, 2), lax.rem(self.p + 2, 4)]
            flipped = lax.rem(self.flips[0] + 2, 4)
            self.flip_columns = [flip * cores + self.c for flip in self.flips + [flipped]]
        self.z_rows = [
            pl.ds(pl.multiple_of(other * token_rows, token_rows), token_rows)
            for other in self.z_others
        ]

    def along_z(self, step):
        return self.z_others[step]

    def in_plane(self, step):
        return self.p_others[step]

    def before(self, step):
        return self.columns_before[step]

    def siblings(self):
        return [self.other_core]


z_steps = (1, 3, 2)


class Fetch:
    def __init__(self, links, place, pieces, gathered, line_only=False):
        self.links, self.place, self.pieces, self.gathered = links, place, pieces, gathered
        self.line_only = line_only
        self.first, self.own = [], []

    def mine(self, columns):
        if self.line_only:
            return at(self.gathered)[self.place.z, :, columns]
        return at(self.gathered)[self.place.z, self.place.column, :, columns]

    def begin(self):
        links, place = self.links, self.place
        mine = self.mine
        for shard, width, start, split in self.pieces:
            for step in z_steps:
                other = place.along_z(step)
                first = pl.multiple_of(other * width, 128) if split else 0
                self.first.append(
                    links.send(at(shard)[:, pl.ds(first, width)], mine(pl.ds(start, width)), z=other)
                )
            first = pl.multiple_of(place.z * width, 128) if split else 0
            self.own.append(
                links.local(at(shard)[:, pl.ds(first, width)], mine(pl.ds(start, width)))
            )

    def arrive(self):
        for copy in self.own:
            copy.wait()
        for copy in self.first:
            copy.wait_recv()

    def spread(self):
        links, place = self.links, self.place
        self.arrive()
        block = at(self.gathered)[:, place.column]
        if place.relayed:
            self.second = [links.send(block, block, p=other) for other in place.flips]
        else:
            self.second = [
                links.send(block, block, p=place.in_plane(step)) for step in range(1, place.plane)
            ]
        self.third = [links.send(block, block, c=other) for other in place.siblings()]
        self.halves = []

    def pass_on(self, column):
        block = at(self.gathered)[:, column]
        self.third += [self.links.send(block, block, c=other) for other in self.place.siblings()]

    def forward(self):
        links, place = self.links, self.place
        if place.relayed:
            for side, copy in enumerate(self.second):
                copy.wait_recv()
                column = place.flip_columns[side]
                half = at(self.gathered)[pl.ds(side * (parts // 2), parts // 2), column]
                self.halves.append(links.send(half, half, p=place.flips[1 - side]))
                self.pass_on(column)
        else:
            for step, copy in enumerate(self.second, 1):
                copy.wait_recv()
                self.pass_on(place.before(step))

    def close(self):
        if self.place.relayed:
            for copy in self.halves:
                copy.wait_recv()
            self.pass_on(self.place.flip_columns[2])

    def finish(self):
        for copy in self.third:
            copy.wait_recv()


def front_kernel(
    plane,
    cores,
    hidden,
    query_weight,
    key_weight,
    value_weight,
    out_weight,
    gate_weight,
    up_weight,
    down_weight,
    gain_block,
    cosine,
    sine_turned,
    query_pos,
    key_pos,
    query_gain,
    key_gain,
    normed_out,
    projection_out,
    lin_out,
    queries_out,
    both_out,
    attended_out,
    out_columns_out,
    normed_mlp_out,
    residual_out,
    gate_out,
    up_out,
    down_out,
    stats_out,
    gains_out,
    hidden_all,
    normed,
    projection,
    lin,
    queries,
    both,
    attended_all,
    out_full,
    residual,
    normed_mlp,
    mixed,
    send_sems,
    recv_sems,
    local_sems,
):
    links = Links(send_sems, recv_sems, local_sems)
    token_rows, width = hidden.shape
    place = Place(plane, cores, token_rows)
    tokens = parts * token_rows
    head = query_gain.shape[1]
    query_width = query_weight.shape[1] // parts
    key_width = key_weight.shape[1] // parts
    query_heads, key_heads = query_width // head, key_width // head
    group = query_heads // key_heads
    hidden_units = gate_weight.shape[1] // parts
    lin_width = query_width + 2 * key_width

    heads_fetch = Fetch(
        links,
        place,
        [
            (query_weight, query_width, 0, True),
            (key_weight, key_width, query_width, True),
            (value_weight, key_width, query_width + key_width, True),
            (gain_block, 128, lin_width, False),
        ],
        projection,
    )
    out_fetch = Fetch(links, place, [(out_weight, out_weight.shape[1], 0, False)], out_full)
    mlp_fetches = [
        Fetch(links, place, [(weight, hidden_units, 0, True)], target)
        for weight, target in ((gate_weight, gate_out), (up_weight, up_out))
    ]
    down_fetch = Fetch(links, place, [(down_weight, hidden_units, 0, True)], down_out, True)
    heads_fetch.begin()
    out_fetch.begin()
    heads_fetch.spread()
    hidden_own = links.local(hidden, hidden_all.at[place.z])
    hidden_gather = LineGather(links, place, hidden, lambda z: at(hidden_all)[z])
    out_fetch.spread()
    heads_fetch.forward()
    hidden_gather.relay()
    heads_fetch.close()
    heads_fetch.finish()
    links.keep(projection, projection_out)
    hidden_own.wait()
    hidden_gather.wait()
    for fetch in mlp_fetches + [down_fetch]:
        fetch.begin()

    gain_columns = projection[:, :, :, lin_width : lin_width + 128].reshape(width, 128)
    gain_rows = gain_columns.astype(f32).T
    gains_out[...] = gain_rows[:8]

    def norm_one(index, carry):
        values = hidden_all[index].astype(f32)
        scale = lax.rsqrt(jnp.mean(values * values, axis=-1, keepdims=True) + epsilon)
        rows = pl.ds(pl.multiple_of(index * token_rows, token_rows), token_rows)
        normed[rows] = (values * scale * gains_out[0:1]).astype(bf16)
        return carry

    lax.fori_loop(0, parts, norm_one, 0)
    links.keep(normed, normed_out)

    tile = 2 * head

    def project(index, carry):
        columns = pl.ds(pl.multiple_of(index * tile, tile), tile)
        weights = projection[:, :, :, columns].reshape(width, tile)
        lin[:, columns] = jnp.dot(normed[...], weights, preferred_element_type=f32)
        return carry

    lax.fori_loop(0, lin_width // tile, project, 0)
    own_both = both.at[place.p]

    def rope(values, gain):
        scale = lax.rsqrt(jnp.mean(values * values, axis=-1, keepdims=True) + epsilon)
        gained = values * scale * gain
        turned = pltpu.roll(gained, head // 2, 1)
        return (gained * cosine[...] + turned * sine_turned[...]).astype(bf16)

    for index in range(key_heads):
        columns = slice(query_width + index * head, query_width + (index + 1) * head)
        own_both[:, index * head : (index + 1) * head] = rope(lin[:, columns], key_gain[...])
    own_both[:, key_width:] = lin[:, query_width + key_width :].astype(bf16)
    both_copies = [
        links.send(own_both, own_both, p=place.in_plane(step)) for step in range(1, plane)
    ]
    for index in range(query_heads):
        columns = slice(index * head, (index + 1) * head)
        queries[index] = rope(lin[:, columns], query_gain[...])
    links.keep(lin.at[:, pl.ds(0, query_width + key_width)], lin_out)
    links.keep(queries, queries_out)
    out_fetch.forward()
    for copy in both_copies:
        copy.wait_recv()
    links.keep(both, both_out)
    mlp_fetches[0].spread()

    factor = head ** (-0.5) * 1.4426950408889634
    chunk = min(256, tokens)
    chunks_each = tokens // chunk
    lanes = group * tokens
    own_attended = attended_all.at[place.z]
    attended_gathers = []
    for key_head in range(key_heads):
        block = queries[key_head * group : (key_head + 1) * group].reshape(lanes, head)
        positions = jnp.concatenate([query_pos[...]] * group, axis=1)
        mixed[...] = jnp.zeros_like(mixed)

        def attend_chunk(index, carry):
            best, summed = carry
            source, row = index // chunks_each, index % chunks_each
            rows = pl.ds(pl.multiple_of(row * chunk, chunk), chunk)
            keys = both[source, rows, pl.ds(key_head * head, head)]
            values = both[source, rows, pl.ds(key_width + key_head * head, head)]
            scores = multiply_trans(keys, block) * factor
            spot = pl.ds(pl.multiple_of(index * chunk, chunk), chunk)
            scores = jnp.where(key_pos[spot] <= positions, scores, masked_score)
            new_best = jnp.maximum(best, jnp.max(scores, axis=0, keepdims=True))
            weights = jnp.exp2(scores - new_best)
            shrink = jnp.exp2(best - new_best)
            summed = summed * shrink + jnp.sum(weights, axis=0, keepdims=True)
            mixed[...] = mixed[...] * shrink + outer_rows(values, weights.astype(bf16))
            return new_best, summed

        best, summed = lax.fori_loop(
            0,
            plane * chunks_each,
            attend_chunk,
            (jnp.full((1, lanes), masked_score, f32), jnp.zeros((1, lanes), f32)),
        )
        mixed_rows = (mixed[...] / summed).T
        stats = best + jnp.log2(summed)
        for member in range(group):
            index = key_head * group + member
            stats_out[index : index + 1] = stats[:, member * tokens : (member + 1) * tokens]
            own_attended[:, index * head : (index + 1) * head] = mixed_rows[
                member * tokens : (member + 1) * tokens
            ].astype(bf16)
        columns = pl.ds(key_head * group * head, group * head)
        attended_gathers.append(
            LineGather(
                links,
                place,
                at(attended_all)[place.z, :, columns],
                lambda z, columns=columns: at(attended_all)[z, :, columns],
            )
        )
        if key_head == 0:
            out_fetch.close()
    links.keep(own_attended, attended_out)
    mlp_fetches[0].forward()
    mlp_fetches[1].spread()
    for gather in attended_gathers:
        gather.relay()
    mlp_fetches[0].close()
    out_fetch.finish()
    links.keep(out_full, out_columns_out)
    mlp_fetches[1].forward()
    for gather in attended_gathers:
        gather.wait()

    def add_out(index, carry):
        weights = out_full[index].reshape(width // parts, parts * query_width)
        columns = pl.ds(pl.multiple_of(index * (width // parts), 128), width // parts)
        total = hidden_all[:, :, columns].reshape(tokens, width // parts).astype(f32)
        for other in range(parts):
            total += multiply_trans(
                attended_all[other], weights[:, other * query_width : (other + 1) * query_width]
            )
        residual[:, columns] = total
        return carry

    lax.fori_loop(0, parts, add_out, 0)

    def norm_two(index, carry):
        rows = pl.ds(pl.multiple_of(index * token_rows, token_rows), token_rows)
        values = residual[rows]
        scale = lax.rsqrt(jnp.mean(values * values, axis=-1, keepdims=True) + epsilon)
        normed_mlp[rows] = (values * scale * gains_out[1:2]).astype(bf16)
        return carry

    lax.fori_loop(0, parts, norm_two, 0)
    links.keep(normed_mlp, normed_mlp_out)
    own_rows = place.z_rows[0]
    links.keep(residual.at[own_rows], residual_out)
    mlp_fetches[1].close()
    down_fetch.arrive()
    for fetch in mlp_fetches:
        fetch.finish()
    for gather in [hidden_gather] + attended_gathers:
        gather.relayed()
    links.finish()


def front(plane, cores, hidden, weights, gain_block, tables, positions, head_gains):
    token_rows, width = hidden.shape
    tokens = parts * token_rows
    shard = weights[0].shape[0]
    head = head_gains[0].shape[1]
    query_width, key_width = weights[0].shape[1] // parts, weights[1].shape[1] // parts
    hidden_units = weights[4].shape[1] // parts
    lin_width = query_width + 2 * key_width
    query_heads = query_width // head
    group = query_width // key_width
    stacked = (parts, plane * cores, shard)
    copies = 24 + 5 * (2 * plane + 8) + plane + 24
    any_space, vmem = pl.BlockSpec(memory_space=pl.ANY), pl.BlockSpec(memory_space=pltpu.VMEM)
    outputs = [
        ((tokens, width), bf16),
        (stacked + (lin_width + 128,), bf16),
        ((tokens, query_width + key_width), f32),
        ((query_heads, tokens, head), bf16),
        ((plane, tokens, 2 * key_width), bf16),
        ((tokens, query_width), bf16),
        (stacked + (parts * query_width,), bf16),
        ((tokens, width), bf16),
        ((token_rows, width), f32),
        (stacked + (hidden_units,), bf16),
        (stacked + (hidden_units,), bf16),
        ((parts, shard, hidden_units), bf16),
        ((8, tokens), f32),
        ((8, width), f32),
    ]
    return pl.pallas_call(
        functools.partial(front_kernel, plane, cores),
        out_shape=[jax.ShapeDtypeStruct(shape, kind) for shape, kind in outputs],
        in_specs=[any_space] * 9 + [vmem] * 6,
        out_specs=[any_space] * 12 + [vmem] * 2,
        scratch_shapes=[
            pltpu.VMEM((parts, token_rows, width), bf16),
            pltpu.VMEM((tokens, width), bf16),
            pltpu.VMEM(stacked + (lin_width + 128,), bf16),
            pltpu.VMEM((tokens, lin_width), f32),
            pltpu.VMEM((query_heads, tokens, head), bf16),
            pltpu.VMEM((plane, tokens, 2 * key_width), bf16),
            pltpu.VMEM((parts, tokens, query_width), bf16),
            pltpu.VMEM(stacked + (parts * query_width,), bf16),
            pltpu.VMEM((tokens, width), f32),
            pltpu.VMEM((tokens, width), bf16),
            pltpu.VMEM((head, group * tokens), f32),
            pltpu.SemaphoreType.DMA((copies,)),
            pltpu.SemaphoreType.DMA((copies,)),
            pltpu.SemaphoreType.DMA((32,)),
        ],
        compiler_params=pltpu.CompilerParams(
            has_side_effects=True, vmem_limit_bytes=60 * 1024 * 1024
        ),
        cost_estimate=pl.CostEstimate(flops=12 * 10**9, bytes_accessed=10**8, transcendentals=10**7),
    )(hidden, *weights, gain_block, *tables, *positions, *head_gains)


def half_turn(values):
    return pltpu.roll(values, values.shape[1] // 2, 1)


def total_of(landed):
    total = landed[0].astype(f32)
    for index in range(1, parts):
        total += landed[index].astype(f32)
    return total


class Returns:
    def __init__(self, links, place, ring, addend, ring_sems, buffers):
        self.links, self.place, self.ring, self.addend = links, place, ring, addend
        self.ring_sems = ring_sems
        self.from_sibling, self.halves, self.from_plane, self.sums, self.final = buffers
        self.pending = [[] for _ in range(ring.shape[0])]
        self.turn, self.used = 0, 0
        self.sibling_copies, self.plane_copies, self.z_copies = {}, {}, {}
        self.mine, self.own_final = {}, {}

    def slot(self):
        slot = self.turn % len(self.pending)
        self.turn += 1
        for wait in self.pending[slot]:
            wait()
        self.pending[slot] = []
        return slot

    def local(self, source, target):
        self.used += 1
        return Copy(source, target, [(self.ring_sems, self.used - 1)])

    def product(self, slot, left, half, right, start, index, added):
        size = right.shape[1]
        tile = 512 if size % 512 == 0 else 256

        def tile_of(step, carry):
            columns = pl.ds(pl.multiple_of(step * tile, tile), tile)
            target = pl.ds(pl.multiple_of(start + step * tile, 128), tile)
            rows = left[index, :, half]
            value = multiply(rows.reshape(-1, rows.shape[2]), right[:, columns])
            value = value.reshape(rows.shape[0], rows.shape[1], tile)
            if added is not None:
                value += self.addend[added, :, :, target].astype(f32)
            self.ring[slot, :, :, target] = value.astype(bf16)
            return carry

        lax.fori_loop(0, size // tile, tile_of, 0)

    def give(self, family, left, right, start=0):
        place, size = self.place, right.shape[1]
        other = place.other_core
        columns = pl.ds(start, size)
        for index in range(parts):
            slot = self.slot()
            self.product(slot, left, other, right, start, index, None)
            copy = self.links.send(
                at(self.ring)[slot, :, :, columns],
                at(self.from_sibling)[family, index, :, :, columns],
                tracked=False,
                c=other,
            )
            self.pending[slot].append(copy.wait_send)
            self.sibling_copies[family, start, index] = copy

    def take(self, family, left, right, start=0):
        size = right.shape[1]
        columns = pl.ds(start, size)
        loads, kept = [], []
        slots = self.addend.shape[0]

        def load(index):
            self.sibling_copies[family, start, index].wait_recv()
            loads.append(
                self.local(
                    at(self.from_sibling)[family, index, :, :, columns],
                    at(self.addend)[index % slots, :, :, columns],
                )
            )

        for index in range(slots):
            load(index)
        for index in range(parts):
            slot = self.slot()
            loads[index].wait()
            self.product(slot, left, self.place.c, right, start, index, index % slots)
            if index + slots < parts:
                load(index + slots)
            kept.append(
                self.local(
                    at(self.ring)[slot, :, :, columns],
                    at(self.halves)[family, index, :, :, columns],
                )
            )
            self.pending[slot].append(kept[-1].wait)
        for waits in self.pending:
            for wait in waits:
                wait()
            waits.clear()
        self.send_plane(family, columns)

    def send_plane(self, family, columns):
        links, place = self.links, self.place
        sent = self.plane_copies.setdefault(family, [])
        for step in range(1, place.plane):
            other = place.in_plane(step)
            sent.append(
                links.send(
                    at(self.halves)[family, :, other, :, columns],
                    at(self.from_plane)[family, place.p, :, :, columns],
                    p=other,
                )
            )
        self.mine.setdefault(family, []).append(
            self.local(
                at(self.halves)[family, :, place.p, :, columns],
                at(self.from_plane)[family, place.p, :, :, columns],
            )
        )

    def along_z(self, family, columns):
        links, place = self.links, self.place
        for copy in self.plane_copies[family]:
            copy.wait_recv()
        for copy in self.mine[family]:
            copy.wait()
        sources = place.plane
        loads = []
        for index in range(parts):
            slot = self.slot()
            loads.append(
                (
                    slot,
                    self.local(
                        at(self.from_plane)[family, pl.ds(0, sources), index, :, columns],
                        at(self.ring)[slot, pl.ds(0, sources), :, columns],
                    ),
                )
            )
        for index, (slot, load) in enumerate(loads):
            load.wait()
            total = self.ring[slot, 0, :, columns].astype(f32)
            for source in range(1, sources):
                total += self.ring[slot, source, :, columns].astype(f32)
            self.sums[family, index, :, columns] = total.astype(bf16)
        copies = []
        for step in z_steps:
            other = place.along_z(step)
            copies.append(
                links.send(
                    at(self.sums)[family, other, :, columns],
                    at(self.final)[family, place.z, :, columns],
                    z=other,
                )
            )
        self.own_final[family] = self.local(
            at(self.sums)[family, place.z, :, columns],
            at(self.final)[family, place.z, :, columns],
        )
        self.z_copies[family] = copies

    def home(self, family):
        for copy in self.z_copies[family]:
            copy.wait_recv()
        self.own_final[family].wait()

    def finish(self):
        assert self.used <= self.ring_sems.shape[0]
        for waits in self.pending:
            for wait in waits:
                wait()


def rear_kernel(
    plane,
    cores,
    normed_mlp_in,
    gate_in,
    up_in,
    down_in,
    residual_in,
    projection_in,
    out_in,
    normed_in,
    lin_in,
    queries_in,
    both_in,
    attended_in,
    hidden,
    grad_out,
    stats,
    gains,
    cosine,
    sine_turned,
    query_pos,
    key_blocks,
    query_gain,
    key_gain,
    output,
    input_grad,
    small_sums,
    from_sibling,
    halves,
    from_plane,
    final,
    both_landed,
    normed,
    turned_left,
    turned_right,
    gate,
    up,
    down,
    part_in,
    landed_in,
    landed_out,
    extra_in,
    extra_out,
    residual,
    grad_residual,
    low_rows,
    sums,
    ring,
    addend,
    gain_rows,
    messages,
    z_messages,
    plane_messages,
    core_messages,
    ring_sems,
    both_sems,
    send_sems,
    recv_sems,
    local_sems,
):
    links = Links(send_sems, recv_sems, local_sems)
    tokens, width = normed.shape
    token_rows = tokens // parts
    place = Place(plane, cores, token_rows)
    returns = Returns(
        links, place, ring, addend, ring_sems, (from_sibling, halves, from_plane, sums, final)
    )
    units = gate.shape[3]
    block = width // parts
    shard = gate.shape[2]
    head = query_gain.shape[1]
    query_heads = queries_in.shape[0]
    query_width = query_heads * head
    key_width = both_in.shape[2] // 2
    key_heads = key_width // head
    group = query_heads // key_heads
    lin_width = query_width + 2 * key_width
    own_rows = place.z_rows[0]
    part_out = normed
    split = (plane, cores, shard, tokens)

    gathers = []
    all_units = pl.ds(0, units)
    out_sum = LineSum(links, place, part_out, landed_out, extra_out)
    back_sum = LineSum(links, place, part_in, landed_in, extra_in)

    def feed_forward(act, d_gate, d_up):
        own_down = links.local(down_in, at(down)[:, place.column])
        loads = [
            links.local(normed_mlp_in, normed),
            links.local(gate_in, gate),
            links.local(up_in, up),
            links.local(residual_in, residual),
        ]
        low_rows[place.z] = grad_out[...]
        gathers.append(LineGather(links, place, grad_out, lambda z: at(low_rows)[z]))
        own_down.wait()
        down_fetch = Fetch(links, place, [], down)
        down_fetch.spread()
        for copy in loads[:3]:
            copy.wait()
        tile = 256

        def hidden_tile(index, carry):
            columns = pl.ds(pl.multiple_of(index * tile, tile), tile)
            gate_lin = multiply(normed[...], gate[:, :, :, columns].reshape(width, tile))
            up_lin = multiply(normed[...], up[:, :, :, columns].reshape(width, tile))
            sigmoid = jax.nn.sigmoid(gate_lin)
            silu = gate_lin * sigmoid
            act[:, columns] = (silu * up_lin).astype(bf16)
            d_up[:, columns] = silu.astype(bf16)
            d_gate[:, columns] = (up_lin * (sigmoid + silu * (1.0 - sigmoid))).astype(bf16)
            return carry

        lax.fori_loop(0, units // tile, hidden_tile, 0)
        gathers[0].relay()
        down_fetch.forward()
        for copy in loads[3:]:
            copy.wait()
        for index in range(parts):
            columns = slice(index * block, (index + 1) * block)
            turned_left[index] = normed[:, columns].T.reshape(split)
        down_fetch.close()
        down_fetch.finish()
        for index in range(parts):
            columns = pl.ds(index * block, block)
            part_out[:, columns] = multiply_trans(
                act[...], down[index].reshape(block, units)
            ).astype(bf16)
        landed_out[place.z] = part_out[own_rows]
        gathers[0].wait()

        def grad_tile(index, carry):
            columns = pl.ds(pl.multiple_of(index * tile, tile), tile)
            grad_act = multiply(
                low_rows[...].reshape(tokens, width), down[:, :, :, columns].reshape(width, tile)
            )
            d_up[:, columns] = (grad_act * d_up[:, columns].astype(f32)).astype(bf16)
            d_gate[:, columns] = (grad_act * d_gate[:, columns].astype(f32)).astype(bf16)
            return carry

        lax.fori_loop(0, units // tile, grad_tile, 0)
        gathers[0].relayed()
        for index in range(parts):
            columns = slice(index * block, (index + 1) * block)
            turned_right[index] = low_rows[:, :, columns].reshape(tokens, block).T.reshape(split)
        in_sum = LineSum(links, place, part_in, landed_in, extra_in)
        for index in range(parts):
            columns = pl.ds(index * block, block)
            part_in[:, columns] = (
                multiply_trans(d_gate[...], gate[index].reshape(block, units))
                + multiply_trans(d_up[...], up[index].reshape(block, units))
            ).astype(bf16)
            in_sum.start(columns, False)
        landed_in[place.z] = part_in[own_rows]
        returns.give(0, turned_left, d_gate)
        returns.give(1, turned_left, d_up)
        in_sum.combine(False)
        returns.take(0, turned_left, d_gate)

        in_sum.wait()
        grad_normed = total_of(landed_in)
        values = residual[...]
        scale = lax.rsqrt(jnp.mean(values * values, axis=-1, keepdims=True) + epsilon)
        unit = values * scale
        gain_rows[1:2] = jnp.sum(grad_normed * unit, axis=0, keepdims=True)
        own_grad = grad_out[...].astype(f32)
        total = own_grad + norm_back(grad_normed * gains[1:2], unit, scale)
        grad_residual[...] = total
        low_rows[place.z] = total.astype(bf16)
        gathers.append(
            LineGather(links, place, at(low_rows)[place.z], lambda z: at(low_rows)[z])
        )
        returns.take(1, turned_left, d_up)
        gathers[1].relay()
        returns.give(2, turned_right, act)
        returns.take(2, turned_right, act)
        for copy in in_sum.sent():
            copy.wait_send()

    pl.run_scoped(
        feed_forward,
        pltpu.VMEM((tokens, units), bf16),
        pltpu.VMEM((tokens, units), bf16),
        pltpu.VMEM((tokens, units), bf16),
    )

    def attention(lin, queries, both, attended, grad_heads, delta, both_stage, both_total, query_total, grad_lin):
        out_at = pl.ds(pl.multiple_of(place.z * query_width, 128), query_width)
        out_columns = at(up)[:, :, :, pl.ds(0, query_width)]
        projection = at(gate)[:, :, :, pl.ds(0, lin_width)]
        loads = [
            links.local(at(out_in)[:, :, :, out_at], out_columns),
            links.local(attended_in, attended),
            links.local(queries_in, queries),
            links.local(both_in, both),
            links.local(lin_in, lin),
            links.local(at(projection_in)[:, :, :, pl.ds(0, lin_width)], projection),
            links.local(normed_in, part_in),
        ]
        for copy in loads:
            copy.wait()
        for index in range(parts):
            columns = slice(index * block, (index + 1) * block)
            turned_left[index] = part_in[:, columns].T.reshape(split)
        gathers[1].wait()
        out_sum.start(pl.ds(0, width))

        tile = group * head
        for index in range(key_heads):
            columns = slice(index * tile, (index + 1) * tile)
            grads = multiply(
                low_rows[...].reshape(tokens, width), up[:, :, :, columns].reshape(width, tile)
            ).astype(bf16)
            for member in range(group):
                number = index * group + member
                own = grads[:, member * head : (member + 1) * head]
                grad_heads[number] = own
                mixed = attended[:, number * head : (number + 1) * head].astype(f32)
                delta[number : number + 1] = jnp.sum(
                    (own.astype(f32) * mixed).T, axis=0, keepdims=True
                )

        factor = head ** (-0.5)
        score_factor = factor * 1.4426950408889634
        chunk = min(256, tokens)
        chunks_each = tokens // chunk
        lanes = group * tokens
        piece_rows = token_rows // 2
        both_copies, both_own = [], []
        for key_head in range(key_heads):
            members = slice(key_head * group, (key_head + 1) * group)
            query_block = queries[members].reshape(lanes, head)
            grad_block = grad_heads[members].reshape(lanes, head)
            numbers = range(key_head * group, (key_head + 1) * group)
            stats_row = jnp.concatenate([stats[number : number + 1] for number in numbers], axis=1)
            delta_row = jnp.concatenate([delta[number : number + 1] for number in numbers], axis=1)
            positions = jnp.concatenate([query_pos[...]] * group, axis=1)
            query_total[...] = jnp.zeros_like(query_total)

            def back_chunk(index, carry):
                source, row = index // chunks_each, index % chunks_each
                rows = pl.ds(pl.multiple_of(row * chunk, chunk), chunk)
                keys = both[source, rows, pl.ds(key_head * head, head)]
                values = both[source, rows, pl.ds(key_width + key_head * head, head)]
                scores = multiply_trans(keys, query_block) * score_factor
                spots = lax.broadcasted_iota(jnp.int32, (chunk, 1), 0)
                starts = jnp.zeros((chunk, 1), jnp.int32)
                for piece in range(chunk // piece_rows):
                    start = key_blocks[index * (chunk // piece_rows) + piece] * piece_rows
                    starts = jnp.where(spots >= piece * piece_rows, start - piece * piece_rows, starts)
                weights = jnp.where(
                    spots + starts <= positions, jnp.exp2(scores - stats_row), 0.0
                )
                grad_weights = multiply_trans(values, grad_block)
                grad_scores = (weights * (grad_weights - delta_row)).astype(bf16)
                query_total[...] += outer_rows(keys, grad_scores)
                both[source, rows, pl.ds(key_head * head, head)] = (
                    multiply(grad_scores, query_block) * factor
                ).astype(bf16)
                both[source, rows, pl.ds(key_width + key_head * head, head)] = multiply(
                    weights.astype(bf16), grad_block
                ).astype(bf16)
                return carry

            lax.fori_loop(0, plane * chunks_each, back_chunk, 0)
            for start in (key_head * head, key_width + key_head * head):
                columns = pl.ds(start, head)
                for step in range(1, plane):
                    other = place.in_plane(step)
                    both_copies.append(
                        links.send(
                            at(both)[other, :, columns],
                            at(both_landed)[place.p, :, columns],
                            tracked=False,
                            p=other,
                        )
                    )
                both_own.append(
                    links.local(
                        at(both)[place.p, :, columns], at(both_landed)[place.p, :, columns]
                    )
                )
            if key_head == 0:
                out_sum.combine()
            grad_queries = query_total[...].T * factor
            for member in range(group):
                number = key_head * group + member
                rows = slice(member * tokens, (member + 1) * tokens)
                own = grad_queries[rows]
                lin_rows = lin[:, number * head : (number + 1) * head]
                scale = lax.rsqrt(jnp.mean(lin_rows * lin_rows, axis=-1, keepdims=True) + epsilon)
                unit = lin_rows * scale
                turned = own * cosine[...] - half_turn(own) * sine_turned[...]
                gained = jnp.sum(turned * unit, axis=0, keepdims=True)
                if number == 0:
                    messages[0, 0:1, block : block + head] = gained
                else:
                    messages[0, 0:1, block : block + head] += gained
                grad_lin[:, number * head : (number + 1) * head] = norm_back(
                    turned * query_gain[...], unit, scale
                ).astype(bf16)

        for index in range(parts):
            columns = slice(index * block, (index + 1) * block)
            turned_right[index] = low_rows[:, :, columns].reshape(tokens, block).T.reshape(split)
        returns.give(3, turned_right, attended, query_width)
        query_lin = at(grad_lin)[:, pl.ds(0, query_width)].get()
        returns.give(3, turned_left, query_lin)
        returns.take(3, turned_right, attended, query_width)
        returns.along_z(0, all_units)
        returns.take(3, turned_left, query_lin)
        returns.along_z(1, all_units)

        for copy in both_copies:
            copy.wait_recv()
        for copy in both_own:
            copy.wait()

        def load_both(source):
            return Copy(
                at(both_landed)[source], at(both_stage)[source % 2], [(both_sems, source)]
            )

        load = load_both(0)
        for source in range(plane):
            load.wait()
            if source + 1 < plane:
                load = load_both(source + 1)
            landed = both_stage[source % 2].astype(f32)
            if source == 0:
                both_total[...] = landed
            else:
                both_total[...] += landed
        for key_head in range(key_heads):
            start = query_width + key_width + key_head * head
            grad_lin[:, start : start + head] = both_total[
                :, key_width + key_head * head : key_width + (key_head + 1) * head
            ].astype(bf16)
            own = both_total[:, key_head * head : (key_head + 1) * head]
            start = query_width + key_head * head
            lin_rows = lin[:, start : start + head]
            scale = lax.rsqrt(jnp.mean(lin_rows * lin_rows, axis=-1, keepdims=True) + epsilon)
            unit = lin_rows * scale
            turned = own * cosine[...] - half_turn(own) * sine_turned[...]
            gained = jnp.sum(turned * unit, axis=0, keepdims=True)
            if key_head == 0:
                messages[0, 1:2, block : block + head] = gained
            else:
                messages[0, 1:2, block : block + head] += gained
            grad_lin[:, start : start + head] = norm_back(turned * key_gain[...], unit, scale).astype(
                bf16
            )

        for index in range(parts):
            columns = pl.ds(index * block, block)
            part_in[:, columns] = multiply_trans(
                grad_lin[...], gate[index, :, :, 0:lin_width].reshape(block, lin_width)
            ).astype(bf16)
            back_sum.start(columns)
        landed_in[place.z] = part_in[own_rows]
        both_lin = at(grad_lin)[:, pl.ds(query_width, 2 * key_width)].get()
        returns.give(4, turned_left, both_lin)
        back_sum.combine()
        returns.take(4, turned_left, both_lin)
        returns.along_z(2, all_units)
        for copy in both_copies:
            copy.wait_send()

    pl.run_scoped(
        attention,
        pltpu.VMEM((tokens, query_width + key_width), f32),
        pltpu.VMEM((query_heads, tokens, head), bf16),
        pltpu.VMEM((plane, tokens, 2 * key_width), bf16),
        pltpu.VMEM((tokens, query_width), bf16),
        pltpu.VMEM((query_heads, tokens, head), bf16),
        pltpu.VMEM((8, tokens), f32),
        pltpu.VMEM((2, tokens, 2 * key_width), bf16),
        pltpu.VMEM((tokens, 2 * key_width), f32),
        pltpu.VMEM((head, group * tokens), f32),
        pltpu.VMEM((tokens, lin_width), bf16),
    )
    back_sum.wait()
    grad_normed = total_of(landed_in)
    values = hidden[...].astype(f32)
    scale = lax.rsqrt(jnp.mean(values * values, axis=-1, keepdims=True) + epsilon)
    unit = values * scale
    gain_rows[0:1] = jnp.sum(grad_normed * unit, axis=0, keepdims=True)
    input_grad[...] = (
        grad_residual[...] + norm_back(grad_normed * gains[0:1], unit, scale)
    ).astype(bf16)

    for index in range(1, parts):
        messages[index, :, block : block + head] = messages[0, :, block : block + head]
    for index in range(parts):
        messages[index, 0:2, 0:block] = gain_rows[:, index * block : (index + 1) * block]
    copies = [
        links.send(at(messages)[place.along_z(step)], at(z_messages)[place.z], z=place.along_z(step))
        for step in z_steps
    ]
    z_messages[place.z] = messages[place.z]
    out_sum.wait()
    output[...] = (residual[...] + total_of(landed_out)).astype(bf16)
    for copy in copies:
        copy.wait_recv()
    plane_messages[place.p] = (z_messages[0] + z_messages[1]) + (z_messages[2] + z_messages[3])
    copies = [
        links.send(
            at(plane_messages)[place.p], at(plane_messages)[place.p], p=place.in_plane(step)
        )
        for step in range(1, plane)
    ]
    returns.along_z(3, pl.ds(0, 2 * query_width))
    returns.along_z(4, pl.ds(0, 2 * key_width))
    for copy in copies:
        copy.wait_recv()
    total = plane_messages[0]
    for source in range(1, plane):
        total += plane_messages[source]
    core_messages[place.c] = total
    copies = [
        links.send(at(core_messages)[place.c], at(core_messages)[place.c], c=other)
        for other in place.siblings()
    ]
    for copy in copies:
        copy.wait_recv()
    total = core_messages[0]
    for source in range(1, cores):
        total += core_messages[source]
    small_sums[...] = total
    for family in range(5):
        returns.home(family)
    gathers[1].relayed()
    returns.finish()
    links.finish()


def rear(plane, cores, large, small):
    normed_mlp, gate = large[0], large[1]
    projection, lin, queries, both = large[5], large[8], large[9], large[10]
    tokens, width = normed_mlp.shape
    token_rows = tokens // parts
    _, columns, shard, units = gate.shape
    query_heads, _, head = queries.shape
    query_width = query_heads * head
    key_width = both.shape[2] // 2
    key_heads = key_width // head
    lin_width = query_width + 2 * key_width
    block = width // parts
    any_space, vmem = pl.BlockSpec(memory_space=pl.ANY), pl.BlockSpec(memory_space=pltpu.VMEM)
    copies = 120 + 10 + 6 + 24 + 24 + 16 * plane + 48 + 16
    assert 2 * max(query_width, key_width) <= units
    shapes = [
        ((token_rows, width), bf16),
        ((token_rows, width), bf16),
        ((8, block + head), f32),
        ((5, parts, plane, shard, units), bf16),
        ((5, parts, plane, shard, units), bf16),
        ((5, plane, parts, shard, units), bf16),
        ((5, parts, shard, units), bf16),
        ((plane, tokens, 2 * key_width), bf16),
    ]
    turned = (parts, plane, cores, shard, tokens)
    message = (8, block + head)
    return pl.pallas_call(
        functools.partial(rear_kernel, plane, cores),
        out_shape=[jax.ShapeDtypeStruct(shape, kind) for shape, kind in shapes],
        in_specs=[any_space] * 12
        + [vmem] * 7
        + [pl.BlockSpec(memory_space=pltpu.SMEM)]
        + [vmem] * 2,
        out_specs=[vmem] * 3 + [any_space] * 5,
        scratch_shapes=[
            pltpu.VMEM((tokens, width), bf16),
            pltpu.VMEM(turned, bf16),
            pltpu.VMEM(turned, bf16),
            pltpu.VMEM(gate.shape, bf16),
            pltpu.VMEM(gate.shape, bf16),
            pltpu.VMEM(gate.shape, bf16),
            pltpu.VMEM((tokens, width), bf16),
            pltpu.VMEM((parts, token_rows, width), bf16),
            pltpu.VMEM((parts, token_rows, width), bf16),
            pltpu.VMEM((token_rows, width), bf16),
            pltpu.VMEM((token_rows, width), bf16),
            pltpu.VMEM((token_rows, width), f32),
            pltpu.VMEM((token_rows, width), f32),
            pltpu.VMEM((parts, token_rows, width), bf16),
            pltpu.VMEM((5, parts, shard, units), bf16),
            pltpu.VMEM((4, plane, shard, units), bf16),
            pltpu.VMEM((parts if plane == 4 else 1, plane, shard, units), bf16),
            pltpu.VMEM((2, width), f32),
            pltpu.VMEM((parts,) + message, f32),
            pltpu.VMEM((parts,) + message, f32),
            pltpu.VMEM((plane,) + message, f32),
            pltpu.VMEM((cores,) + message, f32),
            pltpu.SemaphoreType.DMA((160,)),
            pltpu.SemaphoreType.DMA((plane,)),
            pltpu.SemaphoreType.DMA((copies,)),
            pltpu.SemaphoreType.DMA((copies,)),
            pltpu.SemaphoreType.DMA((24,)),
        ],
        compiler_params=pltpu.CompilerParams(
            has_side_effects=True, vmem_limit_bytes=63 * 1024 * 1024
        ),
        cost_estimate=pl.CostEstimate(flops=4 * 10**10, bytes_accessed=10**8, transcendentals=10**7),
    )(*large, *small)


def make_local(plane, cores):
    def local(
        hidden_in,
        block_map,
        query_weight,
        key_weight,
        value_weight,
        out_weight,
        gate_weight,
        up_weight,
        down_weight,
        attention_norm_gain,
        feedforward_gain,
        query_gain,
        key_gain,
        output_grad,
    ):
        shard = query_weight.shape[0]
        hidden_own, grad_own = hidden_in[0], output_grad[0]
        row_count, features = hidden_own.shape
        piece_rows = row_count // 2
        head_width = query_gain.shape[0]
        p_index = lax.axis_index("p")
        tokens = parts * row_count

        blocks = block_map[0].reshape(parts, plane, 2)
        offsets = jnp.arange(piece_rows, dtype=jnp.int32)
        all_pos = blocks.transpose(1, 0, 2)[..., None] * piece_rows + offsets
        all_pos = all_pos.reshape(plane, tokens)
        query_pos = lax.dynamic_index_in_dim(all_pos, p_index, 0, keepdims=False)
        key_pos = all_pos.reshape(-1)
        cosine, sine_table = rope_tables(query_pos, head_width)
        sign = jnp.where(jnp.arange(head_width) < head_width // 2, -1.0, 1.0).astype(f32)
        query_gain_float = query_gain.astype(f32)
        key_gain_float = key_gain.astype(f32)
        gain_block = jnp.stack([attention_norm_gain, feedforward_gain], axis=1)
        gain_block = jnp.pad(gain_block, ((0, 0), (0, 126)))

        (
            normed,
            projection,
            lin,
            queries,
            both,
            attended_low,
            out_full,
            normed_mlp,
            own_residual,
            gate_columns,
            up_columns,
            down_columns,
            stats,
            gains,
        ) = front(
            plane,
            cores,
            hidden_own,
            (
                query_weight,
                key_weight,
                value_weight,
                out_weight,
                gate_weight,
                up_weight,
                down_weight,
            ),
            gain_block,
            (cosine[:, 0], sine_table[:, 0] * sign),
            (query_pos[None], key_pos[:, None]),
            (query_gain_float[None], key_gain_float[None]),
        )
        results = rear(
            plane,
            cores,
            (
                normed_mlp,
                gate_columns,
                up_columns,
                down_columns,
                own_residual,
                projection,
                out_full,
                normed,
                lin,
                queries,
                both,
                attended_low,
            ),
            (
                hidden_own,
                grad_own,
                stats,
                gains,
                cosine[:, 0],
                sine_table[:, 0] * sign,
                query_pos[None],
                blocks.transpose(1, 0, 2).reshape(-1),
                query_gain_float[None],
                key_gain_float[None],
            ),
        )
        output, input_grad = results[:2]
        small_sums, final = results[2], results[6]

        def home(family, start, count):
            columns = final[family, :, :, start : start + count].transpose(1, 0, 2)
            return columns.astype(f32).reshape(shard, parts * count)

        units = gate_weight.shape[1] // parts
        query_width, key_width = query_weight.shape[1] // parts, key_weight.shape[1] // parts
        block = features // parts
        own_column = p_index * cores + lax.axis_index("c")
        own_gains = lax.dynamic_slice_in_dim(small_sums[:2, :block], own_column * shard, shard, 1)
        head_sums = small_sums[:2, block:]
        return (
            (output[None], input_grad[None])
            + (
                home(3, 0, query_width),
                home(4, 0, key_width),
                home(4, key_width, key_width),
                home(3, query_width, query_width),
                home(0, 0, units),
                home(1, 0, units),
                home(2, 0, units),
            )
            + (own_gains[0], own_gains[1], head_sums[0], head_sums[1])
        )

    return local


def solution(mesh):
    ctx_count, core_count = mesh.shape["ctx"], mesh.shape["fsdp"]
    plane = ctx_count // parts
    fine_mesh = Mesh(mesh.devices.reshape(parts, plane, core_count), ("z", "p", "c"))
    token_spec = P("c", ("z", "p"), None)
    weight_spec = P(("z", "p", "c"), None)
    gain_spec = P(("z", "p", "c"))
    return jax.shard_map(
        make_local(plane, core_count),
        mesh=fine_mesh,
        in_specs=(
            (token_spec, P("c", None)) + (weight_spec,) * 7 + (gain_spec,) * 2 + (P(), P(), token_spec)
        ),
        out_specs=(token_spec,) * 2 + (weight_spec,) * 7 + (gain_spec,) * 2 + (P(), P()),
        check_vma=False,
    )
```

```python
import functools

import jax
import jax.numpy as jnp
from jax import lax
from jax.experimental import pallas as pl
from jax.experimental.pallas import tpu as pltpu
from jax.sharding import Mesh, PartitionSpec as P

epsilon = 1e-06
rotary_base = 1000000.0
masked_score = -1e30
parts = 4
bf16 = jnp.bfloat16
f32 = jnp.float32


def norm_back(weighted, unit, scale_row):
    inner_mean = jnp.mean(weighted * unit, axis=-1, keepdims=True)
    return scale_row * (weighted - unit * inner_mean)


def rope_tables(positions, width):
    half_width = width // 2
    frequency = rotary_base ** (-(jnp.arange(half_width, dtype=f32) * 2.0 / width))
    angles = positions.astype(f32)[:, None] * frequency[None, :]
    angles = jnp.concatenate([angles, angles], axis=-1)
    return jnp.cos(angles)[:, None, :], jnp.sin(angles)[:, None, :]


def multiply(left, right):
    return jnp.dot(left, right, preferred_element_type=f32)


def multiply_trans(left, right):
    return lax.dot_general(left, right, (((1,), (1,)), ((), ())), preferred_element_type=f32)


def outer_rows(left, right):
    return lax.dot_general(left, right, (((0,), (0,)), ((), ())), preferred_element_type=f32)


class Part:
    def __init__(self, ref, index=None):
        self.ref, self.index = ref, index

    def __getitem__(self, index):
        return Part(self.ref, index)

    def get(self):
        return self.ref if self.index is None else self.ref.at[self.index]


def at(ref):
    return Part(ref)


def found(ref):
    return ref.get() if isinstance(ref, Part) else ref


class Copy:
    def __init__(self, source, target, sems, device=None, when=None):
        self.source, self.target, self.sems = source, target, sems
        self.device, self.when = device, when
        self.guarded(lambda: self.describe().start())

    def guarded(self, action):
        if self.when is None:
            action()
        else:
            pl.when(self.when)(action)

    def describe(self):
        source, target = found(self.source), found(self.target)
        sems = [array.at[index] for array, index in self.sems]
        if self.device is None:
            return pltpu.make_async_copy(source, target, sems[0])
        return pltpu.make_async_remote_copy(
            src_ref=source,
            dst_ref=target,
            send_sem=sems[0],
            recv_sem=sems[1],
            device_id=self.device,
            device_id_type=pl.DeviceIdType.MESH,
        )

    def wait(self):
        self.describe().wait()

    def wait_send(self):
        self.guarded(lambda: self.describe().wait_send())

    def wait_recv(self):
        self.describe().wait_recv()


class Links:
    def __init__(self, send_sems, recv_sems, local_sems):
        self.send_sems, self.recv_sems, self.local_sems = send_sems, recv_sems, local_sems
        self.count, self.local_count = 0, 0
        self.sent, self.kept = [], []

    def send(self, source, target, tracked=True, when=None, lands=None, **device):
        index = self.count
        self.count += 1
        received = index if lands is None else lands.sems[1][1]
        copy = Copy(
            source, target, [(self.send_sems, index), (self.recv_sems, received)], device, when
        )
        if tracked:
            self.sent.append(copy)
        return copy

    def local(self, source, target):
        index = self.local_count
        self.local_count += 1
        return Copy(source, target, [(self.local_sems, index)])

    def keep(self, source, target):
        self.kept.append(self.local(source, target))

    def finish(self):
        assert self.count <= self.send_sems.shape[0]
        assert self.local_count <= self.local_sems.shape[0]
        for copy in self.sent:
            copy.wait_send()
        for copy in self.kept:
            copy.wait()


class LineGather:
    def __init__(self, links, place, source, block):
        self.links, self.place, self.block = links, place, block
        target = block(place.z)
        self.far = links.send(source, target, z=place.along_z(2))
        self.above = links.send(source, target, when=place.not_last, z=place.along_z(1))
        self.below = links.send(source, target, when=place.not_first, z=place.along_z(3))

    def relay(self):
        links, place = self.links, self.place
        self.far.wait_recv()
        block = self.block(place.along_z(2))
        self.relays = (
            links.send(block, block, False, place.second, self.above, z=place.along_z(3)),
            links.send(block, block, False, place.third, self.below, z=place.along_z(1)),
        )

    def wait(self):
        self.above.wait_recv()
        self.below.wait_recv()

    def relayed(self):
        for copy in self.relays:
            copy.wait_send()


class LineSum:
    def __init__(self, links, place, part, landed, extra):
        self.links, self.place = links, place
        self.part, self.landed, self.extra = part, landed, extra
        self.near, self.extras, self.far, self.columns = [], [], [], []

    def start(self, columns, tracked=True):
        links, place = self.links, self.place
        target = at(self.landed)[place.z, :, columns]
        rows = place.z_rows
        above, below = at(self.part)[rows[1], columns], at(self.part)[rows[3], columns]
        beyond = at(self.part)[rows[2], columns]
        self.columns.append(columns)
        self.far.append(links.send(beyond, target, tracked, place.at_end, z=place.along_z(2)))
        self.near.append(
            (
                links.send(above, target, tracked, place.not_last, z=place.along_z(1)),
                links.send(below, target, tracked, place.not_first, z=place.along_z(3)),
            )
        )
        extra = at(self.extra)[:, columns]
        self.extras.append(
            (
                links.send(below, extra, tracked, place.first, z=place.along_z(1)),
                links.send(above, extra, tracked, place.last, z=place.along_z(3)),
            )
        )

    def combine(self, tracked=True):
        links, place = self.links, self.place

        @pl.when(place.at_end)
        def nothing_comes():
            self.landed[place.opposite] = jnp.zeros(self.landed.shape[1:], bf16)

        for columns, extras, far in zip(self.columns, self.extras, self.far):
            rows = place.z_rows[2]

            @pl.when(place.second)
            def arrived():
                extras[0].wait_recv()

            @pl.when(place.third)
            def arrived_too():
                extras[1].wait_recv()

            @pl.when(place.inside)
            def add():
                total = self.part[rows, columns].astype(f32) + self.extra[:, columns].astype(f32)
                self.part[rows, columns] = total.astype(bf16)

            self.near.append(
                (
                    links.send(
                        at(self.part)[rows, columns],
                        at(self.landed)[place.z, :, columns],
                        tracked,
                        place.inside,
                        lands=far,
                        z=place.along_z(2),
                    ),
                )
            )

    def wait(self):
        place = self.place
        for index, far in enumerate(self.far):
            above, below = self.near[index]

            @pl.when(place.not_first)
            def from_below():
                above.wait_recv()

            @pl.when(place.not_last)
            def from_above():
                below.wait_recv()

            far.wait_recv()

    def sent(self):
        return self.far + [copy for copies in self.near + self.extras for copy in copies]


class Place:
    def __init__(self, plane, cores, token_rows):
        self.plane, self.cores = plane, cores
        self.z, self.p, self.c = (lax.axis_index(axis) for axis in ("z", "p", "c"))
        self.column = self.p * cores + self.c
        self.other_core = lax.rem(self.c + 1, cores)
        self.z_others = [lax.rem(self.z + step, parts) for step in range(parts)]
        self.p_others = [lax.rem(self.p + step, plane) for step in range(plane)]
        self.columns_before = [
            lax.rem(self.p + plane - step, plane) * cores + self.c for step in range(plane)
        ]
        self.first, self.last = self.z == 0, self.z == parts - 1
        self.second, self.third = self.z == 1, self.z == parts - 2
        self.not_first, self.not_last = self.z != 0, self.z != parts - 1
        self.at_end = jnp.logical_or(self.first, self.last)
        self.inside = jnp.logical_not(self.at_end)
        self.opposite = parts - 1 - self.z
        self.relayed = plane == 4
        if self.relayed:
            self.flips = [self.p + 1 - 2 * lax.rem(self.p, 2), lax.rem(self.p + 2, 4)]
            flipped = lax.rem(self.flips[0] + 2, 4)
            self.flip_columns = [flip * cores + self.c for flip in self.flips + [flipped]]
        self.z_rows = [
            pl.ds(pl.multiple_of(other * token_rows, token_rows), token_rows)
            for other in self.z_others
        ]

    def along_z(self, step):
        return self.z_others[step]

    def in_plane(self, step):
        return self.p_others[step]

    def before(self, step):
        return self.columns_before[step]

    def siblings(self):
        return [self.other_core]


z_steps = (1, 3, 2)


class Fetch:
    def __init__(self, links, place, pieces, gathered, line_only=False):
        self.links, self.place, self.pieces, self.gathered = links, place, pieces, gathered
        self.line_only = line_only
        self.first, self.own = [], []

    def mine(self, columns):
        if self.line_only:
            return at(self.gathered)[self.place.z, :, columns]
        return at(self.gathered)[self.place.z, self.place.column, :, columns]

    def begin(self):
        links, place = self.links, self.place
        mine = self.mine
        for shard, width, start, split in self.pieces:
            for step in z_steps:
                other = place.along_z(step)
                first = pl.multiple_of(other * width, 128) if split else 0
                self.first.append(
                    links.send(at(shard)[:, pl.ds(first, width)], mine(pl.ds(start, width)), z=other)
                )
            first = pl.multiple_of(place.z * width, 128) if split else 0
            self.own.append(
                links.local(at(shard)[:, pl.ds(first, width)], mine(pl.ds(start, width)))
            )

    def arrive(self):
        for copy in self.own:
            copy.wait()
        for copy in self.first:
            copy.wait_recv()

    def spread(self):
        links, place = self.links, self.place
        self.arrive()
        block = at(self.gathered)[:, place.column]
        if place.relayed:
            self.second = [links.send(block, block, p=other) for other in place.flips]
        else:
            self.second = [
                links.send(block, block, p=place.in_plane(step)) for step in range(1, place.plane)
            ]
        self.third = [links.send(block, block, c=other) for other in place.siblings()]
        self.halves = []

    def pass_on(self, column):
        block = at(self.gathered)[:, column]
        self.third += [self.links.send(block, block, c=other) for other in self.place.siblings()]

    def forward(self):
        links, place = self.links, self.place
        if place.relayed:
            for side, copy in enumerate(self.second):
                copy.wait_recv()
                column = place.flip_columns[side]
                half = at(self.gathered)[pl.ds(side * (parts // 2), parts // 2), column]
                self.halves.append(links.send(half, half, p=place.flips[1 - side]))
                self.pass_on(column)
        else:
            for step, copy in enumerate(self.second, 1):
                copy.wait_recv()
                self.pass_on(place.before(step))

    def close(self):
        if self.place.relayed:
            for copy in self.halves:
                copy.wait_recv()
            self.pass_on(self.place.flip_columns[2])

    def finish(self):
        for copy in self.third:
            copy.wait_recv()


def key_positions(key_blocks, index, chunk, piece_rows):
    pieces = chunk // piece_rows
    spots = lax.broadcasted_iota(jnp.int32, (chunk, 1), 0)
    starts = jnp.zeros((chunk, 1), jnp.int32)
    for piece in range(pieces):
        start = key_blocks[index * pieces + piece] * piece_rows - piece * piece_rows
        starts = jnp.where(spots >= piece * piece_rows, start, starts)
    return spots + starts


def front_kernel(
    plane,
    cores,
    hidden,
    query_weight,
    key_weight,
    value_weight,
    out_weight,
    gate_weight,
    up_weight,
    down_weight,
    gain_block,
    grad_out,
    cosine,
    sine_turned,
    query_pos,
    key_blocks,
    query_gain,
    key_gain,
    normed_out,
    projection_out,
    lin_out,
    queries_out,
    both_out,
    attended_out,
    out_columns_out,
    normed_mlp_out,
    residual_out,
    gate_out,
    up_out,
    down_out,
    grad_half_out,
    stats_out,
    gains_out,
    hidden_all,
    normed,
    projection,
    lin,
    queries,
    both,
    attended_all,
    out_full,
    residual,
    normed_mlp,
    mixed,
    send_sems,
    recv_sems,
    local_sems,
):
    links = Links(send_sems, recv_sems, local_sems)
    token_rows, width = hidden.shape
    place = Place(plane, cores, token_rows)
    tokens = parts * token_rows
    head = query_gain.shape[1]
    query_width = query_weight.shape[1] // parts
    key_width = key_weight.shape[1] // parts
    query_heads, key_heads = query_width // head, key_width // head
    group = query_heads // key_heads
    hidden_units = gate_weight.shape[1] // parts
    lin_width = query_width + 2 * key_width

    heads_fetch = Fetch(
        links,
        place,
        [
            (query_weight, query_width, 0, True),
            (key_weight, key_width, query_width, True),
            (value_weight, key_width, query_width + key_width, True),
            (gain_block, 128, lin_width, False),
        ],
        projection,
    )
    out_fetch = Fetch(links, place, [], out_full)
    mlp_fetches = [
        Fetch(links, place, [(weight, hidden_units, 0, True)], target)
        for weight, target in ((gate_weight, gate_out), (up_weight, up_out))
    ]
    down_fetch = Fetch(links, place, [(down_weight, hidden_units, 0, True)], down_out, True)
    heads_fetch.begin()
    mlp_fetches[0].begin()
    heads_fetch.spread()
    hidden_own = links.local(hidden, hidden_all.at[place.z])
    hidden_gather = LineGather(links, place, hidden, lambda z: at(hidden_all)[z])
    mlp_fetches[0].spread()
    heads_fetch.forward()
    hidden_gather.relay()
    heads_fetch.close()
    heads_fetch.finish()
    links.keep(projection, projection_out)
    hidden_own.wait()
    hidden_gather.wait()
    out_fetch.own.append(links.local(out_weight, at(out_full)[place.z, place.column]))
    out_gather = LineGather(
        links, place, out_weight, lambda z: at(out_full)[z, place.column]
    )
    for fetch in (mlp_fetches[1], down_fetch):
        fetch.begin()

    gain_columns = projection[:, :, :, lin_width : lin_width + 128].reshape(width, 128)
    gain_rows = gain_columns.astype(f32).T
    gains_out[...] = gain_rows[:8]

    def norm_one(index, carry):
        values = hidden_all[index].astype(f32)
        scale = lax.rsqrt(jnp.mean(values * values, axis=-1, keepdims=True) + epsilon)
        rows = pl.ds(pl.multiple_of(index * token_rows, token_rows), token_rows)
        normed[rows] = (values * scale * gains_out[0:1]).astype(bf16)
        return carry

    lax.fori_loop(0, parts, norm_one, 0)
    links.keep(normed, normed_out)

    tile = 2 * head

    def project(index, carry):
        columns = pl.ds(pl.multiple_of(index * tile, tile), tile)
        weights = projection[:, :, :, columns].reshape(width, tile)
        lin[:, columns] = jnp.dot(normed[...], weights, preferred_element_type=f32)
        return carry

    lax.fori_loop(0, lin_width // tile, project, 0)
    own_both = both.at[place.p]

    def rope(values, gain):
        scale = lax.rsqrt(jnp.mean(values * values, axis=-1, keepdims=True) + epsilon)
        gained = values * scale * gain
        turned = pltpu.roll(gained, head // 2, 1)
        return (gained * cosine[...] + turned * sine_turned[...]).astype(bf16)

    for index in range(key_heads):
        columns = slice(query_width + index * head, query_width + (index + 1) * head)
        own_both[:, index * head : (index + 1) * head] = rope(lin[:, columns], key_gain[...])
    own_both[:, key_width:] = lin[:, query_width + key_width :].astype(bf16)
    both_copies = [
        links.send(own_both, own_both, p=place.in_plane(step)) for step in range(1, plane)
    ]
    for index in range(query_heads):
        columns = slice(index * head, (index + 1) * head)
        queries[index] = rope(lin[:, columns], query_gain[...])
    links.keep(lin.at[:, pl.ds(0, query_width + key_width)], lin_out)
    links.keep(queries, queries_out)
    mlp_fetches[0].forward()
    for copy in both_copies:
        copy.wait_recv()
    links.keep(both, both_out)
    out_gather.relay()

    factor = head ** (-0.5) * 1.4426950408889634
    chunk = min(256, tokens)
    chunks_each = tokens // chunk
    lanes = group * tokens
    own_attended = attended_all.at[place.z]
    attended_gathers = []
    for key_head in range(key_heads):
        block = queries[key_head * group : (key_head + 1) * group].reshape(lanes, head)
        positions = jnp.concatenate([query_pos[...]] * group, axis=1)
        mixed[...] = jnp.zeros_like(mixed)

        def attend_chunk(index, carry):
            best, summed = carry
            source, row = index // chunks_each, index % chunks_each
            rows = pl.ds(pl.multiple_of(row * chunk, chunk), chunk)
            keys = both[source, rows, pl.ds(key_head * head, head)]
            values = both[source, rows, pl.ds(key_width + key_head * head, head)]
            scores = multiply_trans(keys, block) * factor
            allowed = key_positions(key_blocks, index, chunk, token_rows // 2) <= positions
            scores = jnp.where(allowed, scores, masked_score)
            new_best = jnp.maximum(best, jnp.max(scores, axis=0, keepdims=True))
            weights = jnp.exp2(scores - new_best)
            shrink = jnp.exp2(best - new_best)
            summed = summed * shrink + jnp.sum(weights, axis=0, keepdims=True)
            mixed[...] = mixed[...] * shrink + outer_rows(values, weights.astype(bf16))
            return new_best, summed

        best, summed = lax.fori_loop(
            0,
            plane * chunks_each,
            attend_chunk,
            (jnp.full((1, lanes), masked_score, f32), jnp.zeros((1, lanes), f32)),
        )
        mixed_rows = (mixed[...] / summed).T
        stats = best + jnp.log2(summed)
        for member in range(group):
            index = key_head * group + member
            stats_out[index : index + 1] = stats[:, member * tokens : (member + 1) * tokens]
            own_attended[:, index * head : (index + 1) * head] = mixed_rows[
                member * tokens : (member + 1) * tokens
            ].astype(bf16)
        columns = pl.ds(key_head * group * head, group * head)
        attended_gathers.append(
            LineGather(
                links,
                place,
                at(attended_all)[place.z, :, columns],
                lambda z, columns=columns: at(attended_all)[z, :, columns],
            )
        )
        if key_head == 0:
            mlp_fetches[0].close()
            out_gather.wait()
            out_fetch.spread()
    links.keep(own_attended, attended_out)
    out_fetch.forward()
    mlp_fetches[1].spread()
    for gather in attended_gathers:
        gather.relay()
    out_fetch.close()
    out_fetch.finish()
    links.keep(out_full, out_columns_out)
    mlp_fetches[1].forward()
    for gather in attended_gathers:
        gather.wait()
    half = pl.ds(0, width // 2)
    links.keep(at(grad_out)[:, half], at(grad_half_out)[place.z])
    grad_gather = LineGather(
        links, place, at(grad_out)[:, half], lambda z: at(grad_half_out)[z]
    )

    def add_out(index, carry):
        weights = out_full[index].reshape(width // parts, parts * query_width)
        columns = pl.ds(pl.multiple_of(index * (width // parts), 128), width // parts)
        total = hidden_all[:, :, columns].reshape(tokens, width // parts).astype(f32)
        for other in range(parts):
            total += multiply_trans(
                attended_all[other], weights[:, other * query_width : (other + 1) * query_width]
            )
        residual[:, columns] = total
        return carry

    lax.fori_loop(0, parts, add_out, 0)

    def norm_two(index, carry):
        rows = pl.ds(pl.multiple_of(index * token_rows, token_rows), token_rows)
        values = residual[rows]
        scale = lax.rsqrt(jnp.mean(values * values, axis=-1, keepdims=True) + epsilon)
        normed_mlp[rows] = (values * scale * gains_out[1:2]).astype(bf16)
        return carry

    lax.fori_loop(0, parts, norm_two, 0)
    links.keep(normed_mlp, normed_mlp_out)
    own_rows = place.z_rows[0]
    links.keep(residual.at[own_rows], residual_out)
    grad_gather.relay()
    mlp_fetches[1].close()
    down_fetch.arrive()
    grad_gather.wait()
    for fetch in mlp_fetches:
        fetch.finish()
    for gather in [hidden_gather, out_gather, grad_gather] + attended_gathers:
        gather.relayed()
    links.finish()


def front(plane, cores, hidden, weights, gain_block, grad_out, tables, positions, head_gains):
    token_rows, width = hidden.shape
    tokens = parts * token_rows
    shard = weights[0].shape[0]
    head = head_gains[0].shape[1]
    query_width, key_width = weights[0].shape[1] // parts, weights[1].shape[1] // parts
    hidden_units = weights[4].shape[1] // parts
    lin_width = query_width + 2 * key_width
    query_heads = query_width // head
    group = query_width // key_width
    stacked = (parts, plane * cores, shard)
    copies = 24 + 5 * (2 * plane + 8) + plane + 24
    any_space, vmem = pl.BlockSpec(memory_space=pl.ANY), pl.BlockSpec(memory_space=pltpu.VMEM)
    outputs = [
        ((tokens, width), bf16),
        (stacked + (lin_width + 128,), bf16),
        ((tokens, query_width + key_width), f32),
        ((query_heads, tokens, head), bf16),
        ((plane, tokens, 2 * key_width), bf16),
        ((tokens, query_width), bf16),
        (stacked + (parts * query_width,), bf16),
        ((tokens, width), bf16),
        ((token_rows, width), f32),
        (stacked + (hidden_units,), bf16),
        (stacked + (hidden_units,), bf16),
        ((parts, shard, hidden_units), bf16),
        ((parts, token_rows, width // 2), bf16),
        ((8, tokens), f32),
        ((8, width), f32),
    ]
    return pl.pallas_call(
        functools.partial(front_kernel, plane, cores),
        out_shape=[jax.ShapeDtypeStruct(shape, kind) for shape, kind in outputs],
        in_specs=[any_space] * 10
        + [vmem] * 3
        + [pl.BlockSpec(memory_space=pltpu.SMEM)]
        + [vmem] * 2,
        out_specs=[any_space] * 13 + [vmem] * 2,
        scratch_shapes=[
            pltpu.VMEM((parts, token_rows, width), bf16),
            pltpu.VMEM((tokens, width), bf16),
            pltpu.VMEM(stacked + (lin_width + 128,), bf16),
            pltpu.VMEM((tokens, lin_width), f32),
            pltpu.VMEM((query_heads, tokens, head), bf16),
            pltpu.VMEM((plane, tokens, 2 * key_width), bf16),
            pltpu.VMEM((parts, tokens, query_width), bf16),
            pltpu.VMEM(stacked + (parts * query_width,), bf16),
            pltpu.VMEM((tokens, width), f32),
            pltpu.VMEM((tokens, width), bf16),
            pltpu.VMEM((head, group * tokens), f32),
            pltpu.SemaphoreType.DMA((copies,)),
            pltpu.SemaphoreType.DMA((copies,)),
            pltpu.SemaphoreType.DMA((32,)),
        ],
        compiler_params=pltpu.CompilerParams(
            has_side_effects=True, vmem_limit_bytes=60 * 1024 * 1024
        ),
        cost_estimate=pl.CostEstimate(flops=12 * 10**9, bytes_accessed=10**8, transcendentals=10**7),
    )(hidden, *weights, gain_block, grad_out, *tables, *positions, *head_gains)


def half_turn(values):
    return pltpu.roll(values, values.shape[1] // 2, 1)


def total_of(landed):
    total = landed[0].astype(f32)
    for index in range(1, parts):
        total += landed[index].astype(f32)
    return total


class Returns:
    def __init__(self, links, place, ring, addend, ring_sems, buffers):
        self.links, self.place, self.ring, self.addend = links, place, ring, addend
        self.ring_sems = ring_sems
        self.from_sibling, self.halves, self.from_plane, self.sums, self.final = buffers
        self.pending = [[] for _ in range(ring.shape[0])]
        self.turn, self.used = 0, 0
        self.sibling_copies, self.plane_copies, self.z_copies = {}, {}, {}
        self.mine, self.own_final = {}, {}

    def slot(self):
        slot = self.turn % len(self.pending)
        self.turn += 1
        for wait in self.pending[slot]:
            wait()
        self.pending[slot] = []
        return slot

    def local(self, source, target):
        self.used += 1
        return Copy(source, target, [(self.ring_sems, self.used - 1)])

    def product(self, slot, left, half, right, start, index, added):
        size = right.shape[1]
        tile = 512 if size % 512 == 0 else 256

        def tile_of(step, carry):
            columns = pl.ds(pl.multiple_of(step * tile, tile), tile)
            target = pl.ds(pl.multiple_of(start + step * tile, 128), tile)
            rows = left[index, :, half]
            value = multiply(rows.reshape(-1, rows.shape[2]), right[:, columns])
            value = value.reshape(rows.shape[0], rows.shape[1], tile)
            if added is not None:
                value += self.addend[added, :, :, target].astype(f32)
            self.ring[slot, :, :, target] = value.astype(bf16)
            return carry

        lax.fori_loop(0, size // tile, tile_of, 0)

    def give(self, family, left, right, start=0):
        place, size = self.place, right.shape[1]
        other = place.other_core
        columns = pl.ds(start, size)
        for index in range(parts):
            slot = self.slot()
            self.product(slot, left, other, right, start, index, None)
            copy = self.links.send(
                at(self.ring)[slot, :, :, columns],
                at(self.from_sibling)[family, index, :, :, columns],
                tracked=False,
                c=other,
            )
            self.pending[slot].append(copy.wait_send)
            self.sibling_copies[family, start, index] = copy

    def take(self, family, left, right, start=0, send=True):
        size = right.shape[1]
        columns = pl.ds(start, size)
        loads, kept = [], []
        slots = self.addend.shape[0]

        def load(index):
            self.sibling_copies[family, start, index].wait_recv()
            loads.append(
                self.local(
                    at(self.from_sibling)[family, index, :, :, columns],
                    at(self.addend)[index % slots, :, :, columns],
                )
            )

        for index in range(slots):
            load(index)
        for index in range(parts):
            slot = self.slot()
            loads[index].wait()
            self.product(slot, left, self.place.c, right, start, index, index % slots)
            if index + slots < parts:
                load(index + slots)
            kept.append(
                self.local(
                    at(self.ring)[slot, :, :, columns],
                    at(self.halves)[family, index, :, :, columns],
                )
            )
            self.pending[slot].append(kept[-1].wait)
        for waits in self.pending:
            for wait in waits:
                wait()
            waits.clear()
        if send:
            self.send_plane(family, columns)

    def send_plane(self, family, columns):
        links, place = self.links, self.place
        sent = self.plane_copies.setdefault(family, [])
        for step in range(1, place.plane):
            other = place.in_plane(step)
            sent.append(
                links.send(
                    at(self.halves)[family, :, other, :, columns],
                    at(self.from_plane)[family, place.p, :, :, columns],
                    p=other,
                )
            )
        self.mine.setdefault(family, []).append(
            self.local(
                at(self.halves)[family, :, place.p, :, columns],
                at(self.from_plane)[family, place.p, :, :, columns],
            )
        )

    def along_z(self, family, columns):
        links, place = self.links, self.place
        for copy in self.plane_copies[family]:
            copy.wait_recv()
        for copy in self.mine[family]:
            copy.wait()
        sources = place.plane
        loads = []
        for index in range(parts):
            slot = self.slot()
            loads.append(
                (
                    slot,
                    self.local(
                        at(self.from_plane)[family, pl.ds(0, sources), index, :, columns],
                        at(self.ring)[slot, pl.ds(0, sources), :, columns],
                    ),
                )
            )
        for index, (slot, load) in enumerate(loads):
            load.wait()
            total = self.ring[slot, 0, :, columns].astype(f32)
            for source in range(1, sources):
                total += self.ring[slot, source, :, columns].astype(f32)
            self.sums[family, index, :, columns] = total.astype(bf16)
        copies = []
        for step in z_steps:
            other = place.along_z(step)
            copies.append(
                links.send(
                    at(self.sums)[family, other, :, columns],
                    at(self.final)[family, place.z, :, columns],
                    z=other,
                )
            )
        self.own_final[family] = self.local(
            at(self.sums)[family, place.z, :, columns],
            at(self.final)[family, place.z, :, columns],
        )
        self.z_copies[family] = copies

    def home(self, family):
        for copy in self.z_copies[family]:
            copy.wait_recv()
        self.own_final[family].wait()

    def finish(self):
        assert self.used <= self.ring_sems.shape[0]
        for waits in self.pending:
            for wait in waits:
                wait()


def rear_kernel(
    plane,
    cores,
    normed_mlp_in,
    gate_in,
    up_in,
    down_in,
    grad_half_in,
    residual_in,
    projection_in,
    out_in,
    normed_in,
    lin_in,
    queries_in,
    both_in,
    attended_in,
    hidden,
    grad_out,
    stats,
    gains,
    cosine,
    sine_turned,
    query_pos,
    key_blocks,
    query_gain,
    key_gain,
    output,
    input_grad,
    small_sums,
    from_sibling,
    halves,
    from_plane,
    final,
    both_landed,
    normed,
    turned_left,
    turned_right,
    gate,
    up,
    down,
    part_in,
    landed_in,
    landed_out,
    extra_in,
    extra_out,
    residual,
    grad_residual,
    low_rows,
    sums,
    ring,
    addend,
    gain_rows,
    messages,
    z_messages,
    plane_messages,
    core_messages,
    ring_sems,
    both_sems,
    send_sems,
    recv_sems,
    local_sems,
):
    links = Links(send_sems, recv_sems, local_sems)
    tokens, width = normed.shape
    token_rows = tokens // parts
    place = Place(plane, cores, token_rows)
    returns = Returns(
        links, place, ring, addend, ring_sems, (from_sibling, halves, from_plane, sums, final)
    )
    units = gate.shape[3]
    block = width // parts
    shard = gate.shape[2]
    head = query_gain.shape[1]
    query_heads = queries_in.shape[0]
    query_width = query_heads * head
    key_width = both_in.shape[2] // 2
    key_heads = key_width // head
    group = query_heads // key_heads
    lin_width = query_width + 2 * key_width
    own_rows = place.z_rows[0]
    part_out = normed
    split = (plane, cores, shard, tokens)

    gathers = []
    all_units = pl.ds(0, units)
    out_sum = LineSum(links, place, part_out, landed_out, extra_out)
    back_sum = LineSum(links, place, part_in, landed_in, extra_in)

    def feed_forward(act, d_gate, d_up):
        own_down = links.local(down_in, at(down)[:, place.column])
        loads = [
            links.local(normed_mlp_in, normed),
            links.local(gate_in, gate),
            links.local(up_in, up),
            links.local(residual_in, residual),
            links.local(grad_half_in, at(low_rows)[:, :, pl.ds(0, width // 2)]),
        ]
        half = pl.ds(width // 2, width // 2)
        low_rows[place.z, :, half] = grad_out[:, half]
        gathers.append(
            LineGather(links, place, at(grad_out)[:, half], lambda z: at(low_rows)[z, :, half])
        )
        own_down.wait()
        down_fetch = Fetch(links, place, [], down)
        down_fetch.spread()
        for copy in loads[:3]:
            copy.wait()
        tile = 256

        def hidden_tile(index, carry):
            columns = pl.ds(pl.multiple_of(index * tile, tile), tile)
            gate_lin = multiply(normed[...], gate[:, :, :, columns].reshape(width, tile))
            up_lin = multiply(normed[...], up[:, :, :, columns].reshape(width, tile))
            sigmoid = jax.nn.sigmoid(gate_lin)
            silu = gate_lin * sigmoid
            act[:, columns] = (silu * up_lin).astype(bf16)
            d_up[:, columns] = silu.astype(bf16)
            d_gate[:, columns] = (up_lin * (sigmoid + silu * (1.0 - sigmoid))).astype(bf16)
            return carry

        middle = units // tile // 2
        lax.fori_loop(0, middle, hidden_tile, 0)
        gathers[0].relay()
        lax.fori_loop(middle, units // tile, hidden_tile, 0)
        down_fetch.forward()
        for copy in loads[3:]:
            copy.wait()
        for index in range(parts):
            columns = slice(index * block, (index + 1) * block)
            turned_left[index] = normed[:, columns].T.reshape(split)
        down_fetch.close()
        down_fetch.finish()
        for index in range(parts):
            columns = pl.ds(index * block, block)
            part_out[:, columns] = multiply_trans(
                act[...], down[index].reshape(block, units)
            ).astype(bf16)
        landed_out[place.z] = part_out[own_rows]
        gathers[0].wait()

        def grad_tile(index, carry):
            columns = pl.ds(pl.multiple_of(index * tile, tile), tile)
            grad_act = multiply(
                low_rows[...].reshape(tokens, width), down[:, :, :, columns].reshape(width, tile)
            )
            d_up[:, columns] = (grad_act * d_up[:, columns].astype(f32)).astype(bf16)
            d_gate[:, columns] = (grad_act * d_gate[:, columns].astype(f32)).astype(bf16)
            return carry

        lax.fori_loop(0, units // tile, grad_tile, 0)
        gathers[0].relayed()
        for index in range(parts):
            columns = slice(index * block, (index + 1) * block)
            turned_right[index] = low_rows[:, :, columns].reshape(tokens, block).T.reshape(split)
        in_sum = LineSum(links, place, part_in, landed_in, extra_in)
        for index in range(parts):
            columns = pl.ds(index * block, block)
            part_in[:, columns] = (
                multiply_trans(d_gate[...], gate[index].reshape(block, units))
                + multiply_trans(d_up[...], up[index].reshape(block, units))
            ).astype(bf16)
            in_sum.start(columns, False)
        landed_in[place.z] = part_in[own_rows]
        returns.give(0, turned_left, d_gate)
        returns.give(1, turned_left, d_up)
        in_sum.combine(False)
        returns.take(0, turned_left, d_gate)

        in_sum.wait()
        grad_normed = total_of(landed_in)
        values = residual[...]
        scale = lax.rsqrt(jnp.mean(values * values, axis=-1, keepdims=True) + epsilon)
        unit = values * scale
        gain_rows[1:2] = jnp.sum(grad_normed * unit, axis=0, keepdims=True)
        own_grad = grad_out[...].astype(f32)
        total = own_grad + norm_back(grad_normed * gains[1:2], unit, scale)
        grad_residual[...] = total
        low_rows[place.z] = total.astype(bf16)
        gathers.append(
            LineGather(links, place, at(low_rows)[place.z], lambda z: at(low_rows)[z])
        )
        returns.take(1, turned_left, d_up)
        gathers[1].relay()
        returns.give(2, turned_right, act)
        returns.take(2, turned_right, act, send=False)
        for copy in in_sum.sent():
            copy.wait_send()

    pl.run_scoped(
        feed_forward,
        pltpu.VMEM((tokens, units), bf16),
        pltpu.VMEM((tokens, units), bf16),
        pltpu.VMEM((tokens, units), bf16),
    )

    def attention(lin, queries, both, attended, grad_heads, delta, both_stage, both_total, query_total, grad_lin):
        out_at = pl.ds(pl.multiple_of(place.z * query_width, 128), query_width)
        out_columns = at(up)[:, :, :, pl.ds(0, query_width)]
        projection = at(gate)[:, :, :, pl.ds(0, lin_width)]
        loads = [
            links.local(at(out_in)[:, :, :, out_at], out_columns),
            links.local(attended_in, attended),
            links.local(queries_in, queries),
            links.local(both_in, both),
            links.local(lin_in, lin),
            links.local(at(projection_in)[:, :, :, pl.ds(0, lin_width)], projection),
            links.local(normed_in, part_in),
        ]
        for copy in loads:
            copy.wait()
        for index in range(parts):
            columns = slice(index * block, (index + 1) * block)
            turned_left[index] = part_in[:, columns].T.reshape(split)
        gathers[1].wait()
        out_sum.start(pl.ds(0, width))

        tile = group * head
        for index in range(key_heads):
            columns = slice(index * tile, (index + 1) * tile)
            grads = multiply(
                low_rows[...].reshape(tokens, width), up[:, :, :, columns].reshape(width, tile)
            ).astype(bf16)
            for member in range(group):
                number = index * group + member
                own = grads[:, member * head : (member + 1) * head]
                grad_heads[number] = own
                mixed = attended[:, number * head : (number + 1) * head].astype(f32)
                delta[number : number + 1] = jnp.sum(
                    (own.astype(f32) * mixed).T, axis=0, keepdims=True
                )

        factor = head ** (-0.5)
        score_factor = factor * 1.4426950408889634
        chunk = min(256, tokens)
        chunks_each = tokens // chunk
        lanes = group * tokens
        piece_rows = token_rows // 2
        both_copies, both_own = [], []
        for key_head in range(key_heads):
            members = slice(key_head * group, (key_head + 1) * group)
            query_block = queries[members].reshape(lanes, head)
            grad_block = grad_heads[members].reshape(lanes, head)
            numbers = range(key_head * group, (key_head + 1) * group)
            stats_row = jnp.concatenate([stats[number : number + 1] for number in numbers], axis=1)
            delta_row = jnp.concatenate([delta[number : number + 1] for number in numbers], axis=1)
            positions = jnp.concatenate([query_pos[...]] * group, axis=1)
            query_total[...] = jnp.zeros_like(query_total)

            def back_chunk(index, carry):
                source, row = index // chunks_each, index % chunks_each
                rows = pl.ds(pl.multiple_of(row * chunk, chunk), chunk)
                keys = both[source, rows, pl.ds(key_head * head, head)]
                values = both[source, rows, pl.ds(key_width + key_head * head, head)]
                scores = multiply_trans(keys, query_block) * score_factor
                places = key_positions(key_blocks, index, chunk, piece_rows)
                weights = jnp.where(
                    places <= positions, jnp.exp2(scores - stats_row), 0.0
                )
                grad_weights = multiply_trans(values, grad_block)
                grad_scores = (weights * (grad_weights - delta_row)).astype(bf16)
                query_total[...] += outer_rows(keys, grad_scores)
                both[source, rows, pl.ds(key_head * head, head)] = (
                    multiply(grad_scores, query_block) * factor
                ).astype(bf16)
                both[source, rows, pl.ds(key_width + key_head * head, head)] = multiply(
                    weights.astype(bf16), grad_block
                ).astype(bf16)
                return carry

            lax.fori_loop(0, plane * chunks_each, back_chunk, 0)
            for start in (key_head * head, key_width + key_head * head):
                columns = pl.ds(start, head)
                for step in range(1, plane):
                    other = place.in_plane(step)
                    both_copies.append(
                        links.send(
                            at(both)[other, :, columns],
                            at(both_landed)[place.p, :, columns],
                            tracked=False,
                            p=other,
                        )
                    )
                both_own.append(
                    links.local(
                        at(both)[place.p, :, columns], at(both_landed)[place.p, :, columns]
                    )
                )
            if key_head == 0:
                out_sum.combine()
            grad_queries = query_total[...].T * factor
            for member in range(group):
                number = key_head * group + member
                rows = slice(member * tokens, (member + 1) * tokens)
                own = grad_queries[rows]
                lin_rows = lin[:, number * head : (number + 1) * head]
                scale = lax.rsqrt(jnp.mean(lin_rows * lin_rows, axis=-1, keepdims=True) + epsilon)
                unit = lin_rows * scale
                turned = own * cosine[...] - half_turn(own) * sine_turned[...]
                gained = jnp.sum(turned * unit, axis=0, keepdims=True)
                if number == 0:
                    messages[0, 0:1, block : block + head] = gained
                else:
                    messages[0, 0:1, block : block + head] += gained
                grad_lin[:, number * head : (number + 1) * head] = norm_back(
                    turned * query_gain[...], unit, scale
                ).astype(bf16)

        for index in range(parts):
            columns = slice(index * block, (index + 1) * block)
            turned_right[index] = low_rows[:, :, columns].reshape(tokens, block).T.reshape(split)
        returns.give(3, turned_right, attended, query_width)
        query_lin = at(grad_lin)[:, pl.ds(0, query_width)].get()
        returns.give(3, turned_left, query_lin)
        returns.take(3, turned_right, attended, query_width, send=False)
        returns.along_z(0, all_units)
        returns.take(3, turned_left, query_lin, send=False)

        for copy in both_copies:
            copy.wait_recv()
        for copy in both_own:
            copy.wait()
        returns.send_plane(2, all_units)
        returns.send_plane(3, pl.ds(query_width, query_width))
        returns.send_plane(3, pl.ds(0, query_width))

        def load_both(source):
            return Copy(
                at(both_landed)[source], at(both_stage)[source % 2], [(both_sems, source)]
            )

        load = load_both(0)
        for source in range(plane):
            load.wait()
            if source + 1 < plane:
                load = load_both(source + 1)
            landed = both_stage[source % 2].astype(f32)
            if source == 0:
                both_total[...] = landed
            else:
                both_total[...] += landed
        for key_head in range(key_heads):
            start = query_width + key_width + key_head * head
            grad_lin[:, start : start + head] = both_total[
                :, key_width + key_head * head : key_width + (key_head + 1) * head
            ].astype(bf16)
            own = both_total[:, key_head * head : (key_head + 1) * head]
            start = query_width + key_head * head
            lin_rows = lin[:, start : start + head]
            scale = lax.rsqrt(jnp.mean(lin_rows * lin_rows, axis=-1, keepdims=True) + epsilon)
            unit = lin_rows * scale
            turned = own * cosine[...] - half_turn(own) * sine_turned[...]
            gained = jnp.sum(turned * unit, axis=0, keepdims=True)
            if key_head == 0:
                messages[0, 1:2, block : block + head] = gained
            else:
                messages[0, 1:2, block : block + head] += gained
            grad_lin[:, start : start + head] = norm_back(turned * key_gain[...], unit, scale).astype(
                bf16
            )

        for index in range(parts):
            columns = pl.ds(index * block, block)
            part_in[:, columns] = multiply_trans(
                grad_lin[...], gate[index, :, :, 0:lin_width].reshape(block, lin_width)
            ).astype(bf16)
            back_sum.start(columns)
        landed_in[place.z] = part_in[own_rows]
        both_lin = at(grad_lin)[:, pl.ds(query_width, 2 * key_width)].get()
        returns.give(4, turned_left, both_lin)
        returns.along_z(1, all_units)
        back_sum.combine()
        returns.take(4, turned_left, both_lin)
        for copy in both_copies:
            copy.wait_send()

    pl.run_scoped(
        attention,
        pltpu.VMEM((tokens, query_width + key_width), f32),
        pltpu.VMEM((query_heads, tokens, head), bf16),
        pltpu.VMEM((plane, tokens, 2 * key_width), bf16),
        pltpu.VMEM((tokens, query_width), bf16),
        pltpu.VMEM((query_heads, tokens, head), bf16),
        pltpu.VMEM((8, tokens), f32),
        pltpu.VMEM((2, tokens, 2 * key_width), bf16),
        pltpu.VMEM((tokens, 2 * key_width), f32),
        pltpu.VMEM((head, group * tokens), f32),
        pltpu.VMEM((tokens, lin_width), bf16),
    )
    back_sum.wait()
    grad_normed = total_of(landed_in)
    values = hidden[...].astype(f32)
    scale = lax.rsqrt(jnp.mean(values * values, axis=-1, keepdims=True) + epsilon)
    unit = values * scale
    gain_rows[0:1] = jnp.sum(grad_normed * unit, axis=0, keepdims=True)
    input_grad[...] = (
        grad_residual[...] + norm_back(grad_normed * gains[0:1], unit, scale)
    ).astype(bf16)

    for index in range(1, parts):
        messages[index, :, block : block + head] = messages[0, :, block : block + head]
    for index in range(parts):
        messages[index, 0:2, 0:block] = gain_rows[:, index * block : (index + 1) * block]
    copies = [
        links.send(at(messages)[place.along_z(step)], at(z_messages)[place.z], z=place.along_z(step))
        for step in z_steps
    ]
    z_messages[place.z] = messages[place.z]
    returns.along_z(2, all_units)
    out_sum.wait()
    output[...] = (residual[...] + total_of(landed_out)).astype(bf16)
    for copy in copies:
        copy.wait_recv()
    plane_messages[place.p] = (z_messages[0] + z_messages[1]) + (z_messages[2] + z_messages[3])
    copies = [
        links.send(
            at(plane_messages)[place.p], at(plane_messages)[place.p], p=place.in_plane(step)
        )
        for step in range(1, plane)
    ]
    returns.along_z(3, pl.ds(0, 2 * query_width))
    returns.along_z(4, pl.ds(0, 2 * key_width))
    for copy in copies:
        copy.wait_recv()
    total = plane_messages[0]
    for source in range(1, plane):
        total += plane_messages[source]
    core_messages[place.c] = total
    copies = [
        links.send(at(core_messages)[place.c], at(core_messages)[place.c], c=other)
        for other in place.siblings()
    ]
    for copy in copies:
        copy.wait_recv()
    total = core_messages[0]
    for source in range(1, cores):
        total += core_messages[source]
    small_sums[...] = total
    for family in range(5):
        returns.home(family)
    gathers[1].relayed()
    returns.finish()
    links.finish()


def rear(plane, cores, large, small):
    normed_mlp, gate = large[0], large[1]
    projection, lin, queries, both = large[6], large[9], large[10], large[11]
    tokens, width = normed_mlp.shape
    token_rows = tokens // parts
    _, columns, shard, units = gate.shape
    query_heads, _, head = queries.shape
    query_width = query_heads * head
    key_width = both.shape[2] // 2
    key_heads = key_width // head
    lin_width = query_width + 2 * key_width
    block = width // parts
    any_space, vmem = pl.BlockSpec(memory_space=pl.ANY), pl.BlockSpec(memory_space=pltpu.VMEM)
    copies = 120 + 10 + 6 + 24 + 24 + 16 * plane + 48 + 16
    assert 2 * max(query_width, key_width) <= units
    shapes = [
        ((token_rows, width), bf16),
        ((token_rows, width), bf16),
        ((8, block + head), f32),
        ((5, parts, plane, shard, units), bf16),
        ((5, parts, plane, shard, units), bf16),
        ((5, plane, parts, shard, units), bf16),
        ((5, parts, shard, units), bf16),
        ((plane, tokens, 2 * key_width), bf16),
    ]
    turned = (parts, plane, cores, shard, tokens)
    message = (8, block + head)
    return pl.pallas_call(
        functools.partial(rear_kernel, plane, cores),
        out_shape=[jax.ShapeDtypeStruct(shape, kind) for shape, kind in shapes],
        in_specs=[any_space] * 13
        + [vmem] * 7
        + [pl.BlockSpec(memory_space=pltpu.SMEM)]
        + [vmem] * 2,
        out_specs=[vmem] * 3 + [any_space] * 5,
        scratch_shapes=[
            pltpu.VMEM((tokens, width), bf16),
            pltpu.VMEM(turned, bf16),
            pltpu.VMEM(turned, bf16),
            pltpu.VMEM(gate.shape, bf16),
            pltpu.VMEM(gate.shape, bf16),
            pltpu.VMEM(gate.shape, bf16),
            pltpu.VMEM((tokens, width), bf16),
            pltpu.VMEM((parts, token_rows, width), bf16),
            pltpu.VMEM((parts, token_rows, width), bf16),
            pltpu.VMEM((token_rows, width), bf16),
            pltpu.VMEM((token_rows, width), bf16),
            pltpu.VMEM((token_rows, width), f32),
            pltpu.VMEM((token_rows, width), f32),
            pltpu.VMEM((parts, token_rows, width), bf16),
            pltpu.VMEM((5, parts, shard, units), bf16),
            pltpu.VMEM((4, plane, shard, units), bf16),
            pltpu.VMEM((parts if plane == 4 else 1, plane, shard, units), bf16),
            pltpu.VMEM((2, width), f32),
            pltpu.VMEM((parts,) + message, f32),
            pltpu.VMEM((parts,) + message, f32),
            pltpu.VMEM((plane,) + message, f32),
            pltpu.VMEM((cores,) + message, f32),
            pltpu.SemaphoreType.DMA((160,)),
            pltpu.SemaphoreType.DMA((plane,)),
            pltpu.SemaphoreType.DMA((copies,)),
            pltpu.SemaphoreType.DMA((copies,)),
            pltpu.SemaphoreType.DMA((24,)),
        ],
        compiler_params=pltpu.CompilerParams(
            has_side_effects=True, vmem_limit_bytes=63 * 1024 * 1024
        ),
        cost_estimate=pl.CostEstimate(flops=4 * 10**10, bytes_accessed=10**8, transcendentals=10**7),
    )(*large, *small)


def make_local(plane, cores):
    def local(
        hidden_in,
        block_map,
        query_weight,
        key_weight,
        value_weight,
        out_weight,
        gate_weight,
        up_weight,
        down_weight,
        attention_norm_gain,
        feedforward_gain,
        query_gain,
        key_gain,
        output_grad,
    ):
        shard = query_weight.shape[0]
        hidden_own, grad_own = hidden_in[0], output_grad[0]
        row_count, features = hidden_own.shape
        piece_rows = row_count // 2
        head_width = query_gain.shape[0]
        p_index = lax.axis_index("p")
        tokens = parts * row_count

        blocks = block_map[0].reshape(parts, plane, 2)
        offsets = jnp.arange(piece_rows, dtype=jnp.int32)
        all_pos = blocks.transpose(1, 0, 2)[..., None] * piece_rows + offsets
        all_pos = all_pos.reshape(plane, tokens)
        query_pos = lax.dynamic_index_in_dim(all_pos, p_index, 0, keepdims=False)
        key_blocks = blocks.transpose(1, 0, 2).reshape(-1)
        cosine, sine_table = rope_tables(query_pos, head_width)
        sign = jnp.where(jnp.arange(head_width) < head_width // 2, -1.0, 1.0).astype(f32)
        query_gain_float = query_gain.astype(f32)
        key_gain_float = key_gain.astype(f32)
        gain_block = jnp.stack([attention_norm_gain, feedforward_gain], axis=1)
        gain_block = jnp.pad(gain_block, ((0, 0), (0, 126)))

        (
            normed,
            projection,
            lin,
            queries,
            both,
            attended_low,
            out_full,
            normed_mlp,
            own_residual,
            gate_columns,
            up_columns,
            down_columns,
            grad_half,
            stats,
            gains,
        ) = front(
            plane,
            cores,
            hidden_own,
            (
                query_weight,
                key_weight,
                value_weight,
                out_weight,
                gate_weight,
                up_weight,
                down_weight,
            ),
            gain_block,
            grad_own,
            (cosine[:, 0], sine_table[:, 0] * sign),
            (query_pos[None], key_blocks),
            (query_gain_float[None], key_gain_float[None]),
        )
        results = rear(
            plane,
            cores,
            (
                normed_mlp,
                gate_columns,
                up_columns,
                down_columns,
                grad_half,
                own_residual,
                projection,
                out_full,
                normed,
                lin,
                queries,
                both,
                attended_low,
            ),
            (
                hidden_own,
                grad_own,
                stats,
                gains,
                cosine[:, 0],
                sine_table[:, 0] * sign,
                query_pos[None],
                key_blocks,
                query_gain_float[None],
                key_gain_float[None],
            ),
        )
        output, input_grad = results[:2]
        small_sums, final = results[2], results[6]

        def home(family, start, count):
            columns = final[family, :, :, start : start + count].transpose(1, 0, 2)
            return columns.astype(f32).reshape(shard, parts * count)

        units = gate_weight.shape[1] // parts
        query_width, key_width = query_weight.shape[1] // parts, key_weight.shape[1] // parts
        block = features // parts
        own_column = p_index * cores + lax.axis_index("c")
        own_gains = lax.dynamic_slice_in_dim(small_sums[:2, :block], own_column * shard, shard, 1)
        head_sums = small_sums[:2, block:]
        return (
            (output[None], input_grad[None])
            + (
                home(3, 0, query_width),
                home(4, 0, key_width),
                home(4, key_width, key_width),
                home(3, query_width, query_width),
                home(0, 0, units),
                home(1, 0, units),
                home(2, 0, units),
            )
            + (own_gains[0], own_gains[1], head_sums[0], head_sums[1])
        )

    return local


def solution(mesh):
    ctx_count, core_count = mesh.shape["ctx"], mesh.shape["fsdp"]
    plane = ctx_count // parts
    fine_mesh = Mesh(mesh.devices.reshape(parts, plane, core_count), ("z", "p", "c"))
    token_spec = P("c", ("z", "p"), None)
    weight_spec = P(("z", "p", "c"), None)
    gain_spec = P(("z", "p", "c"))
    return jax.shard_map(
        make_local(plane, core_count),
        mesh=fine_mesh,
        in_specs=(
            (token_spec, P("c", None)) + (weight_spec,) * 7 + (gain_spec,) * 2 + (P(), P(), token_spec)
        ),
        out_specs=(token_spec,) * 2 + (weight_spec,) * 7 + (gain_spec,) * 2 + (P(), P()),
        check_vma=False,
    )
```

```python
import functools

import jax
import jax.numpy as jnp
from jax import lax
from jax.experimental import pallas as pl
from jax.experimental.pallas import tpu as pltpu
from jax.sharding import Mesh, PartitionSpec as P

epsilon = 1e-06
rotary_base = 1000000.0
masked_score = -1e30
parts = 4
bf16 = jnp.bfloat16
f32 = jnp.float32


def norm_back(weighted, unit, scale_row):
    inner_mean = jnp.mean(weighted * unit, axis=-1, keepdims=True)
    return scale_row * (weighted - unit * inner_mean)


def rope_tables(positions, width):
    half_width = width // 2
    frequency = rotary_base ** (-(jnp.arange(half_width, dtype=f32) * 2.0 / width))
    angles = positions.astype(f32)[:, None] * frequency[None, :]
    angles = jnp.concatenate([angles, angles], axis=-1)
    return jnp.cos(angles)[:, None, :], jnp.sin(angles)[:, None, :]


def multiply(left, right):
    return jnp.dot(left, right, preferred_element_type=f32)


def multiply_trans(left, right):
    return lax.dot_general(left, right, (((1,), (1,)), ((), ())), preferred_element_type=f32)


def outer_rows(left, right):
    return lax.dot_general(left, right, (((0,), (0,)), ((), ())), preferred_element_type=f32)


class Part:
    def __init__(self, ref, index=None):
        self.ref, self.index = ref, index

    def __getitem__(self, index):
        return Part(self.ref, index)

    def get(self):
        return self.ref if self.index is None else self.ref.at[self.index]


def at(ref):
    return Part(ref)


def found(ref):
    return ref.get() if isinstance(ref, Part) else ref


class Copy:
    def __init__(self, source, target, sems, device=None, when=None):
        self.source, self.target, self.sems = source, target, sems
        self.device, self.when = device, when
        self.guarded(lambda: self.describe().start())

    def guarded(self, action):
        if self.when is None:
            action()
        else:
            pl.when(self.when)(action)

    def describe(self):
        source, target = found(self.source), found(self.target)
        sems = [array.at[index] for array, index in self.sems]
        if self.device is None:
            return pltpu.make_async_copy(source, target, sems[0])
        return pltpu.make_async_remote_copy(
            src_ref=source,
            dst_ref=target,
            send_sem=sems[0],
            recv_sem=sems[1],
            device_id=self.device,
            device_id_type=pl.DeviceIdType.MESH,
        )

    def wait(self):
        self.describe().wait()

    def wait_send(self):
        self.guarded(lambda: self.describe().wait_send())

    def wait_recv(self):
        self.describe().wait_recv()


class Links:
    def __init__(self, send_sems, recv_sems, local_sems):
        self.send_sems, self.recv_sems, self.local_sems = send_sems, recv_sems, local_sems
        self.count, self.local_count = 0, 0
        self.sent, self.kept = [], []

    def send(self, source, target, tracked=True, when=None, lands=None, **device):
        index = self.count
        self.count += 1
        received = index if lands is None else lands.sems[1][1]
        copy = Copy(
            source, target, [(self.send_sems, index), (self.recv_sems, received)], device, when
        )
        if tracked:
            self.sent.append(copy)
        return copy

    def local(self, source, target):
        index = self.local_count
        self.local_count += 1
        return Copy(source, target, [(self.local_sems, index)])

    def keep(self, source, target):
        self.kept.append(self.local(source, target))

    def finish(self):
        assert self.count <= self.send_sems.shape[0]
        assert self.local_count <= self.local_sems.shape[0]
        for copy in self.sent:
            copy.wait_send()
        for copy in self.kept:
            copy.wait()


class LineGather:
    def __init__(self, links, place, source, block):
        self.links, self.place, self.block = links, place, block
        target = block(place.z)
        self.far = links.send(source, target, z=place.along_z(2))
        self.above = links.send(source, target, when=place.not_last, z=place.along_z(1))
        self.below = links.send(source, target, when=place.not_first, z=place.along_z(3))

    def relay(self):
        links, place = self.links, self.place
        self.far.wait_recv()
        block = self.block(place.along_z(2))
        self.relays = (
            links.send(block, block, False, place.second, self.above, z=place.along_z(3)),
            links.send(block, block, False, place.third, self.below, z=place.along_z(1)),
        )

    def wait(self):
        self.above.wait_recv()
        self.below.wait_recv()

    def relayed(self):
        for copy in self.relays:
            copy.wait_send()


class LineSum:
    def __init__(self, links, place, part, landed, extra):
        self.links, self.place = links, place
        self.part, self.landed, self.extra = part, landed, extra
        self.near, self.extras, self.far, self.columns = [], [], [], []

    def start(self, columns, tracked=True):
        links, place = self.links, self.place
        target = at(self.landed)[place.z, :, columns]
        rows = place.z_rows
        above, below = at(self.part)[rows[1], columns], at(self.part)[rows[3], columns]
        beyond = at(self.part)[rows[2], columns]
        self.columns.append(columns)
        self.far.append(links.send(beyond, target, tracked, place.at_end, z=place.along_z(2)))
        self.near.append(
            (
                links.send(above, target, tracked, place.not_last, z=place.along_z(1)),
                links.send(below, target, tracked, place.not_first, z=place.along_z(3)),
            )
        )
        extra = at(self.extra)[:, columns]
        self.extras.append(
            (
                links.send(below, extra, tracked, place.first, z=place.along_z(1)),
                links.send(above, extra, tracked, place.last, z=place.along_z(3)),
            )
        )

    def combine(self, tracked=True):
        links, place = self.links, self.place

        @pl.when(place.at_end)
        def nothing_comes():
            self.landed[place.opposite] = jnp.zeros(self.landed.shape[1:], bf16)

        for columns, extras, far in zip(self.columns, self.extras, self.far):
            rows = place.z_rows[2]

            @pl.when(place.second)
            def arrived():
                extras[0].wait_recv()

            @pl.when(place.third)
            def arrived_too():
                extras[1].wait_recv()

            @pl.when(place.inside)
            def add():
                total = self.part[rows, columns].astype(f32) + self.extra[:, columns].astype(f32)
                self.part[rows, columns] = total.astype(bf16)

            self.near.append(
                (
                    links.send(
                        at(self.part)[rows, columns],
                        at(self.landed)[place.z, :, columns],
                        tracked,
                        place.inside,
                        lands=far,
                        z=place.along_z(2),
                    ),
                )
            )

    def wait(self):
        place = self.place
        for index, far in enumerate(self.far):
            above, below = self.near[index]

            @pl.when(place.not_first)
            def from_below():
                above.wait_recv()

            @pl.when(place.not_last)
            def from_above():
                below.wait_recv()

            far.wait_recv()

    def sent(self):
        return self.far + [copy for copies in self.near + self.extras for copy in copies]


class Place:
    def __init__(self, plane, cores, token_rows):
        self.plane, self.cores = plane, cores
        self.z, self.p, self.c = (lax.axis_index(axis) for axis in ("z", "p", "c"))
        self.column = self.p * cores + self.c
        self.other_core = lax.rem(self.c + 1, cores)
        self.z_others = [lax.rem(self.z + step, parts) for step in range(parts)]
        self.p_others = [lax.rem(self.p + step, plane) for step in range(plane)]
        self.columns_before = [
            lax.rem(self.p + plane - step, plane) * cores + self.c for step in range(plane)
        ]
        self.first, self.last = self.z == 0, self.z == parts - 1
        self.second, self.third = self.z == 1, self.z == parts - 2
        self.not_first, self.not_last = self.z != 0, self.z != parts - 1
        self.at_end = jnp.logical_or(self.first, self.last)
        self.inside = jnp.logical_not(self.at_end)
        self.opposite = parts - 1 - self.z
        self.relayed = plane == 4
        if self.relayed:
            self.flips = [self.p + 1 - 2 * lax.rem(self.p, 2), lax.rem(self.p + 2, 4)]
            flipped = lax.rem(self.flips[0] + 2, 4)
            self.flip_columns = [flip * cores + self.c for flip in self.flips + [flipped]]
        self.z_rows = [
            pl.ds(pl.multiple_of(other * token_rows, token_rows), token_rows)
            for other in self.z_others
        ]

    def along_z(self, step):
        return self.z_others[step]

    def in_plane(self, step):
        return self.p_others[step]

    def before(self, step):
        return self.columns_before[step]

    def siblings(self):
        return [self.other_core]


z_steps = (1, 3, 2)


class Fetch:
    def __init__(self, links, place, pieces, gathered, line_only=False):
        self.links, self.place, self.pieces, self.gathered = links, place, pieces, gathered
        self.line_only = line_only
        self.first, self.own = [], []

    def mine(self, columns):
        if self.line_only:
            return at(self.gathered)[self.place.z, :, columns]
        return at(self.gathered)[self.place.z, self.place.column, :, columns]

    def begin(self):
        links, place = self.links, self.place
        mine = self.mine
        for shard, width, start, split in self.pieces:
            for step in z_steps:
                other = place.along_z(step)
                first = pl.multiple_of(other * width, 128) if split else 0
                self.first.append(
                    links.send(at(shard)[:, pl.ds(first, width)], mine(pl.ds(start, width)), z=other)
                )
            first = pl.multiple_of(place.z * width, 128) if split else 0
            self.own.append(
                links.local(at(shard)[:, pl.ds(first, width)], mine(pl.ds(start, width)))
            )

    def arrive(self):
        for copy in self.own:
            copy.wait()
        for copy in self.first:
            copy.wait_recv()

    def spread(self):
        links, place = self.links, self.place
        self.arrive()
        block = at(self.gathered)[:, place.column]
        if place.relayed:
            self.second = [links.send(block, block, p=other) for other in place.flips]
        else:
            self.second = [
                links.send(block, block, p=place.in_plane(step)) for step in range(1, place.plane)
            ]
        self.third = [links.send(block, block, c=other) for other in place.siblings()]
        self.halves = []

    def pass_on(self, column):
        block = at(self.gathered)[:, column]
        self.third += [self.links.send(block, block, c=other) for other in self.place.siblings()]

    def forward(self):
        links, place = self.links, self.place
        if place.relayed:
            for side, copy in enumerate(self.second):
                copy.wait_recv()
                column = place.flip_columns[side]
                half = at(self.gathered)[pl.ds(side * (parts // 2), parts // 2), column]
                self.halves.append(links.send(half, half, p=place.flips[1 - side]))
                self.pass_on(column)
        else:
            for step, copy in enumerate(self.second, 1):
                copy.wait_recv()
                self.pass_on(place.before(step))

    def close(self):
        if self.place.relayed:
            for copy in self.halves:
                copy.wait_recv()
            self.pass_on(self.place.flip_columns[2])

    def finish(self):
        for copy in self.third:
            copy.wait_recv()


def key_positions(key_blocks, index, chunk, piece_rows):
    pieces = chunk // piece_rows
    spots = lax.broadcasted_iota(jnp.int32, (chunk, 1), 0)
    starts = jnp.zeros((chunk, 1), jnp.int32)
    for piece in range(pieces):
        start = key_blocks[index * pieces + piece] * piece_rows - piece * piece_rows
        starts = jnp.where(spots >= piece * piece_rows, start, starts)
    return spots + starts


def front_kernel(
    plane,
    cores,
    hidden,
    query_weight,
    key_weight,
    value_weight,
    out_weight,
    gate_weight,
    up_weight,
    down_weight,
    gain_block,
    grad_out,
    cosine,
    sine_turned,
    query_pos,
    key_blocks,
    query_gain,
    key_gain,
    normed_out,
    projection_out,
    lin_out,
    queries_out,
    both_out,
    attended_out,
    out_columns_out,
    normed_mlp_out,
    residual_out,
    gate_out,
    up_out,
    down_out,
    grad_half_out,
    stats_out,
    gains_out,
    hidden_all,
    normed,
    projection,
    lin,
    queries,
    both,
    attended_all,
    out_full,
    residual,
    normed_mlp,
    mixed,
    send_sems,
    recv_sems,
    local_sems,
):
    links = Links(send_sems, recv_sems, local_sems)
    token_rows, width = hidden.shape
    place = Place(plane, cores, token_rows)
    tokens = parts * token_rows
    head = query_gain.shape[1]
    query_width = query_weight.shape[1] // parts
    key_width = key_weight.shape[1] // parts
    query_heads, key_heads = query_width // head, key_width // head
    group = query_heads // key_heads
    hidden_units = gate_weight.shape[1] // parts
    lin_width = query_width + 2 * key_width

    heads_fetch = Fetch(
        links,
        place,
        [
            (query_weight, query_width, 0, True),
            (key_weight, key_width, query_width, True),
            (value_weight, key_width, query_width + key_width, True),
            (gain_block, 128, lin_width, False),
        ],
        projection,
    )
    out_fetch = Fetch(links, place, [], out_full)
    mlp_fetches = [
        Fetch(links, place, [(weight, hidden_units, 0, True)], target)
        for weight, target in ((gate_weight, gate_out), (up_weight, up_out))
    ]
    down_fetch = Fetch(links, place, [(down_weight, hidden_units, 0, True)], down_out, True)
    heads_fetch.begin()
    mlp_fetches[0].begin()
    heads_fetch.spread()
    hidden_own = links.local(hidden, hidden_all.at[place.z])
    hidden_gather = LineGather(links, place, hidden, lambda z: at(hidden_all)[z])
    mlp_fetches[0].spread()
    heads_fetch.forward()
    hidden_gather.relay()
    heads_fetch.close()
    heads_fetch.finish()
    links.keep(projection, projection_out)
    hidden_own.wait()
    hidden_gather.wait()
    out_fetch.own.append(links.local(out_weight, at(out_full)[place.z, place.column]))
    out_gather = LineGather(
        links, place, out_weight, lambda z: at(out_full)[z, place.column]
    )
    for fetch in (mlp_fetches[1], down_fetch):
        fetch.begin()

    gain_columns = projection[:, :, :, lin_width : lin_width + 128].reshape(width, 128)
    gain_rows = gain_columns.astype(f32).T
    gains_out[...] = gain_rows[:8]

    def norm_one(index, carry):
        values = hidden_all[index].astype(f32)
        scale = lax.rsqrt(jnp.mean(values * values, axis=-1, keepdims=True) + epsilon)
        rows = pl.ds(pl.multiple_of(index * token_rows, token_rows), token_rows)
        normed[rows] = (values * scale * gains_out[0:1]).astype(bf16)
        return carry

    lax.fori_loop(0, parts, norm_one, 0)
    links.keep(normed, normed_out)

    tile = 2 * head

    def project(index, carry):
        columns = pl.ds(pl.multiple_of(index * tile, tile), tile)
        weights = projection[:, :, :, columns].reshape(width, tile)
        lin[:, columns] = jnp.dot(normed[...], weights, preferred_element_type=f32)
        return carry

    lax.fori_loop(0, lin_width // tile, project, 0)
    own_both = both.at[place.p]

    def rope(values, gain):
        scale = lax.rsqrt(jnp.mean(values * values, axis=-1, keepdims=True) + epsilon)
        gained = values * scale * gain
        turned = pltpu.roll(gained, head // 2, 1)
        return (gained * cosine[...] + turned * sine_turned[...]).astype(bf16)

    for index in range(key_heads):
        columns = slice(query_width + index * head, query_width + (index + 1) * head)
        own_both[:, index * head : (index + 1) * head] = rope(lin[:, columns], key_gain[...])
    own_both[:, key_width:] = lin[:, query_width + key_width :].astype(bf16)
    both_copies = [
        links.send(own_both, own_both, p=place.in_plane(step)) for step in range(1, plane)
    ]
    for index in range(query_heads):
        columns = slice(index * head, (index + 1) * head)
        queries[index] = rope(lin[:, columns], query_gain[...])
    links.keep(lin.at[:, pl.ds(0, query_width + key_width)], lin_out)
    links.keep(queries, queries_out)
    mlp_fetches[0].forward()
    for copy in both_copies:
        copy.wait_recv()
    links.keep(both, both_out)
    out_gather.relay()

    factor = head ** (-0.5) * 1.4426950408889634
    chunk = min(256, tokens)
    chunks_each = tokens // chunk
    lanes = group * tokens
    own_attended = attended_all.at[place.z]
    attended_gathers = []
    for key_head in range(key_heads):
        block = queries[key_head * group : (key_head + 1) * group].reshape(lanes, head)
        positions = jnp.concatenate([query_pos[...]] * group, axis=1)
        mixed[...] = jnp.zeros_like(mixed)

        def attend_chunk(index, carry):
            best, summed = carry
            source, row = index // chunks_each, index % chunks_each
            rows = pl.ds(pl.multiple_of(row * chunk, chunk), chunk)
            keys = both[source, rows, pl.ds(key_head * head, head)]
            values = both[source, rows, pl.ds(key_width + key_head * head, head)]
            scores = multiply_trans(keys, block) * factor
            allowed = key_positions(key_blocks, index, chunk, token_rows // 2) <= positions
            scores = jnp.where(allowed, scores, masked_score)
            new_best = jnp.maximum(best, jnp.max(scores, axis=0, keepdims=True))
            weights = jnp.exp2(scores - new_best)
            shrink = jnp.exp2(best - new_best)
            summed = summed * shrink + jnp.sum(weights, axis=0, keepdims=True)
            mixed[...] = mixed[...] * shrink + outer_rows(values, weights.astype(bf16))
            return new_best, summed

        best, summed = lax.fori_loop(
            0,
            plane * chunks_each,
            attend_chunk,
            (jnp.full((1, lanes), masked_score, f32), jnp.zeros((1, lanes), f32)),
        )
        mixed_rows = (mixed[...] / summed).T
        stats = best + jnp.log2(summed)
        for member in range(group):
            index = key_head * group + member
            stats_out[index : index + 1] = stats[:, member * tokens : (member + 1) * tokens]
            own_attended[:, index * head : (index + 1) * head] = mixed_rows[
                member * tokens : (member + 1) * tokens
            ].astype(bf16)
        columns = pl.ds(key_head * group * head, group * head)
        attended_gathers.append(
            LineGather(
                links,
                place,
                at(attended_all)[place.z, :, columns],
                lambda z, columns=columns: at(attended_all)[z, :, columns],
            )
        )
        if key_head == 0:
            mlp_fetches[0].close()
            out_gather.wait()
            out_fetch.spread()
    links.keep(own_attended, attended_out)
    out_fetch.forward()
    mlp_fetches[1].spread()
    for gather in attended_gathers:
        gather.relay()
    out_fetch.close()
    out_fetch.finish()
    links.keep(out_full, out_columns_out)
    mlp_fetches[1].forward()
    for gather in attended_gathers:
        gather.wait()
    half = pl.ds(0, width // 2)
    links.keep(at(grad_out)[:, half], at(grad_half_out)[place.z])
    grad_gather = LineGather(
        links, place, at(grad_out)[:, half], lambda z: at(grad_half_out)[z]
    )

    def add_out(index, carry):
        weights = out_full[index].reshape(width // parts, parts * query_width)
        columns = pl.ds(pl.multiple_of(index * (width // parts), 128), width // parts)
        total = hidden_all[:, :, columns].reshape(tokens, width // parts).astype(f32)
        for other in range(parts):
            total += multiply_trans(
                attended_all[other], weights[:, other * query_width : (other + 1) * query_width]
            )
        residual[:, columns] = total
        return carry

    lax.fori_loop(0, parts, add_out, 0)

    def norm_two(index, carry):
        rows = pl.ds(pl.multiple_of(index * token_rows, token_rows), token_rows)
        values = residual[rows]
        scale = lax.rsqrt(jnp.mean(values * values, axis=-1, keepdims=True) + epsilon)
        normed_mlp[rows] = (values * scale * gains_out[1:2]).astype(bf16)
        return carry

    lax.fori_loop(0, parts, norm_two, 0)
    links.keep(normed_mlp, normed_mlp_out)
    own_rows = place.z_rows[0]
    links.keep(residual.at[own_rows], residual_out)
    grad_gather.relay()
    mlp_fetches[1].close()
    down_fetch.arrive()
    grad_gather.wait()
    for fetch in mlp_fetches:
        fetch.finish()
    for gather in [hidden_gather, out_gather, grad_gather] + attended_gathers:
        gather.relayed()
    links.finish()


def front(plane, cores, hidden, weights, gain_block, grad_out, tables, positions, head_gains):
    token_rows, width = hidden.shape
    tokens = parts * token_rows
    shard = weights[0].shape[0]
    head = head_gains[0].shape[1]
    query_width, key_width = weights[0].shape[1] // parts, weights[1].shape[1] // parts
    hidden_units = weights[4].shape[1] // parts
    lin_width = query_width + 2 * key_width
    query_heads = query_width // head
    group = query_width // key_width
    stacked = (parts, plane * cores, shard)
    copies = 24 + 5 * (2 * plane + 8) + plane + 24
    any_space, vmem = pl.BlockSpec(memory_space=pl.ANY), pl.BlockSpec(memory_space=pltpu.VMEM)
    outputs = [
        ((tokens, width), bf16),
        (stacked + (lin_width + 128,), bf16),
        ((tokens, query_width + key_width), f32),
        ((query_heads, tokens, head), bf16),
        ((plane, tokens, 2 * key_width), bf16),
        ((tokens, query_width), bf16),
        (stacked + (parts * query_width,), bf16),
        ((tokens, width), bf16),
        ((token_rows, width), f32),
        (stacked + (hidden_units,), bf16),
        (stacked + (hidden_units,), bf16),
        ((parts, shard, hidden_units), bf16),
        ((parts, token_rows, width // 2), bf16),
        ((8, tokens), f32),
        ((8, width), f32),
    ]
    return pl.pallas_call(
        functools.partial(front_kernel, plane, cores),
        out_shape=[jax.ShapeDtypeStruct(shape, kind) for shape, kind in outputs],
        in_specs=[any_space] * 10
        + [vmem] * 3
        + [pl.BlockSpec(memory_space=pltpu.SMEM)]
        + [vmem] * 2,
        out_specs=[any_space] * 13 + [vmem] * 2,
        scratch_shapes=[
            pltpu.VMEM((parts, token_rows, width), bf16),
            pltpu.VMEM((tokens, width), bf16),
            pltpu.VMEM(stacked + (lin_width + 128,), bf16),
            pltpu.VMEM((tokens, lin_width), f32),
            pltpu.VMEM((query_heads, tokens, head), bf16),
            pltpu.VMEM((plane, tokens, 2 * key_width), bf16),
            pltpu.VMEM((parts, tokens, query_width), bf16),
            pltpu.VMEM(stacked + (parts * query_width,), bf16),
            pltpu.VMEM((tokens, width), f32),
            pltpu.VMEM((tokens, width), bf16),
            pltpu.VMEM((head, group * tokens), f32),
            pltpu.SemaphoreType.DMA((copies,)),
            pltpu.SemaphoreType.DMA((copies,)),
            pltpu.SemaphoreType.DMA((32,)),
        ],
        compiler_params=pltpu.CompilerParams(
            has_side_effects=True, vmem_limit_bytes=60 * 1024 * 1024
        ),
        cost_estimate=pl.CostEstimate(flops=12 * 10**9, bytes_accessed=10**8, transcendentals=10**7),
    )(hidden, *weights, gain_block, grad_out, *tables, *positions, *head_gains)


def half_turn(values):
    return pltpu.roll(values, values.shape[1] // 2, 1)


def total_of(landed):
    total = landed[0].astype(f32)
    for index in range(1, parts):
        total += landed[index].astype(f32)
    return total


class Returns:
    def __init__(self, links, place, ring, addend, ring_sems, buffers):
        self.links, self.place, self.ring, self.addend = links, place, ring, addend
        self.ring_sems = ring_sems
        self.from_sibling, self.halves, self.from_plane, self.sums, self.final = buffers
        self.pending = [[] for _ in range(ring.shape[0])]
        self.turn, self.used = 0, 0
        self.sibling_copies, self.plane_copies, self.z_copies = {}, {}, {}
        self.mine, self.own_final = {}, {}

    def slot(self):
        slot = self.turn % len(self.pending)
        self.turn += 1
        for wait in self.pending[slot]:
            wait()
        self.pending[slot] = []
        return slot

    def local(self, source, target):
        self.used += 1
        return Copy(source, target, [(self.ring_sems, self.used - 1)])

    def product(self, slot, left, half, right, start, index, added):
        size = right.shape[1]
        tile = 512 if size % 512 == 0 else 256

        def tile_of(step, carry):
            columns = pl.ds(pl.multiple_of(step * tile, tile), tile)
            target = pl.ds(pl.multiple_of(start + step * tile, 128), tile)
            rows = left[index, :, half]
            value = multiply(rows.reshape(-1, rows.shape[2]), right[:, columns])
            value = value.reshape(rows.shape[0], rows.shape[1], tile)
            if added is not None:
                value += self.addend[added, :, :, target].astype(f32)
            self.ring[slot, :, :, target] = value.astype(bf16)
            return carry

        lax.fori_loop(0, size // tile, tile_of, 0)

    def give(self, family, left, right, start=0):
        place, size = self.place, right.shape[1]
        other = place.other_core
        columns = pl.ds(start, size)
        for index in range(parts):
            slot = self.slot()
            self.product(slot, left, other, right, start, index, None)
            copy = self.links.send(
                at(self.ring)[slot, :, :, columns],
                at(self.from_sibling)[family, index, :, :, columns],
                tracked=False,
                c=other,
            )
            self.pending[slot].append(copy.wait_send)
            self.sibling_copies[family, start, index] = copy

    def take(self, family, left, right, start=0, send=True):
        size = right.shape[1]
        columns = pl.ds(start, size)
        loads, kept = [], []
        slots = self.addend.shape[0]

        def load(index):
            self.sibling_copies[family, start, index].wait_recv()
            loads.append(
                self.local(
                    at(self.from_sibling)[family, index, :, :, columns],
                    at(self.addend)[index % slots, :, :, columns],
                )
            )

        for index in range(slots):
            load(index)
        for index in range(parts):
            slot = self.slot()
            loads[index].wait()
            self.product(slot, left, self.place.c, right, start, index, index % slots)
            if index + slots < parts:
                load(index + slots)
            kept.append(
                self.local(
                    at(self.ring)[slot, :, :, columns],
                    at(self.halves)[family, index, :, :, columns],
                )
            )
            self.pending[slot].append(kept[-1].wait)
        for waits in self.pending:
            for wait in waits:
                wait()
            waits.clear()
        if send:
            self.send_plane(family, columns)

    def send_plane(self, family, columns):
        links, place = self.links, self.place
        sent = self.plane_copies.setdefault(family, [])
        for step in range(1, place.plane):
            other = place.in_plane(step)
            sent.append(
                links.send(
                    at(self.halves)[family, :, other, :, columns],
                    at(self.from_plane)[family, place.p, :, :, columns],
                    p=other,
                )
            )
        self.mine.setdefault(family, []).append(
            self.local(
                at(self.halves)[family, :, place.p, :, columns],
                at(self.from_plane)[family, place.p, :, :, columns],
            )
        )

    def along_z(self, family, columns):
        links, place = self.links, self.place
        for copy in self.plane_copies[family]:
            copy.wait_recv()
        for copy in self.mine[family]:
            copy.wait()
        sources = place.plane
        loads = []
        for index in range(parts):
            slot = self.slot()
            loads.append(
                (
                    slot,
                    self.local(
                        at(self.from_plane)[family, pl.ds(0, sources), index, :, columns],
                        at(self.ring)[slot, pl.ds(0, sources), :, columns],
                    ),
                )
            )
        for index, (slot, load) in enumerate(loads):
            load.wait()
            total = self.ring[slot, 0, :, columns].astype(f32)
            for source in range(1, sources):
                total += self.ring[slot, source, :, columns].astype(f32)
            self.sums[family, index, :, columns] = total.astype(bf16)
        copies = []
        for step in z_steps:
            other = place.along_z(step)
            copies.append(
                links.send(
                    at(self.sums)[family, other, :, columns],
                    at(self.final)[family, place.z, :, columns],
                    z=other,
                )
            )
        self.own_final[family] = self.local(
            at(self.sums)[family, place.z, :, columns],
            at(self.final)[family, place.z, :, columns],
        )
        self.z_copies[family] = copies

    def home(self, family):
        for copy in self.z_copies[family]:
            copy.wait_recv()
        self.own_final[family].wait()

    def finish(self):
        assert self.used <= self.ring_sems.shape[0]
        for waits in self.pending:
            for wait in waits:
                wait()


def rear_kernel(
    plane,
    cores,
    normed_mlp_in,
    gate_in,
    up_in,
    down_in,
    grad_half_in,
    residual_in,
    projection_in,
    out_in,
    normed_in,
    lin_in,
    queries_in,
    both_in,
    attended_in,
    hidden,
    grad_out,
    stats,
    gains,
    cosine,
    sine_turned,
    query_pos,
    key_blocks,
    query_gain,
    key_gain,
    output,
    input_grad,
    small_sums,
    from_sibling,
    halves,
    from_plane,
    final,
    both_landed,
    normed,
    turned_left,
    turned_right,
    gate,
    up,
    down,
    part_in,
    landed_in,
    landed_out,
    extra_in,
    extra_out,
    residual,
    grad_residual,
    low_rows,
    sums,
    ring,
    addend,
    gain_rows,
    messages,
    z_messages,
    plane_messages,
    core_messages,
    ring_sems,
    both_sems,
    send_sems,
    recv_sems,
    local_sems,
):
    links = Links(send_sems, recv_sems, local_sems)
    tokens, width = normed.shape
    token_rows = tokens // parts
    place = Place(plane, cores, token_rows)
    returns = Returns(
        links, place, ring, addend, ring_sems, (from_sibling, halves, from_plane, sums, final)
    )
    units = gate.shape[3]
    block = width // parts
    shard = gate.shape[2]
    head = query_gain.shape[1]
    query_heads = queries_in.shape[0]
    query_width = query_heads * head
    key_width = both_in.shape[2] // 2
    key_heads = key_width // head
    group = query_heads // key_heads
    lin_width = query_width + 2 * key_width
    own_rows = place.z_rows[0]
    part_out = normed
    split = (plane, cores, shard, tokens)

    gathers = []
    all_units = pl.ds(0, units)
    out_sum = LineSum(links, place, part_out, landed_out, extra_out)
    back_sum = LineSum(links, place, part_in, landed_in, extra_in)

    def feed_forward(act, d_gate, d_up):
        own_down = links.local(down_in, at(down)[:, place.column])
        loads = [
            links.local(normed_mlp_in, normed),
            links.local(gate_in, gate),
            links.local(up_in, up),
            links.local(residual_in, residual),
            links.local(grad_half_in, at(low_rows)[:, :, pl.ds(0, width // 2)]),
        ]
        half = pl.ds(width // 2, width // 2)
        low_rows[place.z, :, half] = grad_out[:, half]
        gathers.append(
            LineGather(links, place, at(grad_out)[:, half], lambda z: at(low_rows)[z, :, half])
        )
        own_down.wait()
        down_fetch = Fetch(links, place, [], down)
        down_fetch.spread()
        for copy in loads[:3]:
            copy.wait()
        tile = 256

        def hidden_tile(index, carry):
            columns = pl.ds(pl.multiple_of(index * tile, tile), tile)
            gate_lin = multiply(normed[...], gate[:, :, :, columns].reshape(width, tile))
            up_lin = multiply(normed[...], up[:, :, :, columns].reshape(width, tile))
            sigmoid = jax.nn.sigmoid(gate_lin)
            silu = gate_lin * sigmoid
            act[:, columns] = (silu * up_lin).astype(bf16)
            d_up[:, columns] = silu.astype(bf16)
            d_gate[:, columns] = (up_lin * (sigmoid + silu * (1.0 - sigmoid))).astype(bf16)
            return carry

        middle = units // tile // 2
        lax.fori_loop(0, middle, hidden_tile, 0)
        gathers[0].relay()
        lax.fori_loop(middle, units // tile, hidden_tile, 0)
        down_fetch.forward()
        for copy in loads[3:]:
            copy.wait()
        for index in range(parts):
            columns = slice(index * block, (index + 1) * block)
            turned_left[index] = normed[:, columns].T.reshape(split)
        down_fetch.close()
        down_fetch.finish()
        for index in range(parts):
            columns = pl.ds(index * block, block)
            part_out[:, columns] = multiply_trans(
                act[...], down[index].reshape(block, units)
            ).astype(bf16)
        landed_out[place.z] = part_out[own_rows]
        gathers[0].wait()

        def grad_tile(index, carry):
            columns = pl.ds(pl.multiple_of(index * tile, tile), tile)
            grad_act = multiply(
                low_rows[...].reshape(tokens, width), down[:, :, :, columns].reshape(width, tile)
            )
            d_up[:, columns] = (grad_act * d_up[:, columns].astype(f32)).astype(bf16)
            d_gate[:, columns] = (grad_act * d_gate[:, columns].astype(f32)).astype(bf16)
            return carry

        lax.fori_loop(0, units // tile, grad_tile, 0)
        gathers[0].relayed()
        for index in range(parts):
            columns = slice(index * block, (index + 1) * block)
            turned_right[index] = low_rows[:, :, columns].reshape(tokens, block).T.reshape(split)
        in_sum = LineSum(links, place, part_in, landed_in, extra_in)
        for index in range(parts):
            columns = pl.ds(index * block, block)
            part_in[:, columns] = (
                multiply_trans(d_gate[...], gate[index].reshape(block, units))
                + multiply_trans(d_up[...], up[index].reshape(block, units))
            ).astype(bf16)
            in_sum.start(columns, False)
        landed_in[place.z] = part_in[own_rows]
        returns.give(0, turned_left, d_gate)
        returns.give(1, turned_left, d_up)
        in_sum.combine(False)
        returns.take(0, turned_left, d_gate)

        in_sum.wait()
        grad_normed = total_of(landed_in)
        values = residual[...]
        scale = lax.rsqrt(jnp.mean(values * values, axis=-1, keepdims=True) + epsilon)
        unit = values * scale
        gain_rows[1:2] = jnp.sum(grad_normed * unit, axis=0, keepdims=True)
        own_grad = grad_out[...].astype(f32)
        total = own_grad + norm_back(grad_normed * gains[1:2], unit, scale)
        grad_residual[...] = total
        low_rows[place.z] = total.astype(bf16)
        gathers.append(
            LineGather(links, place, at(low_rows)[place.z], lambda z: at(low_rows)[z])
        )
        returns.take(1, turned_left, d_up)
        gathers[1].relay()
        returns.give(2, turned_right, act)
        returns.take(2, turned_right, act, send=False)
        for copy in in_sum.sent():
            copy.wait_send()

    pl.run_scoped(
        feed_forward,
        pltpu.VMEM((tokens, units), bf16),
        pltpu.VMEM((tokens, units), bf16),
        pltpu.VMEM((tokens, units), bf16),
    )

    def attention(lin, queries, both, attended, grad_heads, delta, both_stage, both_total, query_total, grad_lin):
        out_at = pl.ds(pl.multiple_of(place.z * query_width, 128), query_width)
        out_columns = at(up)[:, :, :, pl.ds(0, query_width)]
        projection = at(gate)[:, :, :, pl.ds(0, lin_width)]
        loads = [
            links.local(at(out_in)[:, :, :, out_at], out_columns),
            links.local(attended_in, attended),
            links.local(queries_in, queries),
            links.local(both_in, both),
            links.local(lin_in, lin),
            links.local(at(projection_in)[:, :, :, pl.ds(0, lin_width)], projection),
            links.local(normed_in, part_in),
        ]
        for copy in loads:
            copy.wait()
        for index in range(parts):
            columns = slice(index * block, (index + 1) * block)
            turned_left[index] = part_in[:, columns].T.reshape(split)
        gathers[1].wait()
        out_sum.start(pl.ds(0, width))

        tile = group * head
        for index in range(key_heads):
            columns = slice(index * tile, (index + 1) * tile)
            grads = multiply(
                low_rows[...].reshape(tokens, width), up[:, :, :, columns].reshape(width, tile)
            ).astype(bf16)
            for member in range(group):
                number = index * group + member
                own = grads[:, member * head : (member + 1) * head]
                grad_heads[number] = own
                mixed = attended[:, number * head : (number + 1) * head].astype(f32)
                delta[number : number + 1] = jnp.sum(
                    (own.astype(f32) * mixed).T, axis=0, keepdims=True
                )

        factor = head ** (-0.5)
        score_factor = factor * 1.4426950408889634
        chunk = min(256, tokens)
        chunks_each = tokens // chunk
        lanes = group * tokens
        piece_rows = token_rows // 2
        both_copies, both_own = [], []
        for key_head in range(key_heads):
            members = slice(key_head * group, (key_head + 1) * group)
            query_block = queries[members].reshape(lanes, head)
            grad_block = grad_heads[members].reshape(lanes, head)
            numbers = range(key_head * group, (key_head + 1) * group)
            stats_row = jnp.concatenate([stats[number : number + 1] for number in numbers], axis=1)
            delta_row = jnp.concatenate([delta[number : number + 1] for number in numbers], axis=1)
            positions = jnp.concatenate([query_pos[...]] * group, axis=1)
            query_total[...] = jnp.zeros_like(query_total)

            def back_chunk(index, carry):
                source, row = index // chunks_each, index % chunks_each
                rows = pl.ds(pl.multiple_of(row * chunk, chunk), chunk)
                keys = both[source, rows, pl.ds(key_head * head, head)]
                values = both[source, rows, pl.ds(key_width + key_head * head, head)]
                scores = multiply_trans(keys, query_block) * score_factor
                places = key_positions(key_blocks, index, chunk, piece_rows)
                weights = jnp.where(
                    places <= positions, jnp.exp2(scores - stats_row), 0.0
                )
                grad_weights = multiply_trans(values, grad_block)
                grad_scores = (weights * (grad_weights - delta_row)).astype(bf16)
                query_total[...] += outer_rows(keys, grad_scores)
                both[source, rows, pl.ds(key_head * head, head)] = (
                    multiply(grad_scores, query_block) * factor
                ).astype(bf16)
                both[source, rows, pl.ds(key_width + key_head * head, head)] = multiply(
                    weights.astype(bf16), grad_block
                ).astype(bf16)
                return carry

            lax.fori_loop(0, plane * chunks_each, back_chunk, 0)
            for start in (key_head * head, key_width + key_head * head):
                columns = pl.ds(start, head)
                for step in range(1, plane):
                    other = place.in_plane(step)
                    both_copies.append(
                        links.send(
                            at(both)[other, :, columns],
                            at(both_landed)[place.p, :, columns],
                            tracked=False,
                            p=other,
                        )
                    )
                both_own.append(
                    links.local(
                        at(both)[place.p, :, columns], at(both_landed)[place.p, :, columns]
                    )
                )
            if key_head == 0:
                out_sum.combine()
            grad_queries = query_total[...].T * factor
            for member in range(group):
                number = key_head * group + member
                rows = slice(member * tokens, (member + 1) * tokens)
                own = grad_queries[rows]
                lin_rows = lin[:, number * head : (number + 1) * head]
                scale = lax.rsqrt(jnp.mean(lin_rows * lin_rows, axis=-1, keepdims=True) + epsilon)
                unit = lin_rows * scale
                turned = own * cosine[...] - half_turn(own) * sine_turned[...]
                gained = jnp.sum(turned * unit, axis=0, keepdims=True)
                if number == 0:
                    messages[0, 0:1, block : block + head] = gained
                else:
                    messages[0, 0:1, block : block + head] += gained
                grad_lin[:, number * head : (number + 1) * head] = norm_back(
                    turned * query_gain[...], unit, scale
                ).astype(bf16)

        for index in range(parts):
            columns = slice(index * block, (index + 1) * block)
            turned_right[index] = low_rows[:, :, columns].reshape(tokens, block).T.reshape(split)
        returns.give(3, turned_right, attended, query_width)
        query_lin = at(grad_lin)[:, pl.ds(0, query_width)].get()
        returns.give(3, turned_left, query_lin)
        returns.take(3, turned_right, attended, query_width, send=False)
        returns.along_z(0, all_units)
        returns.take(3, turned_left, query_lin, send=False)

        for copy in both_copies:
            copy.wait_recv()
        for copy in both_own:
            copy.wait()
        returns.send_plane(2, all_units)
        returns.send_plane(3, pl.ds(query_width, query_width))
        returns.send_plane(3, pl.ds(0, query_width))

        def load_both(source):
            return Copy(
                at(both_landed)[source], at(both_stage)[source % 2], [(both_sems, source)]
            )

        load = load_both(0)
        for source in range(plane):
            load.wait()
            if source + 1 < plane:
                load = load_both(source + 1)
            landed = both_stage[source % 2].astype(f32)
            if source == 0:
                both_total[...] = landed
            else:
                both_total[...] += landed
        for key_head in range(key_heads):
            start = query_width + key_width + key_head * head
            grad_lin[:, start : start + head] = both_total[
                :, key_width + key_head * head : key_width + (key_head + 1) * head
            ].astype(bf16)
            own = both_total[:, key_head * head : (key_head + 1) * head]
            start = query_width + key_head * head
            lin_rows = lin[:, start : start + head]
            scale = lax.rsqrt(jnp.mean(lin_rows * lin_rows, axis=-1, keepdims=True) + epsilon)
            unit = lin_rows * scale
            turned = own * cosine[...] - half_turn(own) * sine_turned[...]
            gained = jnp.sum(turned * unit, axis=0, keepdims=True)
            if key_head == 0:
                messages[0, 1:2, block : block + head] = gained
            else:
                messages[0, 1:2, block : block + head] += gained
            grad_lin[:, start : start + head] = norm_back(turned * key_gain[...], unit, scale).astype(
                bf16
            )

        for index in range(parts):
            columns = pl.ds(index * block, block)
            part_in[:, columns] = multiply_trans(
                grad_lin[...], gate[index, :, :, 0:lin_width].reshape(block, lin_width)
            ).astype(bf16)
            back_sum.start(columns)
        landed_in[place.z] = part_in[own_rows]
        both_lin = at(grad_lin)[:, pl.ds(query_width, 2 * key_width)].get()
        returns.give(4, turned_left, both_lin)
        returns.along_z(1, all_units)
        back_sum.combine()
        returns.take(4, turned_left, both_lin)
        for copy in both_copies:
            copy.wait_send()

    pl.run_scoped(
        attention,
        pltpu.VMEM((tokens, query_width + key_width), f32),
        pltpu.VMEM((query_heads, tokens, head), bf16),
        pltpu.VMEM((plane, tokens, 2 * key_width), bf16),
        pltpu.VMEM((tokens, query_width), bf16),
        pltpu.VMEM((query_heads, tokens, head), bf16),
        pltpu.VMEM((8, tokens), f32),
        pltpu.VMEM((2, tokens, 2 * key_width), bf16),
        pltpu.VMEM((tokens, 2 * key_width), f32),
        pltpu.VMEM((head, group * tokens), f32),
        pltpu.VMEM((tokens, lin_width), bf16),
    )
    back_sum.wait()
    grad_normed = total_of(landed_in)
    values = hidden[...].astype(f32)
    scale = lax.rsqrt(jnp.mean(values * values, axis=-1, keepdims=True) + epsilon)
    unit = values * scale
    gain_rows[0:1] = jnp.sum(grad_normed * unit, axis=0, keepdims=True)
    input_grad[...] = (
        grad_residual[...] + norm_back(grad_normed * gains[0:1], unit, scale)
    ).astype(bf16)

    for index in range(1, parts):
        messages[index, :, block : block + head] = messages[0, :, block : block + head]
    for index in range(parts):
        messages[index, 0:2, 0:block] = gain_rows[:, index * block : (index + 1) * block]
    copies = [
        links.send(at(messages)[place.along_z(step)], at(z_messages)[place.z], z=place.along_z(step))
        for step in z_steps
    ]
    z_messages[place.z] = messages[place.z]
    returns.along_z(2, all_units)
    out_sum.wait()
    output[...] = (residual[...] + total_of(landed_out)).astype(bf16)
    for copy in copies:
        copy.wait_recv()
    plane_messages[place.p] = (z_messages[0] + z_messages[1]) + (z_messages[2] + z_messages[3])
    copies = [
        links.send(
            at(plane_messages)[place.p], at(plane_messages)[place.p], p=place.in_plane(step)
        )
        for step in range(1, plane)
    ]
    returns.along_z(3, pl.ds(0, 2 * query_width))
    returns.along_z(4, pl.ds(0, 2 * key_width))
    for copy in copies:
        copy.wait_recv()
    total = plane_messages[0]
    for source in range(1, plane):
        total += plane_messages[source]
    core_messages[place.c] = total
    copies = [
        links.send(at(core_messages)[place.c], at(core_messages)[place.c], c=other)
        for other in place.siblings()
    ]
    for copy in copies:
        copy.wait_recv()
    total = core_messages[0]
    for source in range(1, cores):
        total += core_messages[source]
    small_sums[...] = total
    for family in range(5):
        returns.home(family)
    gathers[1].relayed()
    returns.finish()
    links.finish()


def rear(plane, cores, large, small):
    normed_mlp, gate = large[0], large[1]
    projection, lin, queries, both = large[6], large[9], large[10], large[11]
    tokens, width = normed_mlp.shape
    token_rows = tokens // parts
    _, columns, shard, units = gate.shape
    query_heads, _, head = queries.shape
    query_width = query_heads * head
    key_width = both.shape[2] // 2
    key_heads = key_width // head
    lin_width = query_width + 2 * key_width
    block = width // parts
    any_space, vmem = pl.BlockSpec(memory_space=pl.ANY), pl.BlockSpec(memory_space=pltpu.VMEM)
    copies = 120 + 10 + 6 + 24 + 24 + 16 * plane + 48 + 16
    assert 2 * max(query_width, key_width) <= units
    shapes = [
        ((token_rows, width), bf16),
        ((token_rows, width), bf16),
        ((8, block + head), f32),
        ((5, parts, plane, shard, units), bf16),
        ((5, parts, plane, shard, units), bf16),
        ((5, plane, parts, shard, units), bf16),
        ((5, parts, shard, units), bf16),
        ((plane, tokens, 2 * key_width), bf16),
    ]
    turned = (parts, plane, cores, shard, tokens)
    message = (8, block + head)
    return pl.pallas_call(
        functools.partial(rear_kernel, plane, cores),
        out_shape=[jax.ShapeDtypeStruct(shape, kind) for shape, kind in shapes],
        in_specs=[any_space] * 13
        + [vmem] * 7
        + [pl.BlockSpec(memory_space=pltpu.SMEM)]
        + [vmem] * 2,
        out_specs=[vmem] * 3 + [any_space] * 5,
        scratch_shapes=[
            pltpu.VMEM((tokens, width), bf16),
            pltpu.VMEM(turned, bf16),
            pltpu.VMEM(turned, bf16),
            pltpu.VMEM(gate.shape, bf16),
            pltpu.VMEM(gate.shape, bf16),
            pltpu.VMEM(gate.shape, bf16),
            pltpu.VMEM((tokens, width), bf16),
            pltpu.VMEM((parts, token_rows, width), bf16),
            pltpu.VMEM((parts, token_rows, width), bf16),
            pltpu.VMEM((token_rows, width), bf16),
            pltpu.VMEM((token_rows, width), bf16),
            pltpu.VMEM((token_rows, width), f32),
            pltpu.VMEM((token_rows, width), f32),
            pltpu.VMEM((parts, token_rows, width), bf16),
            pltpu.VMEM((5, parts, shard, units), bf16),
            pltpu.VMEM((4, plane, shard, units), bf16),
            pltpu.VMEM((parts if plane == 4 else 1, plane, shard, units), bf16),
            pltpu.VMEM((2, width), f32),
            pltpu.VMEM((parts,) + message, f32),
            pltpu.VMEM((parts,) + message, f32),
            pltpu.VMEM((plane,) + message, f32),
            pltpu.VMEM((cores,) + message, f32),
            pltpu.SemaphoreType.DMA((160,)),
            pltpu.SemaphoreType.DMA((plane,)),
            pltpu.SemaphoreType.DMA((copies,)),
            pltpu.SemaphoreType.DMA((copies,)),
            pltpu.SemaphoreType.DMA((24,)),
        ],
        compiler_params=pltpu.CompilerParams(
            has_side_effects=True, vmem_limit_bytes=63 * 1024 * 1024
        ),
        cost_estimate=pl.CostEstimate(flops=4 * 10**10, bytes_accessed=10**8, transcendentals=10**7),
    )(*large, *small)


def make_local(plane, cores):
    def local(
        hidden_in,
        block_map,
        query_weight,
        key_weight,
        value_weight,
        out_weight,
        gate_weight,
        up_weight,
        down_weight,
        attention_norm_gain,
        feedforward_gain,
        query_gain,
        key_gain,
        output_grad,
    ):
        shard = query_weight.shape[0]
        hidden_own, grad_own = hidden_in[0], output_grad[0]
        row_count, features = hidden_own.shape
        piece_rows = row_count // 2
        head_width = query_gain.shape[0]
        p_index = lax.axis_index("p")
        tokens = parts * row_count

        blocks = block_map[0].reshape(parts, plane, 2)
        offsets = jnp.arange(piece_rows, dtype=jnp.int32)
        own_blocks = lax.dynamic_slice_in_dim(blocks, p_index, 1, 1)
        query_pos = (own_blocks.reshape(-1, 1) * piece_rows + offsets).reshape(tokens)
        key_blocks = blocks.transpose(1, 0, 2).reshape(-1)
        cosine, sine_table = rope_tables(query_pos, head_width)
        sign = jnp.where(jnp.arange(head_width) < head_width // 2, -1.0, 1.0).astype(f32)
        query_gain_float = query_gain.astype(f32)
        key_gain_float = key_gain.astype(f32)
        lanes = lax.broadcasted_iota(jnp.int32, (shard, 128), 1)
        gain_block = jnp.where(
            lanes == 0, attention_norm_gain[:, None], feedforward_gain[:, None]
        )

        (
            normed,
            projection,
            lin,
            queries,
            both,
            attended_low,
            out_full,
            normed_mlp,
            own_residual,
            gate_columns,
            up_columns,
            down_columns,
            grad_half,
            stats,
            gains,
        ) = front(
            plane,
            cores,
            hidden_own,
            (
                query_weight,
                key_weight,
                value_weight,
                out_weight,
                gate_weight,
                up_weight,
                down_weight,
            ),
            gain_block,
            grad_own,
            (cosine[:, 0], sine_table[:, 0] * sign),
            (query_pos[None], key_blocks),
            (query_gain_float[None], key_gain_float[None]),
        )
        results = rear(
            plane,
            cores,
            (
                normed_mlp,
                gate_columns,
                up_columns,
                down_columns,
                grad_half,
                own_residual,
                projection,
                out_full,
                normed,
                lin,
                queries,
                both,
                attended_low,
            ),
            (
                hidden_own,
                grad_own,
                stats,
                gains,
                cosine[:, 0],
                sine_table[:, 0] * sign,
                query_pos[None],
                key_blocks,
                query_gain_float[None],
                key_gain_float[None],
            ),
        )
        output, input_grad = results[:2]
        small_sums, final = results[2], results[6]

        def home(family, start, count):
            columns = final[family, :, :, start : start + count].transpose(1, 0, 2)
            return columns.astype(f32).reshape(shard, parts * count)

        units = gate_weight.shape[1] // parts
        query_width, key_width = query_weight.shape[1] // parts, key_weight.shape[1] // parts
        block = features // parts
        own_column = p_index * cores + lax.axis_index("c")
        own_gains = lax.dynamic_slice_in_dim(small_sums[:2, :block], own_column * shard, shard, 1)
        head_sums = small_sums[:2, block:]
        return (
            (output[None], input_grad[None])
            + (
                home(3, 0, query_width),
                home(4, 0, key_width),
                home(4, key_width, key_width),
                home(3, query_width, query_width),
                home(0, 0, units),
                home(1, 0, units),
                home(2, 0, units),
            )
            + (own_gains[0], own_gains[1], head_sums[0], head_sums[1])
        )

    return local


def solution(mesh):
    ctx_count, core_count = mesh.shape["ctx"], mesh.shape["fsdp"]
    plane = ctx_count // parts
    fine_mesh = Mesh(mesh.devices.reshape(parts, plane, core_count), ("z", "p", "c"))
    token_spec = P("c", ("z", "p"), None)
    weight_spec = P(("z", "p", "c"), None)
    gain_spec = P(("z", "p", "c"))
    return jax.shard_map(
        make_local(plane, core_count),
        mesh=fine_mesh,
        in_specs=(
            (token_spec, P("c", None)) + (weight_spec,) * 7 + (gain_spec,) * 2 + (P(), P(), token_spec)
        ),
        out_specs=(token_spec,) * 2 + (weight_spec,) * 7 + (gain_spec,) * 2 + (P(), P()),
        check_vma=False,
    )
```
